512 devices in a mesh: ctx: 64 (over z, x, core), tp: 8 (over y).
Axes of the slice: x: 4, y: 8, z: 8, core: 2. Of those that a mesh axis runs over, the one named last changes fastest.
Arguments:
- inner_input: bfloat16 [8192, 8192], P('ctx', 'tp'), may hold values from -6 to 6
- gate_input: bfloat16 [8192, 8192], P('ctx', 'tp'), may hold values from -6 to 6
- state_inputs: bfloat16 [2, 8192, 1024], P(None, 'ctx', 'tp'), may hold values from -6 to 6
- step_size: float32 [128, 8192], P('tp', 'ctx'), may hold values from 0.5 to 2
- resets: int32 [8192], P('ctx'), may hold values 0 or 1
- decay_rate: float32 [128], P('tp'), may hold values from 0 to 0.04
- skip_gain: float32 [128], P('tp'), may hold values from 0.5 to 1.5
- conv_inner: float32 [4, 8192], P(None, 'tp'), may hold values from -3 to 3
- conv_state: float32 [2, 4, 1024], P(None, None, 'tp'), may hold values from -3 to 3
- norm_gain: float32 [8192], P('tp'), may hold values from 0.5 to 1.5
- out_weight: bfloat16 [8192, 4096], P('tp', 'ctx'), may hold values from -0.0625 to 0.0625
- residual: bfloat16 [8192, 4096], P('ctx', 'tp'), may hold values from -6 to 6
- final_gain: float32 [4096], replicated, may hold values from 0.5 to 1.5
- head_weight: bfloat16 [4096, 65536], P(None, ('ctx', 'tp')), may hold values from -8 to 8
- scored: int32 [512], P('ctx'), may hold values from 0 to 8191, as said below
- targets: int32 [512], replicated, may hold values from 0 to 65535
- policy_logprob: float32 [512], replicated, may hold values from -20 to -10
Outputs:
- ref_logprob: float32 [512], replicated
- token_kl: float32 [512], replicated
The draws below stay inside these ranges and needn't reach their ends.
Inputs may be any that keep to these rules, and one draw needn't show every extreme that they name: `scored`: entries j * 8 to (j + 1) * 8 - 1 are distinct positions in j * 128 to (j + 1) * 128 - 1.
All inputs are finite; a program needn't handle non-finite values. No bound on the sum of `resets` on one device may be relied on, other than what follows from the above.
Results may differ from the reference program's by a relative error of at most 0.00215.
The reference program's roundings to bfloat16 on the way (of `inner_conv`, `normed`, `hidden`, `chosen` and `features`) count: a program that leaves them out, or rounds other values in their place, can miss the bound.
Values may be sent and summed in bfloat16 or wider, within the bound.
No kernel may reach another device: no remote copies, remote signals or barrier semaphores. Data moves between devices by JAX's collectives and lax.ppermute only.
A program may use at most 128 MiB of HBM per device.

```python
import math
import jax
import jax.numpy as jnp
from jax import lax

D = 4096
HEADS = 128
HEAD_DIM = 64
STATE = 128
GROUPS = 8
VOCAB = 65536
CONV = 4
SPAN = 128
TOK_DEV = 128
SC_DEV = 8
INNER = 8192
TOKENS = 8192
SCORED = 512


def draw_decay_rate(key, part):
    pick_key, slow_key, fast_key = jax.random.split(key, 3)
    share = 0.5
    slow_heads = jax.random.uniform(pick_key, (HEADS,), jnp.float32) < share
    slow_rate = jnp.exp(jax.random.uniform(slow_key, (HEADS,), jnp.float32, math.log(0.1 / TOKENS), math.log(1.0 / TOKENS)))
    fast_rate = jnp.exp(jax.random.uniform(fast_key, (HEADS,), jnp.float32, math.log(0.02), math.log(0.04)))
    return jnp.where(slow_heads, slow_rate, fast_rate)


def draw_head_weight(key, part):
    base_key = jax.random.fold_in(key, 0)
    weights = jnp.clip(jax.random.normal(base_key, (D, VOCAB), jnp.float32), -6.0, 6.0) * (3.0 / D ** 0.5)
    return weights.astype(jnp.bfloat16)


def draw_scored(key, part):
    blocks = SCORED // SC_DEV

    def one_block(index):
        order = jax.random.permutation(jax.random.fold_in(key, index), TOK_DEV)
        return order[:SC_DEV] + index * TOK_DEV
    return jax.vmap(one_block)(jnp.arange(blocks)).reshape(SCORED).astype(jnp.int32)


def with_ends(entries, own_key, low, top_value):
    longest = entries.shape.index(max(entries.shape))
    spots = []
    for shift in (0, 1):
        where = [jax.random.randint(jax.random.fold_in(own_key, axis), (), 0, length) for axis, length in enumerate(entries.shape)]
        where[longest] = (where[longest] + shift) % entries.shape[longest]
        spots.append(tuple(where))
    return entries.at[spots[0]].set(low).at[spots[1]].set(top_value)


def block_levels(key, shape, cuts, low, high):
    def one(position, parts):
        draws = jax.random.uniform(jax.random.fold_in(jax.random.fold_in(key, 6), position), (parts,), jnp.float32, low / len(cuts), high / len(cuts))
        return jnp.repeat(jnp.exp(draws), shape[position] // parts).reshape((-1,) + (1,) * (len(shape) - position - 1))

    factor_of = one(*cuts[0])
    for cut in cuts[1:]:
        factor_of = factor_of * one(*cut)
    return factor_of


def centred(key, shape, deviation, bound, cuts=(), held_as=jnp.bfloat16):
    factor_of = block_levels(key, shape, cuts, -0.22, 0.18) if cuts else 1.0
    values = jax.random.normal(key, shape, jnp.float32) * deviation * factor_of
    return jnp.minimum(jnp.maximum(values, -bound), bound).astype(held_as)


def setup_inputs(seed: int = 0) -> dict:
    keys = jax.random.split(jax.random.key(seed), 18)
    inner_input = centred(keys[0], (TOKENS, INNER), 1.0, 6.0, ((0, 64), (1, 8)))
    gate_input = centred(keys[1], (TOKENS, INNER), 1.0, 6.0, ((0, 64), (1, 8)))
    state_inputs = centred(keys[2], (2, TOKENS, GROUPS * STATE), 1.0, 6.0, ((1, 64), (2, 8)))
    step_size = jnp.clip(jnp.exp(math.log(2.0) - 1.3862944 * jax.random.uniform(keys[3], (HEADS, TOKENS), jnp.float32) ** block_levels(keys[3], (HEADS, TOKENS), ((0, 8), (1, 64)), -0.2, 0.2)), 0.5, 2.0)
    resets = with_ends((jax.random.randint(keys[4], (TOKENS,), 0, TOKENS // 4) < 1).astype(jnp.int32), jax.random.fold_in(keys[4], 1), 0, 1)
    decay_rate = draw_decay_rate(jax.random.fold_in(keys[17], 71), 0)
    skip_gain = jnp.clip(0.5 + 1.0 * jax.random.uniform(keys[6], (HEADS,), jnp.float32) ** block_levels(keys[6], (HEADS,), ((0, 8),), -0.2, 0.2), 0.5, 1.5)
    conv_inner = centred(keys[7], (CONV, INNER), CONV ** -0.5, 3.0, ((1, 8),), jnp.float32)
    conv_state = centred(keys[8], (2, CONV, GROUPS * STATE), CONV ** -0.5, 3.0, ((2, 8),), jnp.float32)
    norm_gain = jnp.clip(1.0 + 0.1 * jax.random.normal(keys[9], (INNER,), jnp.float32), 0.5, 1.5)
    out_weight = centred(keys[10], (INNER, D), INNER ** -0.5, 0.0625, ((0, 8), (1, 64)))
    residual = centred(keys[11], (TOKENS, D), 1.0, 6.0, ((0, 64), (1, 8)))
    final_gain = jnp.clip(1.0 + 0.1 * jax.random.normal(keys[12], (D,), jnp.float32), 0.5, 1.5)
    head_weight = draw_head_weight(jax.random.fold_in(keys[17], 71), 0)
    scored = draw_scored(jax.random.fold_in(keys[17], 71), 0)
    targets = with_ends(jax.random.randint(keys[15], (SCORED,), 0, VOCAB), jax.random.fold_in(keys[15], 1), 0, VOCAB - 1).astype(jnp.int32)
    policy_logprob = jnp.clip(jax.random.uniform(keys[16], (SCORED,), jnp.float32, -20.0, -10.0), -20.0, -10.0)
    return dict(inner_input=inner_input, gate_input=gate_input, state_inputs=state_inputs, step_size=step_size, resets=resets, decay_rate=decay_rate, skip_gain=skip_gain, conv_inner=conv_inner, conv_state=conv_state, norm_gain=norm_gain, out_weight=out_weight, residual=residual, final_gain=final_gain, head_weight=head_weight, scored=scored, targets=targets, policy_logprob=policy_logprob)


epsilon = 1e-05
precise = lax.Precision.HIGHEST

def causal_filter(stream, kernel, counted):
    kernel_taps = kernel.shape[0]
    rows_total = stream.shape[0]
    values = stream.astype(jnp.float32)
    summed = jnp.zeros_like(values)
    for offset in range(kernel_taps):
        shifted = jnp.concatenate([jnp.zeros((offset, values.shape[1]), jnp.float32), values[:rows_total - offset]], axis=0)
        earlier = jnp.concatenate([jnp.zeros((offset,), counted.dtype), counted[:rows_total - offset]])
        keeping = (counted - earlier == 0).astype(jnp.float32)
        summed = summed + keeping[:, None] * kernel[offset][None, :] * shifted
    return jax.nn.silu(summed).astype(jnp.bfloat16)

def reference(inner_input, gate_input, state_inputs, step_size, resets, decay_rate, skip_gain, conv_inner, conv_state, norm_gain, out_weight, residual, final_gain, head_weight, scored, targets, policy_logprob):
    counted = jnp.cumsum(resets)
    inner_conv = causal_filter(inner_input, conv_inner, counted)
    write_map = causal_filter(state_inputs[0], conv_state[0], counted)
    read_map = causal_filter(state_inputs[1], conv_state[1], counted)
    spans = TOKENS // SPAN
    per_group = HEADS // GROUPS
    values = inner_conv.reshape(spans, SPAN, HEADS, HEAD_DIM).astype(jnp.float32)
    writes = jnp.repeat(write_map.reshape(spans, SPAN, GROUPS, STATE), per_group, axis=2).astype(jnp.float32)
    reads = jnp.repeat(read_map.reshape(spans, SPAN, GROUPS, STATE), per_group, axis=2).astype(jnp.float32)
    steps_blocked = step_size.reshape(HEADS, spans, SPAN).transpose(1, 0, 2)
    segments = resets.reshape(spans, SPAN)
    positions = jnp.arange(SPAN)
    lower = positions[:, None] >= positions[None, :]

    def span_update(states, item):
        value_block, write_block, read_block, step_block, reset_block = item
        cumulated = jnp.cumsum(-decay_rate[:, None] * step_block, axis=1)
        segment = jnp.cumsum(reset_block)
        causal = lower & (segment[:, None] == segment[None, :])
        gaps = cumulated[:, :, None] - cumulated[:, None, :]
        decay_matrix = jnp.where(causal[None], jnp.exp(jnp.where(causal[None], gaps, 0.0)), 0.0)
        scores = jnp.einsum('ihn,jhn->hij', read_block, write_block, precision=precise)
        mixing = scores * decay_matrix * step_block[:, None, :]
        within = jnp.einsum('hij,jhp->ihp', mixing, value_block, precision=precise)
        from_start = jnp.exp(cumulated) * (segment == 0)[None, :]
        across = jnp.einsum('ihn,hpn->ihp', read_block, states, precision=precise) * from_start.T[:, :, None]
        to_end = jnp.exp(cumulated[:, -1:] - cumulated) * (segment == segment[-1])[None, :] * step_block
        weighted = value_block * to_end.T[:, :, None]
        span_decay = jnp.exp(cumulated[:, -1]) * (segment[-1] == 0)
        updated = span_decay[:, None, None] * states + jnp.einsum('jhp,jhn->hpn', weighted, write_block, precision=precise)
        return (updated, within + across)
    empty_state = jnp.zeros((HEADS, HEAD_DIM, STATE), jnp.float32)
    _, outputs = lax.scan(span_update, empty_state, (values, writes, reads, steps_blocked, segments))
    mixed_out = outputs.reshape(TOKENS, HEADS * HEAD_DIM) + jnp.repeat(skip_gain, HEAD_DIM)[None, :] * values.reshape(TOKENS, HEADS * HEAD_DIM)
    gated = mixed_out * jax.nn.silu(gate_input.astype(jnp.float32))
    grouped = gated.reshape(TOKENS, GROUPS, -1)
    inverse_rms = lax.rsqrt(lax.optimization_barrier(jnp.mean(grouped * grouped, axis=2, keepdims=True)) + epsilon)
    normed = ((grouped * inverse_rms).reshape(TOKENS, -1) * norm_gain[None, :]).astype(jnp.bfloat16)
    branch = jnp.dot(normed, out_weight, preferred_element_type=jnp.float32)
    hidden = (residual.astype(jnp.float32) + branch).astype(jnp.bfloat16)
    chosen = hidden[scored]
    squares = lax.optimization_barrier(jnp.sum(jnp.square(chosen.astype(jnp.float32)), axis=1))
    features = (chosen.astype(jnp.float32) * lax.rsqrt(squares / D + epsilon)[:, None] * final_gain[None, :]).astype(jnp.bfloat16)
    logits = jnp.dot(features, head_weight, preferred_element_type=jnp.float32)
    row_top = lax.optimization_barrier(jnp.max(logits, axis=1))
    summed = lax.optimization_barrier(jnp.sum(jnp.exp(logits - row_top[:, None]), axis=1))
    picked = jnp.take_along_axis(logits, targets[:, None], axis=1)[:, 0]
    ref_logprob = picked - row_top - jnp.log(summed)
    token_kl = 0.5 * jnp.square(ref_logprob - policy_logprob)
    return (ref_logprob, token_kl)
```

```python
import functools

import jax
import jax.numpy as jnp
from jax import lax
from jax.experimental import pallas as pl
from jax.experimental.pallas import tpu as pltpu
from jax.sharding import Mesh
from jax.sharding import PartitionSpec as P

CTX = ("z", "x", "core")
SUB = ("x", "core")
PLANE = ("z", "tp")

epsilon = 1e-05
blocked = -1e9
precise = lax.Precision.HIGHEST
f32 = jnp.float32
bf16 = jnp.bfloat16


def exchange(blocks, axes):
    return lax.all_to_all(blocks, axes, 0, 0, tiled=True)


def to_everyone(shard, axes):
    return exchange(jnp.broadcast_to(shard[None], (lax.axis_size(axes), *shard.shape)), axes)


whole = pl.BlockSpec(memory_space=pltpu.VMEM)


def split(value, count):
    parts = []
    for _ in range(count):
        part = value.astype(bf16)
        parts.append(part)
        value = value - part.astype(f32)
    return parts


def exponent(value, axis):
    top = jnp.max(jnp.abs(value), axis=axis, keepdims=True)
    return jnp.floor(jnp.log2(jnp.maximum(top, 1e-30))) + 1.0


def coded(value, power):
    return jnp.clip(jnp.round(value * jnp.exp2(15.0 - power)), -32767.0, 32767.0)


def coded_log(value, free):
    high = jnp.round(value * 2048.0)
    low = jnp.round((value - high / 2048.0) * 2.0**26)
    return jnp.where(free, high, -32768.0), jnp.where(free, low, 0.0)


def decoded_log(high, low):
    return jnp.where(high < -32767.5, blocked, high / 2048.0 + low * 2.0**-26)


def local_kernel(
    place_ref, stream_ref, state_ref, tail_ref, gate_ref, step_ref, reset_ref, head_ref, taps_ref, state_taps_ref, out_ref, pad_ref
):
    rows, channels = stream_ref.shape
    states = state_ref.shape[2]
    heads = step_ref.shape[0]
    margin = tail_ref.shape[0]
    width = tail_ref.shape[1] - 128
    count = place_ref.shape[0]
    lane = lax.broadcasted_iota(jnp.int32, (8, 128), 1)
    line = lax.broadcasted_iota(jnp.int32, (8, 128), 0)

    flag = jnp.broadcast_to(reset_ref[...].astype(f32), (8, rows))
    free = 1.0 - flag
    earlier = 1.0 - tail_ref[:, width:].astype(f32)
    one, two = earlier[margin - 1 :], earlier[margin - 2 : margin - 1]
    second = free * jnp.where(lane == 0, one, pltpu.roll(free, 1, 1))
    third = second * jnp.where(lane == 0, two, jnp.where(lane == 1, one, pltpu.roll(free, 2, 1)))
    turned = jnp.where(line == 0, free, jnp.where(line == 1, second, third)).T
    keeping = [jnp.broadcast_to(turned[:, k : k + 1], (rows, 128)) for k in range(3)]

    def filtered(block, tail, taps):
        pad_ref[:margin] = tail.astype(f32)
        pad_ref[margin:] = block.astype(f32)
        summed = taps[0:1] * pad_ref[margin:]
        for k in range(1, 4):
            summed = summed + keeping[k - 1] * taps[k : k + 1] * pad_ref[margin - k : margin - k + rows]
        return (summed * jax.nn.sigmoid(summed)).astype(bf16)

    writes = filtered(state_ref[0], tail_ref[:, channels : channels + states], state_taps_ref[0])
    reads = filtered(state_ref[1], tail_ref[:, channels + states : width], state_taps_ref[1])

    chosen = lane == place_ref[...]
    pick = chosen.astype(bf16)
    rows_reads = jnp.dot(pick, reads, preferred_element_type=f32)
    first = lax.broadcasted_iota(jnp.int32, (rows, rows), 0)
    upto = (first <= lax.broadcasted_iota(jnp.int32, (rows, rows), 1)).astype(bf16)
    step = step_ref[...]
    drift = jnp.concatenate(split(-head_ref[:, 0:1] * step, 3), axis=0)
    summed = jnp.dot(drift, upto, preferred_element_type=f32)
    cumulated = summed[:heads] + summed[heads : 2 * heads] + summed[2 * heads :]
    segment = jnp.dot(flag.astype(bf16), upto, preferred_element_type=f32)
    rows_segment = jnp.sum(jnp.where(chosen, segment, 0.0), axis=1, keepdims=True)
    rows_log = jnp.sum(jnp.where(chosen[None], cumulated[:, None, :], 0.0), axis=2, keepdims=True)
    causal = (lane <= place_ref[...]) & (segment == rows_segment)
    scores = lax.dot_general(
        rows_reads.astype(bf16), writes, (((1,), (1,)), ((), ())), preferred_element_type=f32
    )
    gaps = jnp.where(causal[None], rows_log - cumulated[:, None, :], 0.0)
    mixing = jnp.where(causal[None], jnp.exp(gaps), 0.0) * scores[None] * step[:, None, :]
    mixing = mixing + jnp.where(chosen[None], head_ref[:, 1:2][:, :, None], 0.0)
    mixing = split(mixing.reshape(heads * count, rows), 3)

    end_segment = segment[0:1, rows - 1 :]
    end_log = cumulated[:, rows - 1 :]
    to_end = jnp.where(segment[0:1] == end_segment, jnp.exp(end_log - cumulated) * step, 0.0)
    end_high, end_low = coded_log(end_log, jnp.broadcast_to(end_segment == 0.0, end_log.shape))
    log_high, log_low = coded_log(rows_log, jnp.broadcast_to((rows_segment == 0.0)[None], rows_log.shape))

    power = exponent(rows_reads, 1)
    rows_reads = coded(rows_reads, power)
    folded = jnp.concatenate([pltpu.roll(rows_reads, 64, 1), rows_reads], axis=0)
    folded = jnp.broadcast_to(folded[None], (8, 16, 128)).reshape(128, 128)
    powers = jnp.broadcast_to(power, (8, 128))
    left = lane < 64
    wide = lax.broadcasted_iota(jnp.int32, (128, 128), 1)
    empty = jnp.zeros((80, 128), f32)
    for b in range(channels // 128):
        span = slice(b * 128, (b + 1) * 128)
        p, q = 2 * b, 2 * b + 1
        values = filtered(stream_ref[:, span], tail_ref[:, span], taps_ref[:, span])
        ends = jnp.concatenate(
            [jnp.broadcast_to(to_end[p : p + 1], (64, rows)), jnp.broadcast_to(to_end[q : q + 1], (64, rows))], axis=0
        )
        high, low = split(values.astype(f32).T * ends, 2)
        state = jnp.dot(high, writes, preferred_element_type=f32) + jnp.dot(low, writes, preferred_element_type=f32)
        both = jnp.concatenate([part[16 * b : 16 * b + 16] for part in mixing], axis=0)
        met = jnp.dot(both, values, preferred_element_type=f32)
        met = met[:16] + met[16:32] + met[32:]
        local = jnp.where(left, met[:8], met[8:])
        gate = jnp.dot(pick, gate_ref[:, span], preferred_element_type=f32)
        local_power, gate_power, state_power = exponent(local, 0), exponent(gate, 0), exponent(state, 1)
        others = jnp.where(line == 2, local_power, jnp.where(line == 3, gate_power, 0.0))
        others = jnp.where(line == 1, jnp.where(left, end_low[p : p + 1], end_low[q : q + 1]), others)
        others = jnp.where(line == 0, jnp.where(left, end_high[p : p + 1], end_high[q : q + 1]), others)
        side = jnp.concatenate(
            [
                coded(local, local_power),
                coded(gate, gate_power),
                jnp.where(left, log_high[p], log_high[q]),
                jnp.where(left, log_low[p], log_low[q]),
                others,
                powers,
                empty,
            ],
            axis=0,
        ).T
        side = jnp.where(wide == 36, state_power, jnp.where(wide < 64, side, folded))
        for at, part in ((0, coded(state, state_power)), (16, side)):
            part = part.astype(jnp.int32).reshape(8, 16, 128)
            out_ref[8 * b : 8 * b + 8, at : at + 16, :] = part.astype(jnp.int16)


def local_part(place, stream, states, tail, gate, step, resets, by_head, taps, state_taps):
    channels = stream.shape[1]
    return pl.pallas_call(
        local_kernel,
        out_shape=jax.ShapeDtypeStruct((channels // 16, 32, 128), jnp.int16),
        in_specs=[whole] * 10,
        out_specs=whole,
        scratch_shapes=[pltpu.VMEM((tail.shape[0] + stream.shape[0], 128), f32)],
        compiler_params=pltpu.CompilerParams(vmem_limit_bytes=16 * 2**20),
        cost_estimate=pl.CostEstimate(flops=1 << 27, bytes_accessed=2 << 20, transcendentals=1 << 18),
    )(place, stream, states, tail, gate, step, resets, by_head, taps, state_taps)


def project_kernel(gated_ref, gain_ref, weight_ref, out_ref):
    gated = gated_ref[...]
    lanes = gated.shape[1]
    half = lanes // 2
    depth = gated.shape[0]
    squares = jnp.broadcast_to(jnp.sum(gated * gated, axis=0, keepdims=True), (8, lanes))
    squares = squares + pltpu.roll(squares, half, 1)
    inverse = lax.rsqrt(squares[:1] / (2 * depth) + epsilon)
    normed = (gated * inverse * gain_ref[...]).T.astype(bf16)
    contract = (((1,), (1,)), ((), ()))
    out_ref[...] = lax.dot_general(
        normed[:half], weight_ref[:, :depth], contract, preferred_element_type=f32
    ) + lax.dot_general(normed[half:], weight_ref[:, depth:], contract, preferred_element_type=f32)


def project(gated, gain, weight):
    return pl.pallas_call(
        project_kernel,
        out_shape=jax.ShapeDtypeStruct((gated.shape[1] // 2, weight.shape[0]), f32),
        in_specs=[whole] * 3,
        out_specs=whole,
        compiler_params=pltpu.CompilerParams(vmem_limit_bytes=8 * 2**20),
        cost_estimate=pl.CostEstimate(flops=2 * 64 * 1024 * 512, bytes_accessed=1 << 21, transcendentals=0),
    )(gated, gain, weight)


def logits_kernel(start_ref, chosen_ref, gain_ref, target_ref, weight_ref, out_ref, total_ref, inverse_ref, *, steps, stride):
    step = pl.program_id(0)
    slabs, group, width = chosen_ref.shape
    subs, _, columns = weight_ref.shape

    @pl.when(step == 0)
    def _():
        squares = jnp.zeros((group, 1), f32)
        for k in range(slabs):
            slab = chosen_ref[k].astype(f32)
            squares = squares + jnp.sum(slab * slab, axis=1, keepdims=True)
        inverse_ref[...] = jnp.broadcast_to(lax.rsqrt(squares / (slabs * width) + epsilon), inverse_ref.shape)
        total_ref[...] = jnp.zeros_like(total_ref)

    features = chosen_ref[step].astype(f32) * inverse_ref[:, :1] * gain_ref[pl.ds(step, 1), :]
    weight = jnp.concatenate([weight_ref[k] for k in range(subs)], axis=1)
    total_ref[...] += jnp.dot(features.astype(bf16), weight, preferred_element_type=f32)

    @pl.when(step == steps - 1)
    def _():
        logits = total_ref[...]
        top = jnp.max(logits, axis=1, keepdims=True)
        summed = jnp.sum(jnp.exp(logits - top), axis=1, keepdims=True)
        picked = jnp.zeros((group, 1), f32)
        lane = lax.broadcasted_iota(jnp.int32, (group, columns), 1)
        for k in range(subs):
            own = lane + (start_ref[0] + k * stride) == target_ref[...]
            picked = picked + jnp.sum(
                jnp.where(own, logits[:, k * columns : (k + 1) * columns], 0.0), axis=1, keepdims=True
            )
        place = lax.broadcasted_iota(jnp.int32, (group, 128), 1)
        found = jnp.where(place == 0, top, jnp.where(place == 1, summed, picked)).T
        pair = jnp.concatenate([found[0:1], found[1:2], found[2:3], found[2:3]], axis=1)
        out_ref[...] = pair


def score(start, chosen, gain, target, weight, stride):
    slabs, group, width = chosen.shape
    subs, _, columns = weight.shape
    fixed = lambda *shape: pl.BlockSpec(shape, lambda k: (0,) * len(shape))
    return pl.pallas_call(
        functools.partial(logits_kernel, steps=slabs, stride=stride),
        grid=(slabs,),
        out_shape=jax.ShapeDtypeStruct((1, 4 * group), f32),
        in_specs=[
            pl.BlockSpec(memory_space=pltpu.SMEM),
            fixed(slabs, group, width),
            fixed(slabs, width),
            fixed(group, 1),
            pl.BlockSpec((subs, width, columns), lambda k: (0, k, 0)),
        ],
        out_specs=fixed(1, 4 * group),
        scratch_shapes=[pltpu.VMEM((group, subs * columns), f32), pltpu.VMEM((group, 128), f32)],
        compiler_params=pltpu.CompilerParams(
            dimension_semantics=("arbitrary",), vmem_limit_bytes=24 * 2**20
        ),
        cost_estimate=pl.CostEstimate(flops=2 * 64 * 4096 * 1024, bytes_accessed=9 << 20, transcendentals=0),
    )(start, chosen, gain, target, weight)


def body(
    inner_input,
    gate_input,
    state_inputs,
    step_size,
    resets,
    decay_rate,
    skip_gain,
    conv_inner,
    conv_state,
    norm_gain,
    out_weight,
    residual,
    final_gain,
    head_weight,
    scored,
    targets,
    policy_logprob,
):
    rows, channels = inner_input.shape
    chunks = lax.axis_size(CTX)
    part = channels // chunks
    planes, subs = lax.axis_size("z"), lax.axis_size(SUB)
    count = scored.shape[0]
    group = planes * count
    total = chunks * count
    local_rows = scored - lax.axis_index(CTX) * rows

    margin = 16
    flags = jnp.broadcast_to(resets[rows - margin :, None].astype(bf16), (margin, 128))
    tail = [inner_input[rows - margin :], state_inputs[0, rows - margin :], state_inputs[1, rows - margin :], flags]
    tail = lax.ppermute(jnp.concatenate(tail, axis=1), CTX, [(i, i + 1) for i in range(chunks - 1)])

    half = part // 2
    by_half = lambda a: jnp.swapaxes(a.reshape(chunks, 2, half, -1), 0, 1).reshape(channels, -1)
    out_full = lax.all_gather(by_half(out_weight).T, SUB, axis=0, tiled=True)
    gain = by_half(norm_gain)
    gain = jnp.repeat(gain.reshape(2, channels // 2), group, axis=0).T
    head_full = lax.all_gather(head_weight, SUB, axis=0)
    pick = (jnp.arange(rows)[None, :] == local_rows[:, None]).astype(bf16)
    rows_residual = jnp.dot(pick, residual, preferred_element_type=f32).astype(bf16)
    swap = [(i * planes + k, k * planes + i) for i in range(planes) for k in range(planes)]
    rows_residual = lax.ppermute(rows_residual, PLANE, swap)
    own = lax.dynamic_index_in_dim(targets.reshape(planes, subs, count), lax.axis_index(SUB), 1, False).reshape(group, 1)

    by_head = jnp.stack([decay_rate, skip_gain], axis=1)
    message = local_part(
        local_rows.reshape(-1, 1), inner_input, state_inputs, tail, gate_input, step_size, resets.reshape(1, rows), by_head, conv_inner, conv_state
    )
    message, rows_residual = lax.optimization_barrier((message, rows_residual))
    came = exchange(message, CTX)

    side = came[:, part:].astype(f32)
    states = (came[:, :part].astype(f32) * jnp.exp2(side[:, :, 36:37] - 15.0)).reshape(channels, -1)
    one = side[:, 0]
    reads = jnp.concatenate([side[:, :count, 64:], side[:, count:, 64:]], axis=2)
    reads = reads * jnp.exp2(one[:, 40:48] - 15.0)[:, :, None]

    def by_group(a):
        return jnp.swapaxes(a.reshape(planes, subs, *a.shape[1:]), 0, 1)

    reads = by_group(reads).reshape(total, -1)
    met = lax.dot_general(states, reads, (((1,), (1,)), ((), ())), precision=lax.Precision.HIGH).reshape(chunks, part, total)
    end_log = decoded_log(one[:, 32], one[:, 33])
    rows_log = by_group(decoded_log(one[:, 16:24], one[:, 24:32])).reshape(1, total)
    lane = jnp.arange(total)
    chunk_of = (lane // count) % planes * subs + lane // group
    index = jnp.arange(chunks)
    before = index[:, None] < chunk_of[None, :]
    between = jnp.dot(
        (index[None, :] > index[:, None]).astype(f32), jnp.where(before, end_log[:, None], 0.0), precision=precise
    )
    weights = jnp.where(before, jnp.exp(between + rows_log), 0.0)
    across = jnp.sum(weights[:, None, :] * met, axis=0)
    local = side[:, :, :8] * jnp.exp2(side[:, :, 34:35] - 15.0)
    gate = side[:, :, 8:16] * jnp.exp2(side[:, :, 35:36] - 15.0)
    pair = jnp.stack([local, gate], axis=0).reshape(2, planes, subs, part, count)
    local, gate = pair.transpose(0, 3, 2, 1, 4).reshape(2, part, total)
    gated = (across + local) * jax.nn.silu(gate)
    gated = gated.reshape(2, half, subs, group).transpose(2, 1, 0, 3).reshape(subs, half, 2 * group)
    gated = jnp.broadcast_to(gated[None], (planes, subs, half, 2 * group)).reshape(chunks, half, 2 * group)

    gated = exchange(gated, CTX).reshape(channels // 2, 2 * group)

    partial = exchange(project(gated, gain, out_full).reshape(planes, count, -1), "tp")
    chosen = (jnp.sum(partial, axis=0) + rows_residual.astype(f32)).astype(bf16)

    chosen = to_everyone(chosen, PLANE).reshape(planes, group, -1)
    columns = head_weight.shape[1]
    ways = lax.axis_size("tp")
    start = (lax.axis_index("z") * subs * ways + lax.axis_index("tp")) * columns
    found = score(start.reshape(1), chosen, final_gain.reshape(planes, -1), own, head_full, ways * columns)

    found = to_everyone(found, PLANE).reshape(chunks, 4, group)
    top = jnp.max(found[:, 0], axis=0)
    summed = jnp.sum(found[:, 1] * jnp.exp(found[:, 0] - top[None, :]), axis=0)
    ref = jnp.sum(found[:, 2], axis=0) - top - jnp.log(summed)
    ref = to_everyone(ref.reshape(planes, count), SUB)
    ref_logprob = ref.swapaxes(0, 1).reshape(total)
    token_kl = 0.5 * jnp.square(ref_logprob - policy_logprob)
    return (ref_logprob, token_kl)


def solution(mesh):
    heads_split = mesh.shape["tp"]
    finer = Mesh(mesh.devices.reshape(heads_split, -1, 2, heads_split), ("z", "x", "core", "tp"))
    placed = (
        P(CTX, "tp"),
        P(CTX, "tp"),
        P(None, CTX, "tp"),
        P("tp", CTX),
        P(CTX),
        P("tp"),
        P("tp"),
        P(None, "tp"),
        P(None, None, "tp"),
        P("tp"),
        P("tp", CTX),
        P(CTX, "tp"),
        P(),
        P(None, (*CTX, "tp")),
        P(CTX),
        P(),
        P(),
    )
    return jax.shard_map(body, mesh=finer, in_specs=placed, out_specs=(P(), P()), check_vma=False)
```

```python
import functools

import jax
import jax.numpy as jnp
from jax import lax
from jax.experimental import pallas as pl
from jax.experimental.pallas import tpu as pltpu
from jax.sharding import Mesh
from jax.sharding import PartitionSpec as P

CTX = ("z", "x", "core")
SUB = ("x", "core")
PLANE = ("z", "tp")

epsilon = 1e-05
blocked = -1e9
precise = lax.Precision.HIGHEST
f32 = jnp.float32
bf16 = jnp.bfloat16


def exchange(blocks, axes):
    return lax.all_to_all(blocks, axes, 0, 0, tiled=True)


def to_everyone(shard, axes):
    return exchange(jnp.broadcast_to(shard[None], (lax.axis_size(axes), *shard.shape)), axes)


whole = pl.BlockSpec(memory_space=pltpu.VMEM)


def split(value, count):
    parts = []
    for _ in range(count):
        part = value.astype(bf16)
        parts.append(part)
        value = value - part.astype(f32)
    return parts


def exponent(value, axis):
    top = jnp.max(jnp.abs(value), axis=axis, keepdims=True)
    return jnp.floor(jnp.log2(jnp.maximum(top, 1e-30))) + 1.0


def coded(value, power):
    return jnp.clip(jnp.round(value * jnp.exp2(15.0 - power)), -32767.0, 32767.0)


def coded_log(value, free):
    high = jnp.round(value * 2048.0)
    low = jnp.round((value - high / 2048.0) * 2.0**26)
    return jnp.where(free, high, -32768.0), jnp.where(free, low, 0.0)


def decoded_log(high, low):
    return jnp.where(high < -32767.5, blocked, high / 2048.0 + low * 2.0**-26)


def local_kernel(
    place_ref, stream_ref, state_ref, tail_ref, gate_ref, step_ref, reset_ref, head_ref, taps_ref, state_taps_ref, out_ref, pad_ref
):
    rows, channels = stream_ref.shape
    states = state_ref.shape[2]
    heads = step_ref.shape[0]
    margin = tail_ref.shape[0]
    width = tail_ref.shape[1] - 128
    count = place_ref.shape[0]
    lane = lax.broadcasted_iota(jnp.int32, (8, 128), 1)
    line = lax.broadcasted_iota(jnp.int32, (8, 128), 0)

    flag = jnp.broadcast_to(reset_ref[...].astype(f32), (8, rows))
    free = 1.0 - flag
    earlier = 1.0 - tail_ref[:, width:].astype(f32)
    one, two = earlier[margin - 1 :], earlier[margin - 2 : margin - 1]
    second = free * jnp.where(lane == 0, one, pltpu.roll(free, 1, 1))
    third = second * jnp.where(lane == 0, two, jnp.where(lane == 1, one, pltpu.roll(free, 2, 1)))
    turned = jnp.where(line == 0, free, jnp.where(line == 1, second, third)).T
    keeping = [jnp.broadcast_to(turned[:, k : k + 1], (rows, 128)) for k in range(3)]

    def filtered(block, tail, taps):
        pad_ref[:margin] = tail.astype(f32)
        pad_ref[margin:] = block.astype(f32)
        summed = taps[0:1] * pad_ref[margin:]
        for k in range(1, 4):
            summed = summed + keeping[k - 1] * taps[k : k + 1] * pad_ref[margin - k : margin - k + rows]
        return (summed * jax.nn.sigmoid(summed)).astype(bf16)

    writes = filtered(state_ref[0], tail_ref[:, channels : channels + states], state_taps_ref[0])
    reads = filtered(state_ref[1], tail_ref[:, channels + states : width], state_taps_ref[1])

    chosen = lane == place_ref[...]
    pick = chosen.astype(bf16)
    rows_reads = jnp.dot(pick, reads, preferred_element_type=f32)
    first = lax.broadcasted_iota(jnp.int32, (rows, rows), 0)
    upto = (first <= lax.broadcasted_iota(jnp.int32, (rows, rows), 1)).astype(bf16)
    step = step_ref[...]
    drift = jnp.concatenate(split(-head_ref[:, 0:1] * step, 3), axis=0)
    summed = jnp.dot(drift, upto, preferred_element_type=f32)
    cumulated = summed[:heads] + summed[heads : 2 * heads] + summed[2 * heads :]
    segment = jnp.dot(flag.astype(bf16), upto, preferred_element_type=f32)
    rows_segment = jnp.sum(jnp.where(chosen, segment, 0.0), axis=1, keepdims=True)
    rows_log = jnp.sum(jnp.where(chosen[None], cumulated[:, None, :], 0.0), axis=2, keepdims=True)
    causal = (lane <= place_ref[...]) & (segment == rows_segment)
    scores = lax.dot_general(
        rows_reads.astype(bf16), writes, (((1,), (1,)), ((), ())), preferred_element_type=f32
    )
    gaps = jnp.where(causal[None], rows_log - cumulated[:, None, :], 0.0)
    mixing = jnp.where(causal[None], jnp.exp(gaps), 0.0) * scores[None] * step[:, None, :]
    mixing = mixing + jnp.where(chosen[None], head_ref[:, 1:2][:, :, None], 0.0)
    mixing = split(mixing.reshape(heads * count, rows), 3)

    end_segment = segment[0:1, rows - 1 :]
    end_log = cumulated[:, rows - 1 :]
    to_end = jnp.where(segment[0:1] == end_segment, jnp.exp(end_log - cumulated) * step, 0.0)
    end_high, end_low = coded_log(end_log, jnp.broadcast_to(end_segment == 0.0, end_log.shape))
    log_high, log_low = coded_log(rows_log, jnp.broadcast_to((rows_segment == 0.0)[None], rows_log.shape))

    power = exponent(rows_reads, 1)
    rows_reads = coded(rows_reads, power)
    folded = jnp.concatenate([pltpu.roll(rows_reads, 64, 1), rows_reads], axis=0)
    folded = jnp.broadcast_to(folded[None], (8, 16, 128)).reshape(128, 128)
    powers = jnp.broadcast_to(power, (8, 128))
    left = lane < 64
    wide = lax.broadcasted_iota(jnp.int32, (128, 128), 1)
    empty = jnp.zeros((80, 128), f32)
    for b in range(channels // 128):
        span = slice(b * 128, (b + 1) * 128)
        p, q = 2 * b, 2 * b + 1
        values = filtered(stream_ref[:, span], tail_ref[:, span], taps_ref[:, span])
        ends = jnp.concatenate(
            [jnp.broadcast_to(to_end[p : p + 1], (64, rows)), jnp.broadcast_to(to_end[q : q + 1], (64, rows))], axis=0
        )
        high, low = split(values.astype(f32).T * ends, 2)
        state = jnp.dot(high, writes, preferred_element_type=f32) + jnp.dot(low, writes, preferred_element_type=f32)
        both = jnp.concatenate([part[16 * b : 16 * b + 16] for part in mixing], axis=0)
        met = jnp.dot(both, values, preferred_element_type=f32)
        met = met[:16] + met[16:32] + met[32:]
        local = jnp.where(left, met[:8], met[8:])
        gate = jnp.dot(pick, gate_ref[:, span], preferred_element_type=f32)
        local_power, gate_power, state_power = exponent(local, 0), exponent(gate, 0), exponent(state, 1)
        others = jnp.where(line == 2, local_power, jnp.where(line == 3, gate_power, 0.0))
        others = jnp.where(line == 1, jnp.where(left, end_low[p : p + 1], end_low[q : q + 1]), others)
        others = jnp.where(line == 0, jnp.where(left, end_high[p : p + 1], end_high[q : q + 1]), others)
        side = jnp.concatenate(
            [
                coded(local, local_power),
                coded(gate, gate_power),
                jnp.where(left, log_high[p], log_high[q]),
                jnp.where(left, log_low[p], log_low[q]),
                others,
                powers,
                empty,
            ],
            axis=0,
        ).T
        side = jnp.where(wide == 36, state_power, jnp.where(wide < 64, side, folded))
        for at, part in ((0, coded(state, state_power)), (16, side)):
            part = part.astype(jnp.int32).reshape(8, 16, 128)
            out_ref[8 * b : 8 * b + 8, at : at + 16, :] = part.astype(jnp.int16)


def local_part(place, stream, states, tail, gate, step, resets, by_head, taps, state_taps):
    channels = stream.shape[1]
    return pl.pallas_call(
        local_kernel,
        out_shape=jax.ShapeDtypeStruct((channels // 16, 32, 128), jnp.int16),
        in_specs=[whole] * 10,
        out_specs=whole,
        scratch_shapes=[pltpu.VMEM((tail.shape[0] + stream.shape[0], 128), f32)],
        compiler_params=pltpu.CompilerParams(vmem_limit_bytes=58 * 2**20),
        cost_estimate=pl.CostEstimate(flops=1 << 27, bytes_accessed=2 << 20, transcendentals=1 << 18),
    )(place, stream, states, tail, gate, step, resets, by_head, taps, state_taps)


def carry_kernel(came_ref, out_ref, side_ref, met_ref, weight_ref, *, planes, subs):
    chunks, _, states = came_ref.shape
    part = 16
    count = 8
    group = planes * count
    total = chunks * count
    side = came_ref[:, part:, :].astype(jnp.int32).astype(f32)
    side_ref[...] = side.reshape(chunks * part, 128)
    scale = jnp.exp2(side - 15.0)
    state = came_ref[:, :part, :].astype(jnp.int32).astype(f32) * scale[:, :, 36:37]
    state_high, state_low = split(state.reshape(chunks * part, states), 2)
    wide = lax.broadcasted_iota(jnp.int32, (chunks, 8, 128), 2)
    reads = jnp.where(wide < 64, pltpu.roll(side[:, :8], 64, 2), side[:, 8:])
    order = [z * subs + k for k in range(subs) for z in range(planes)]
    reads = jnp.concatenate([reads[c] for c in order], axis=0)
    reads_high, reads_low = split(reads, 2)
    contract = (((1,), (1,)), ((), ()))
    met_ref[...] = (
        lax.dot_general(state_high, reads_high, contract, preferred_element_type=f32)
        + lax.dot_general(state_high, reads_low, contract, preferred_element_type=f32)
        + lax.dot_general(state_low, reads_high, contract, preferred_element_type=f32)
    )

    lane = lax.broadcasted_iota(jnp.int32, (8, 128), 1)

    def by_lane(block_of, offset):
        columns = []
        for j in range(chunks // 16):
            column = None
            for i in range(16):
                block = block_of(order[16 * j + i])
                tall = block.shape[0]
                if (8 * i - offset) % 128:
                    block = pltpu.roll(block, (8 * i - offset) % 128, 1)
                place = lax.broadcasted_iota(jnp.int32, (tall, 128), 1)
                column = block if column is None else jnp.where(place >= 8 * i, block, column)
            columns.append(column)
        return jnp.concatenate(columns, axis=1)

    local = side * scale[:, :, 34:35]
    gate = side * scale[:, :, 35:36]
    local = by_lane(lambda c: local[c], 0)
    gate = by_lane(lambda c: gate[c], 8)
    log_high = by_lane(lambda c: side[c, :8], 16)[:1]
    log_low = by_lane(lambda c: side[c, :8], 24)[:1]
    power = by_lane(lambda c: side[c, :8], 40)[:1]
    rows_log = decoded_log(log_high, log_low)

    one = side_ref[pl.ds(0, chunks, stride=part), :]
    end_log = decoded_log(one[:, 32:33], one[:, 33:34])
    chunk = lax.broadcasted_iota(jnp.int32, (chunks, total), 0)
    at = lax.broadcasted_iota(jnp.int32, (chunks, total), 1)
    before = chunk < ((at // count) % planes) * subs + at // group
    upper = lax.broadcasted_iota(jnp.int32, (chunks, chunks), 0) < lax.broadcasted_iota(jnp.int32, (chunks, chunks), 1)
    upper = upper.astype(bf16)
    between = jnp.zeros((chunks, total), f32)
    for piece in split(jnp.where(before, end_log, 0.0), 3):
        between = between + jnp.dot(upper, piece, preferred_element_type=f32)
    weight_ref[...] = jnp.where(before, jnp.exp(between + rows_log), 0.0) * jnp.exp2(power - 15.0)

    across = jnp.zeros((part, total), f32)
    for c in range(chunks):
        across = across + weight_ref[c : c + 1, :] * met_ref[part * c : part * c + part, :]
    gated = (across + local) * (gate * jax.nn.sigmoid(gate))
    for k in range(subs):
        columns = slice(k // 2 * 128, k // 2 * 128 + 128)
        first, second = gated[:8, columns], gated[8:, columns]
        if k % 2:
            first = pltpu.roll(first, 64, 1)
        else:
            second = pltpu.roll(second, 64, 1)
        tile = jnp.where(lane < 64, first, second)
        for z in range(planes):
            out_ref[z * subs + k] = tile


def carry(came, planes, subs):
    chunks = came.shape[0]
    return pl.pallas_call(
        functools.partial(carry_kernel, planes=planes, subs=subs),
        out_shape=jax.ShapeDtypeStruct((chunks, 8, 128), f32),
        in_specs=[whole],
        out_specs=whole,
        scratch_shapes=[
            pltpu.VMEM((chunks * 16, 128), f32),
            pltpu.VMEM((chunks * 16, chunks * 8), f32),
            pltpu.VMEM((chunks, chunks * 8), f32),
        ],
        compiler_params=pltpu.CompilerParams(vmem_limit_bytes=24 * 2**20),
        cost_estimate=pl.CostEstimate(flops=1 << 28, bytes_accessed=1 << 20, transcendentals=1 << 16),
    )(came)


def project_kernel(gated_ref, gain_ref, weight_ref, out_ref):
    gated = gated_ref[...]
    depth, lanes = gated.shape
    half = lanes // 2
    squares = jnp.broadcast_to(jnp.sum(gated * gated, axis=0, keepdims=True), (8, lanes))
    squares = squares + pltpu.roll(squares, half, 1)
    normed = gated * lax.rsqrt(squares[:1] / (2 * depth) + epsilon)
    pair = [a.reshape(depth // 8, 1, 8, lanes) for a in (normed, pltpu.roll(normed, half, 1))]
    normed = jnp.concatenate(pair, axis=1).reshape(2 * depth, lanes).T[:half]
    normed = (normed * gain_ref[...]).astype(bf16)
    out_ref[...] = lax.dot_general(
        normed, weight_ref[...], (((1,), (1,)), ((), ())), preferred_element_type=f32
    )


def project(gated, gain, weight):
    return pl.pallas_call(
        project_kernel,
        out_shape=jax.ShapeDtypeStruct((gated.shape[1] // 2, weight.shape[0]), f32),
        in_specs=[whole] * 3,
        out_specs=whole,
        compiler_params=pltpu.CompilerParams(vmem_limit_bytes=8 * 2**20),
        cost_estimate=pl.CostEstimate(flops=2 * 64 * 1024 * 512, bytes_accessed=1 << 21, transcendentals=0),
    )(gated, gain, weight)


def logits_kernel(start_ref, chosen_ref, gain_ref, target_ref, weight_ref, out_ref, total_ref, inverse_ref, *, steps, stride):
    step = pl.program_id(0)
    slabs, group, width = chosen_ref.shape
    subs, _, columns = weight_ref.shape

    @pl.when(step == 0)
    def _():
        squares = jnp.zeros((group, 1), f32)
        for k in range(slabs):
            slab = chosen_ref[k].astype(f32)
            squares = squares + jnp.sum(slab * slab, axis=1, keepdims=True)
        inverse_ref[...] = jnp.broadcast_to(lax.rsqrt(squares / (slabs * width) + epsilon), inverse_ref.shape)
        total_ref[...] = jnp.zeros_like(total_ref)

    features = chosen_ref[step].astype(f32) * inverse_ref[:, :1] * gain_ref[pl.ds(step, 1), :]
    weight = jnp.concatenate([weight_ref[k] for k in range(subs)], axis=1)
    total_ref[...] += jnp.dot(features.astype(bf16), weight, preferred_element_type=f32)

    @pl.when(step == steps - 1)
    def _():
        logits = total_ref[...]
        top = jnp.max(logits, axis=1, keepdims=True)
        summed = jnp.sum(jnp.exp(logits - top), axis=1, keepdims=True)
        picked = jnp.zeros((group, 1), f32)
        lane = lax.broadcasted_iota(jnp.int32, (group, columns), 1)
        for k in range(subs):
            own = lane + (start_ref[0] + k * stride) == target_ref[...]
            picked = picked + jnp.sum(
                jnp.where(own, logits[:, k * columns : (k + 1) * columns], 0.0), axis=1, keepdims=True
            )
        place = lax.broadcasted_iota(jnp.int32, (group, 128), 1)
        found = jnp.where(place == 0, top, jnp.where(place == 1, summed, picked)).T
        pair = jnp.concatenate([found[0:1], found[1:2], found[2:3], found[2:3]], axis=1)
        out_ref[...] = pair


def score(start, chosen, gain, target, weight, stride):
    slabs, group, width = chosen.shape
    subs, _, columns = weight.shape
    fixed = lambda *shape: pl.BlockSpec(shape, lambda k: (0,) * len(shape))
    return pl.pallas_call(
        functools.partial(logits_kernel, steps=slabs, stride=stride),
        grid=(slabs,),
        out_shape=jax.ShapeDtypeStruct((1, 4 * group), f32),
        in_specs=[
            pl.BlockSpec(memory_space=pltpu.SMEM),
            fixed(slabs, group, width),
            fixed(slabs, width),
            fixed(group, 1),
            pl.BlockSpec((subs, width, columns), lambda k: (0, k, 0)),
        ],
        out_specs=fixed(1, 4 * group),
        scratch_shapes=[pltpu.VMEM((group, subs * columns), f32), pltpu.VMEM((group, 128), f32)],
        compiler_params=pltpu.CompilerParams(
            dimension_semantics=("arbitrary",), vmem_limit_bytes=58 * 2**20
        ),
        cost_estimate=pl.CostEstimate(flops=2 * 64 * 4096 * 1024, bytes_accessed=9 << 20, transcendentals=0),
    )(start, chosen, gain, target, weight)


def body(
    inner_input,
    gate_input,
    state_inputs,
    step_size,
    resets,
    decay_rate,
    skip_gain,
    conv_inner,
    conv_state,
    norm_gain,
    out_weight,
    residual,
    final_gain,
    head_weight,
    scored,
    targets,
    policy_logprob,
):
    rows, channels = inner_input.shape
    chunks = lax.axis_size(CTX)
    part = channels // chunks
    planes, subs = lax.axis_size("z"), lax.axis_size(SUB)
    count = scored.shape[0]
    group = planes * count
    total = chunks * count
    local_rows = scored - lax.axis_index(CTX) * rows

    margin = 16
    flags = jnp.broadcast_to(resets[rows - margin :, None].astype(bf16), (margin, 128))
    tail = [inner_input[rows - margin :], state_inputs[0, rows - margin :], state_inputs[1, rows - margin :], flags]
    tail = lax.ppermute(jnp.concatenate(tail, axis=1), CTX, [(i, i + 1) for i in range(chunks - 1)])

    out_full = lax.all_gather(out_weight.T, SUB, axis=0, tiled=True)
    head_full = lax.all_gather(head_weight, SUB, axis=0)
    pick = (jnp.arange(rows)[None, :] == local_rows[:, None]).astype(bf16)
    rows_residual = jnp.dot(pick, residual, preferred_element_type=f32).astype(bf16)
    own = lax.dynamic_index_in_dim(targets.reshape(planes, subs, count), lax.axis_index(SUB), 1, False).reshape(group, 1)

    by_head = jnp.stack([decay_rate, skip_gain], axis=1)
    message = local_part(
        local_rows.reshape(-1, 1), inner_input, state_inputs, tail, gate_input, step_size, resets.reshape(1, rows), by_head, conv_inner, conv_state
    )
    message, rows_residual = lax.optimization_barrier((message, rows_residual))
    came = exchange(message, CTX)
    swap = [(i * planes + k, k * planes + i) for i in range(planes) for k in range(planes)]
    rows_residual = lax.ppermute(rows_residual, PLANE, swap)
    came, rows_residual = lax.optimization_barrier((came, rows_residual))

    gated, out_full = lax.optimization_barrier((carry(came, planes, subs), out_full))
    gated = exchange(gated, CTX).reshape(channels // 2, 2 * group)

    partial = exchange(project(gated, norm_gain.reshape(1, -1), out_full).reshape(planes, count, -1), "tp")
    chosen = (jnp.sum(partial, axis=0) + rows_residual.astype(f32)).astype(bf16)

    chosen = to_everyone(chosen, PLANE).reshape(planes, group, -1)
    columns = head_weight.shape[1]
    ways = lax.axis_size("tp")
    start = (lax.axis_index("z") * subs * ways + lax.axis_index("tp")) * columns
    found = score(start.reshape(1), chosen, final_gain.reshape(planes, -1), own, head_full, ways * columns)

    found = to_everyone(found, PLANE).reshape(chunks, 4, group)
    top = jnp.max(found[:, 0], axis=0)
    summed = jnp.sum(found[:, 1] * jnp.exp(found[:, 0] - top[None, :]), axis=0)
    ref = jnp.sum(found[:, 2], axis=0) - top - jnp.log(summed)
    ref = to_everyone(ref.reshape(planes, count), SUB)
    ref_logprob = ref.swapaxes(0, 1).reshape(total)
    token_kl = 0.5 * jnp.square(ref_logprob - policy_logprob)
    return (ref_logprob, token_kl)


def solution(mesh):
    heads_split = mesh.shape["tp"]
    finer = Mesh(mesh.devices.reshape(heads_split, -1, 2, heads_split), ("z", "x", "core", "tp"))
    placed = (
        P(CTX, "tp"),
        P(CTX, "tp"),
        P(None, CTX, "tp"),
        P("tp", CTX),
        P(CTX),
        P("tp"),
        P("tp"),
        P(None, "tp"),
        P(None, None, "tp"),
        P("tp"),
        P("tp", CTX),
        P(CTX, "tp"),
        P(),
        P(None, (*CTX, "tp")),
        P(CTX),
        P(),
        P(),
    )
    return jax.shard_map(body, mesh=finer, in_specs=placed, out_specs=(P(), P()), check_vma=False)
```

```python
import functools

import jax
import jax.numpy as jnp
from jax import lax
from jax.experimental import pallas as pl
from jax.experimental.pallas import tpu as pltpu
from jax.sharding import Mesh
from jax.sharding import PartitionSpec as P

CTX = ("z", "x", "core")
SUB = ("x", "core")
PLANE = ("z", "tp")

epsilon = 1e-05
blocked = -1e9
precise = lax.Precision.HIGHEST
f32 = jnp.float32
bf16 = jnp.bfloat16


def exchange(blocks, axes):
    return lax.all_to_all(blocks, axes, 0, 0, tiled=True)


def to_everyone(shard, axes):
    return exchange(jnp.broadcast_to(shard[None], (lax.axis_size(axes), *shard.shape)), axes)


whole = pl.BlockSpec(memory_space=pltpu.VMEM)


def split(value, count):
    parts = []
    for _ in range(count):
        part = value.astype(bf16)
        parts.append(part)
        value = value - part.astype(f32)
    return parts


def exponent(value, axis):
    top = jnp.max(jnp.abs(value), axis=axis, keepdims=True)
    return jnp.floor(jnp.log2(jnp.maximum(top, 1e-30))) + 1.0


def coded(value, power):
    return jnp.clip(jnp.round(value * jnp.exp2(15.0 - power)), -32767.0, 32767.0)


def coded_log(value, free):
    high = jnp.round(value * 2048.0)
    low = jnp.round((value - high / 2048.0) * 2.0**26)
    return jnp.where(free, high, -32768.0), jnp.where(free, low, 0.0)


def decoded_log(high, low):
    return jnp.where(high < -32767.5, blocked, high / 2048.0 + low * 2.0**-26)


def local_kernel(
    place_ref, stream_ref, state_ref, tail_ref, gate_ref, step_ref, reset_ref, head_ref, taps_ref, state_taps_ref, out_ref, pad_ref
):
    rows, channels = stream_ref.shape
    states = state_ref.shape[2]
    heads = step_ref.shape[0]
    margin = tail_ref.shape[0]
    width = tail_ref.shape[1] - 128
    count = place_ref.shape[0]
    lane = lax.broadcasted_iota(jnp.int32, (8, 128), 1)
    line = lax.broadcasted_iota(jnp.int32, (8, 128), 0)

    flag = jnp.broadcast_to(reset_ref[...].astype(f32), (8, rows))
    free = 1.0 - flag
    earlier = 1.0 - tail_ref[:, width:].astype(f32)
    one, two = earlier[margin - 1 :], earlier[margin - 2 : margin - 1]
    second = free * jnp.where(lane == 0, one, pltpu.roll(free, 1, 1))
    third = second * jnp.where(lane == 0, two, jnp.where(lane == 1, one, pltpu.roll(free, 2, 1)))
    turned = jnp.where(line == 0, free, jnp.where(line == 1, second, third)).T
    keeping = [jnp.broadcast_to(turned[:, k : k + 1], (rows, 128)) for k in range(3)]

    def filtered(block, tail, taps):
        pad_ref[:margin] = tail.astype(f32)
        pad_ref[margin:] = block.astype(f32)
        summed = taps[0:1] * pad_ref[margin:]
        for k in range(1, 4):
            summed = summed + keeping[k - 1] * taps[k : k + 1] * pad_ref[margin - k : margin - k + rows]
        return (summed * jax.nn.sigmoid(summed)).astype(bf16)

    writes = filtered(state_ref[0], tail_ref[:, channels : channels + states], state_taps_ref[0])
    reads = filtered(state_ref[1], tail_ref[:, channels + states : width], state_taps_ref[1])

    chosen = lane == place_ref[...]
    pick = chosen.astype(bf16)
    rows_reads = jnp.dot(pick, reads, preferred_element_type=f32)
    first = lax.broadcasted_iota(jnp.int32, (rows, rows), 0)
    upto = (first <= lax.broadcasted_iota(jnp.int32, (rows, rows), 1)).astype(bf16)
    step = step_ref[...]
    drift = jnp.concatenate(split(-head_ref[:, 0:1] * step, 3), axis=0)
    summed = jnp.dot(drift, upto, preferred_element_type=f32)
    cumulated = summed[:heads] + summed[heads : 2 * heads] + summed[2 * heads :]
    segment = jnp.dot(flag.astype(bf16), upto, preferred_element_type=f32)
    rows_segment = jnp.sum(jnp.where(chosen, segment, 0.0), axis=1, keepdims=True)
    rows_log = jnp.sum(jnp.where(chosen[None], cumulated[:, None, :], 0.0), axis=2, keepdims=True)
    causal = (lane <= place_ref[...]) & (segment == rows_segment)
    scores = lax.dot_general(
        rows_reads.astype(bf16), writes, (((1,), (1,)), ((), ())), preferred_element_type=f32
    )
    gaps = jnp.where(causal[None], rows_log - cumulated[:, None, :], 0.0)
    mixing = jnp.where(causal[None], jnp.exp(gaps), 0.0) * scores[None] * step[:, None, :]
    mixing = mixing + jnp.where(chosen[None], head_ref[:, 1:2][:, :, None], 0.0)
    mixing = split(mixing.reshape(heads * count, rows), 3)

    end_segment = segment[0:1, rows - 1 :]
    end_log = cumulated[:, rows - 1 :]
    to_end = jnp.where(segment[0:1] == end_segment, jnp.exp(end_log - cumulated) * step, 0.0)
    end_high, end_low = coded_log(end_log, jnp.broadcast_to(end_segment == 0.0, end_log.shape))
    log_high, log_low = coded_log(rows_log, jnp.broadcast_to((rows_segment == 0.0)[None], rows_log.shape))

    power = exponent(rows_reads, 1)
    rows_reads = coded(rows_reads, power)
    folded = jnp.concatenate([pltpu.roll(rows_reads, 64, 1), rows_reads], axis=0)
    folded = jnp.broadcast_to(folded[None], (8, 16, 128)).reshape(128, 128)
    powers = jnp.broadcast_to(power, (8, 128))
    left = lane < 64
    wide = lax.broadcasted_iota(jnp.int32, (128, 128), 1)
    empty = jnp.zeros((80, 128), f32)
    for b in range(channels // 128):
        span = slice(b * 128, (b + 1) * 128)
        p, q = 2 * b, 2 * b + 1
        values = filtered(stream_ref[:, span], tail_ref[:, span], taps_ref[:, span])
        ends = jnp.concatenate(
            [jnp.broadcast_to(to_end[p : p + 1], (64, rows)), jnp.broadcast_to(to_end[q : q + 1], (64, rows))], axis=0
        )
        high, low = split(values.astype(f32).T * ends, 2)
        state = jnp.dot(high, writes, preferred_element_type=f32) + jnp.dot(low, writes, preferred_element_type=f32)
        both = jnp.concatenate([part[16 * b : 16 * b + 16] for part in mixing], axis=0)
        met = jnp.dot(both, values, preferred_element_type=f32)
        met = met[:16] + met[16:32] + met[32:]
        local = jnp.where(left, met[:8], met[8:])
        gate = jnp.dot(pick, gate_ref[:, span], preferred_element_type=f32)
        local_power, gate_power, state_power = exponent(local, 0), exponent(gate, 0), exponent(state, 1)
        others = jnp.where(line == 2, local_power, jnp.where(line == 3, gate_power, 0.0))
        others = jnp.where(line == 1, jnp.where(left, end_low[p : p + 1], end_low[q : q + 1]), others)
        others = jnp.where(line == 0, jnp.where(left, end_high[p : p + 1], end_high[q : q + 1]), others)
        side = jnp.concatenate(
            [
                coded(local, local_power),
                coded(gate, gate_power),
                jnp.where(left, log_high[p], log_high[q]),
                jnp.where(left, log_low[p], log_low[q]),
                others,
                powers,
                empty,
            ],
            axis=0,
        ).T
        side = jnp.where(wide == 36, state_power, jnp.where(wide < 64, side, folded))
        for at, part in ((0, coded(state, state_power)), (16, side)):
            part = part.astype(jnp.int32).reshape(8, 16, 128)
            out_ref[8 * b : 8 * b + 8, at : at + 16, :] = part.astype(jnp.int16)


def local_part(place, stream, states, tail, gate, step, resets, by_head, taps, state_taps):
    channels = stream.shape[1]
    return pl.pallas_call(
        local_kernel,
        out_shape=jax.ShapeDtypeStruct((channels // 16, 32, 128), jnp.int16),
        in_specs=[whole] * 10,
        out_specs=whole,
        scratch_shapes=[pltpu.VMEM((tail.shape[0] + stream.shape[0], 128), f32)],
        compiler_params=pltpu.CompilerParams(vmem_limit_bytes=58 * 2**20),
        cost_estimate=pl.CostEstimate(flops=1 << 27, bytes_accessed=2 << 20, transcendentals=1 << 18),
    )(place, stream, states, tail, gate, step, resets, by_head, taps, state_taps)


def carry_kernel(came_ref, out_ref, side_ref, met_ref, weight_ref, *, planes, subs):
    chunks, _, states = came_ref.shape
    part = 16
    count = 8
    group = planes * count
    total = chunks * count
    side = came_ref[:, part:, :].astype(jnp.int32).astype(f32)
    side_ref[...] = side.reshape(chunks * part, 128)
    scale = jnp.exp2(side - 15.0)
    state = came_ref[:, :part, :].astype(jnp.int32).astype(f32) * scale[:, :, 36:37]
    state_high, state_low = split(state.reshape(chunks * part, states), 2)
    wide = lax.broadcasted_iota(jnp.int32, (chunks, 8, 128), 2)
    reads = jnp.where(wide < 64, pltpu.roll(side[:, :8], 64, 2), side[:, 8:])
    order = [z * subs + k for k in range(subs) for z in range(planes)]
    reads = jnp.concatenate([reads[c] for c in order], axis=0)
    reads_high, reads_low = split(reads, 2)
    contract = (((1,), (1,)), ((), ()))
    met_ref[...] = (
        lax.dot_general(state_high, reads_high, contract, preferred_element_type=f32)
        + lax.dot_general(state_high, reads_low, contract, preferred_element_type=f32)
        + lax.dot_general(state_low, reads_high, contract, preferred_element_type=f32)
    )

    lane = lax.broadcasted_iota(jnp.int32, (8, 128), 1)

    def by_lane(block_of, offset):
        columns = []
        for j in range(chunks // 16):
            column = None
            for i in range(16):
                block = block_of(order[16 * j + i])
                tall = block.shape[0]
                if (8 * i - offset) % 128:
                    block = pltpu.roll(block, (8 * i - offset) % 128, 1)
                place = lax.broadcasted_iota(jnp.int32, (tall, 128), 1)
                column = block if column is None else jnp.where(place >= 8 * i, block, column)
            columns.append(column)
        return jnp.concatenate(columns, axis=1)

    local = side * scale[:, :, 34:35]
    gate = side * scale[:, :, 35:36]
    local = by_lane(lambda c: local[c], 0)
    gate = by_lane(lambda c: gate[c], 8)
    log_high = by_lane(lambda c: side[c, :8], 16)[:1]
    log_low = by_lane(lambda c: side[c, :8], 24)[:1]
    power = by_lane(lambda c: side[c, :8], 40)[:1]
    rows_log = decoded_log(log_high, log_low)

    one = side_ref[pl.ds(0, chunks, stride=part), :]
    end_log = decoded_log(one[:, 32:33], one[:, 33:34])
    chunk = lax.broadcasted_iota(jnp.int32, (chunks, total), 0)
    at = lax.broadcasted_iota(jnp.int32, (chunks, total), 1)
    before = chunk < ((at // count) % planes) * subs + at // group
    upper = lax.broadcasted_iota(jnp.int32, (chunks, chunks), 0) < lax.broadcasted_iota(jnp.int32, (chunks, chunks), 1)
    upper = upper.astype(bf16)
    between = jnp.zeros((chunks, total), f32)
    for piece in split(jnp.where(before, end_log, 0.0), 3):
        between = between + jnp.dot(upper, piece, preferred_element_type=f32)
    weight_ref[...] = jnp.where(before, jnp.exp(between + rows_log), 0.0) * jnp.exp2(power - 15.0)

    across = jnp.zeros((part, total), f32)
    for c in range(chunks):
        across = across + weight_ref[c : c + 1, :] * met_ref[part * c : part * c + part, :]
    gated = (across + local) * (gate * jax.nn.sigmoid(gate))
    for k in range(subs):
        columns = slice(k // 2 * 128, k // 2 * 128 + 128)
        first, second = gated[:8, columns], gated[8:, columns]
        if k % 2:
            first = pltpu.roll(first, 64, 1)
        else:
            second = pltpu.roll(second, 64, 1)
        tile = jnp.where(lane < 64, first, second)
        for z in range(planes):
            out_ref[z * subs + k] = tile


def carry(came, planes, subs):
    chunks = came.shape[0]
    return pl.pallas_call(
        functools.partial(carry_kernel, planes=planes, subs=subs),
        out_shape=jax.ShapeDtypeStruct((chunks, 8, 128), f32),
        in_specs=[whole],
        out_specs=whole,
        scratch_shapes=[
            pltpu.VMEM((chunks * 16, 128), f32),
            pltpu.VMEM((chunks * 16, chunks * 8), f32),
            pltpu.VMEM((chunks, chunks * 8), f32),
        ],
        compiler_params=pltpu.CompilerParams(vmem_limit_bytes=24 * 2**20),
        cost_estimate=pl.CostEstimate(flops=1 << 28, bytes_accessed=1 << 20, transcendentals=1 << 16),
    )(came)


def project_kernel(place_ref, gated_ref, gain_ref, *refs):
    weights, out_ref = refs[:-1], refs[-1]
    gated = gated_ref[...]
    depth, lanes = gated.shape
    half = lanes // 2
    squares = jnp.broadcast_to(jnp.sum(gated * gated, axis=0, keepdims=True), (8, lanes))
    squares = squares + pltpu.roll(squares, half, 1)
    normed = gated * lax.rsqrt(squares[:1] / (2 * depth) + epsilon)
    pair = [a.reshape(depth // 8, 1, 8, lanes) for a in (normed, pltpu.roll(normed, half, 1))]
    normed = jnp.concatenate(pair, axis=1).reshape(2 * depth, lanes).T[:half]
    normed = (normed * gain_ref[...]).astype(bf16)
    for k, weight_ref in enumerate(weights):
        width = weight_ref.shape[0]
        columns = pl.ds(pl.multiple_of(place_ref[k] * width, width), width)
        out_ref[:, columns] = lax.dot_general(
            normed, weight_ref[...], (((1,), (1,)), ((), ())), preferred_element_type=f32
        )


def project(place, gated, gain, weights):
    columns = sum(weight.shape[0] for weight in weights)
    return pl.pallas_call(
        project_kernel,
        out_shape=jax.ShapeDtypeStruct((gated.shape[1] // 2, columns), f32),
        in_specs=[pl.BlockSpec(memory_space=pltpu.SMEM)] + [whole] * (2 + len(weights)),
        out_specs=whole,
        compiler_params=pltpu.CompilerParams(vmem_limit_bytes=8 * 2**20),
        cost_estimate=pl.CostEstimate(flops=2 * 64 * 1024 * 512, bytes_accessed=1 << 21, transcendentals=0),
    )(place, gated, gain, *weights)


def logits_kernel(start_ref, chosen_ref, gain_ref, target_ref, *refs, steps):
    weights, (out_ref, total_ref, inverse_ref) = refs[:-3], refs[-3:]
    step = pl.program_id(0)
    slabs, group, width = chosen_ref.shape
    columns = weights[0].shape[1]

    @pl.when(step == 0)
    def _():
        squares = jnp.zeros((group, 1), f32)
        for k in range(slabs):
            slab = chosen_ref[k].astype(f32)
            squares = squares + jnp.sum(slab * slab, axis=1, keepdims=True)
        inverse_ref[...] = jnp.broadcast_to(lax.rsqrt(squares / (slabs * width) + epsilon), inverse_ref.shape)
        total_ref[...] = jnp.zeros_like(total_ref)

    features = chosen_ref[step].astype(f32) * inverse_ref[:, :1] * gain_ref[pl.ds(step, 1), :]
    weight = jnp.concatenate([weight_ref[...] for weight_ref in weights], axis=1)
    total_ref[...] += jnp.dot(features.astype(bf16), weight, preferred_element_type=f32)

    @pl.when(step == steps - 1)
    def _():
        logits = total_ref[...]
        top = jnp.max(logits, axis=1, keepdims=True)
        summed = jnp.sum(jnp.exp(logits - top), axis=1, keepdims=True)
        picked = jnp.zeros((group, 1), f32)
        lane = lax.broadcasted_iota(jnp.int32, (group, columns), 1)
        for k in range(len(weights)):
            own = lane + start_ref[k] == target_ref[...]
            picked = picked + jnp.sum(
                jnp.where(own, logits[:, k * columns : (k + 1) * columns], 0.0), axis=1, keepdims=True
            )
        place = lax.broadcasted_iota(jnp.int32, (group, 128), 1)
        found = jnp.where(place == 0, top, jnp.where(place == 1, summed, picked)).T
        pair = jnp.concatenate([found[0:1], found[1:2], found[2:3], found[2:3]], axis=1)
        out_ref[...] = pair


def score(starts, chosen, gain, target, weights):
    slabs, group, width = chosen.shape
    columns = weights[0].shape[1]
    fixed = lambda *shape: pl.BlockSpec(shape, lambda k: (0,) * len(shape))
    return pl.pallas_call(
        functools.partial(logits_kernel, steps=slabs),
        grid=(slabs,),
        out_shape=jax.ShapeDtypeStruct((1, 4 * group), f32),
        in_specs=[
            pl.BlockSpec(memory_space=pltpu.SMEM),
            fixed(slabs, group, width),
            fixed(slabs, width),
            fixed(group, 1),
            *[pl.BlockSpec((width, columns), lambda k: (k, 0)) for _ in weights],
        ],
        out_specs=fixed(1, 4 * group),
        scratch_shapes=[pltpu.VMEM((group, len(weights) * columns), f32), pltpu.VMEM((group, 128), f32)],
        compiler_params=pltpu.CompilerParams(
            dimension_semantics=("arbitrary",), vmem_limit_bytes=24 * 2**20
        ),
        cost_estimate=pl.CostEstimate(flops=2 * 64 * 4096 * 1024, bytes_accessed=9 << 20, transcendentals=0),
    )(starts, chosen, gain, target, *weights)


def shifted(shard, axis, by):
    size = lax.axis_size(axis)
    return lax.ppermute(shard, axis, [(i, (i + by) % size) for i in range(size)])


together = lambda *arrays: lax.optimization_barrier(arrays)


def body(
    inner_input,
    gate_input,
    state_inputs,
    step_size,
    resets,
    decay_rate,
    skip_gain,
    conv_inner,
    conv_state,
    norm_gain,
    out_weight,
    residual,
    final_gain,
    head_weight,
    scored,
    targets,
    policy_logprob,
):
    rows, channels = inner_input.shape
    chunks = lax.axis_size(CTX)
    part = channels // chunks
    planes, subs = lax.axis_size("z"), lax.axis_size(SUB)
    count = scored.shape[0]
    group = planes * count
    total = chunks * count
    local_rows = scored - lax.axis_index(CTX) * rows

    margin = 16
    flags = jnp.broadcast_to(resets[rows - margin :, None].astype(bf16), (margin, 128))
    tail = [inner_input[rows - margin :], state_inputs[0, rows - margin :], state_inputs[1, rows - margin :], flags]
    tail = lax.ppermute(jnp.concatenate(tail, axis=1), CTX, [(i, i + 1) for i in range(chunks - 1)])

    pick = (jnp.arange(rows)[None, :] == local_rows[:, None]).astype(bf16)
    rows_residual = jnp.dot(pick, residual, preferred_element_type=f32).astype(bf16)
    own = lax.dynamic_index_in_dim(targets.reshape(planes, subs, count), lax.axis_index(SUB), 1, False).reshape(group, 1)

    by_head = jnp.stack([decay_rate, skip_gain], axis=1)
    message = local_part(
        local_rows.reshape(-1, 1), inner_input, state_inputs, tail, gate_input, step_size, resets.reshape(1, rows), by_head, conv_inner, conv_state
    )
    across = lax.axis_index("x")
    core = lax.axis_index("core")
    message, rows_residual, own_out = together(message, rows_residual, out_weight.T)
    heads = head_weight
    came = exchange(message, CTX)
    swap = [(i * planes + k, k * planes + i) for i in range(planes) for k in range(planes)]
    rows_residual = lax.ppermute(rows_residual, PLANE, swap)
    other_out = shifted(own_out, "core", 1)
    heads_left = shifted(heads, "x", 1)
    heads_right = shifted(heads, "x", -1)
    pair = jnp.concatenate([jnp.where(core == 0, own_out, other_out), jnp.where(core == 0, other_out, own_out)], axis=0)
    came, rows_residual, pair, heads_left, heads_right = together(came, rows_residual, pair, heads_left, heads_right)

    gated, pair = together(carry(came, planes, subs), pair)
    gated = exchange(gated, CTX).reshape(channels // 2, 2 * group)
    pairs = [pair, *(shifted(pair, "x", by) for by in (1, -1, 2))]
    heads_far = shifted(heads, "x", 2)
    gated, pairs, heads_far = together(gated, pairs, heads_far)

    width = lax.axis_size("x")
    places = [(across - by) % width for by in (0, 1, -1, 2)]
    partial = project(jnp.stack(places), gated, norm_gain.reshape(1, -1), pairs)
    partial, heads_left = together(partial, heads_left)
    partial = exchange(partial.reshape(planes, count, -1), "tp")
    others = [shifted(heads, "core", 1), shifted(heads_left, "core", 1)]
    partial, others = together(partial, others)
    chosen = (jnp.sum(partial, axis=0) + rows_residual.astype(f32)).astype(bf16)

    chosen, heads_right, heads_far = together(chosen, heads_right, heads_far)
    chosen = to_everyone(chosen, PLANE).reshape(planes, group, -1)
    others = [*others, shifted(heads_right, "core", 1), shifted(heads_far, "core", 1)]
    chosen, others = together(chosen, others)
    columns = head_weight.shape[1]
    starts = jnp.stack([lax.axis_index("z") * subs + x * 2 + c for c in (core, 1 - core) for x in places])
    starts = (starts * lax.axis_size("tp") + lax.axis_index("tp")) * columns
    weights = [heads, heads_left, heads_right, heads_far, *others]
    found = score(starts, chosen, final_gain.reshape(planes, -1), own, weights)

    found = to_everyone(found, PLANE).reshape(chunks, 4, group)
    top = jnp.max(found[:, 0], axis=0)
    summed = jnp.sum(found[:, 1] * jnp.exp(found[:, 0] - top[None, :]), axis=0)
    ref = jnp.sum(found[:, 2], axis=0) - top - jnp.log(summed)
    ref = to_everyone(ref.reshape(planes, count), SUB)
    ref_logprob = ref.swapaxes(0, 1).reshape(total)
    token_kl = 0.5 * jnp.square(ref_logprob - policy_logprob)
    return (ref_logprob, token_kl)


def solution(mesh):
    heads_split = mesh.shape["tp"]
    finer = Mesh(mesh.devices.reshape(heads_split, -1, 2, heads_split), ("z", "x", "core", "tp"))
    placed = (
        P(CTX, "tp"),
        P(CTX, "tp"),
        P(None, CTX, "tp"),
        P("tp", CTX),
        P(CTX),
        P("tp"),
        P("tp"),
        P(None, "tp"),
        P(None, None, "tp"),
        P("tp"),
        P("tp", CTX),
        P(CTX, "tp"),
        P(),
        P(None, (*CTX, "tp")),
        P(CTX),
        P(),
        P(),
    )
    return jax.shard_map(body, mesh=finer, in_specs=placed, out_specs=(P(), P()), check_vma=False)
```

```python
import functools

import jax
import jax.numpy as jnp
from jax import lax
from jax.experimental import pallas as pl
from jax.experimental.pallas import tpu as pltpu
from jax.sharding import Mesh
from jax.sharding import PartitionSpec as P

CTX = ("z", "x", "core")
SUB = ("x", "core")
PLANE = ("z", "tp")

epsilon = 1e-05
blocked = -1e9
precise = lax.Precision.HIGHEST
f32 = jnp.float32
bf16 = jnp.bfloat16


def exchange(blocks, axes):
    return lax.all_to_all(blocks, axes, 0, 0, tiled=True)


def to_everyone(shard, axes):
    return exchange(jnp.broadcast_to(shard[None], (lax.axis_size(axes), *shard.shape)), axes)


whole = pl.BlockSpec(memory_space=pltpu.VMEM)


def split(value, count):
    parts = []
    for _ in range(count):
        part = value.astype(bf16)
        parts.append(part)
        value = value - part.astype(f32)
    return parts


def exponent(value, axis):
    top = jnp.max(jnp.abs(value), axis=axis, keepdims=True)
    return jnp.floor(jnp.log2(jnp.maximum(top, 1e-30))) + 1.0


def coded(value, power):
    return jnp.clip(jnp.round(value * jnp.exp2(15.0 - power)), -32767.0, 32767.0)


def coded_log(value, free):
    high = jnp.round(value * 2048.0)
    low = jnp.round((value - high / 2048.0) * 2.0**26)
    return jnp.where(free, high, -32768.0), jnp.where(free, low, 0.0)


def decoded_log(high, low):
    return jnp.where(high < -32767.5, blocked, high / 2048.0 + low * 2.0**-26)


def tail_kernel(stream_ref, state_ref, reset_ref, out_ref):
    channels, states = stream_ref.shape[1], state_ref.shape[2]
    out_ref[:, :channels] = stream_ref[...]
    out_ref[:, channels : channels + states] = state_ref[0]
    out_ref[:, channels + states : channels + 2 * states] = state_ref[1]
    flags = jnp.broadcast_to(reset_ref[...].astype(f32), (out_ref.shape[0], reset_ref.shape[1]))
    out_ref[:, channels + 2 * states :] = flags.astype(bf16)


def last_rows(stream, states, resets, margin):
    rows, channels = stream.shape
    at = rows // margin - 1
    width = states.shape[2]
    return pl.pallas_call(
        tail_kernel,
        grid=(1,),
        out_shape=jax.ShapeDtypeStruct((margin, channels + 2 * width + rows), bf16),
        in_specs=[
            pl.BlockSpec((margin, channels), lambda k: (at, 0)),
            pl.BlockSpec((2, margin, width), lambda k: (0, at, 0)),
            pl.BlockSpec((1, rows), lambda k: (0, 0)),
        ],
        out_specs=pl.BlockSpec((margin, channels + 2 * width + rows), lambda k: (0, 0)),
        compiler_params=pltpu.CompilerParams(vmem_limit_bytes=58 * 2**20),
    )(stream, states, resets)


def local_kernel(
    base_ref,
    scored_ref,
    rate_ref,
    skip_ref,
    stream_ref,
    state_ref,
    tail_ref,
    gate_ref,
    step_ref,
    reset_ref,
    taps_ref,
    state_taps_ref,
    out_ref,
    pad_ref,
):
    rows, channels = stream_ref.shape
    states = state_ref.shape[2]
    heads = step_ref.shape[0]
    margin = tail_ref.shape[0]
    width = tail_ref.shape[1] - 128
    count = scored_ref.shape[0]
    lane = lax.broadcasted_iota(jnp.int32, (8, 128), 1)
    line = lax.broadcasted_iota(jnp.int32, (8, 128), 0)

    flag = jnp.broadcast_to(reset_ref[...].astype(f32), (8, rows))
    free = 1.0 - flag
    earlier = 1.0 - tail_ref[:, width:].astype(f32)[:8]
    second = free * pltpu.roll(jnp.where(lane == rows - 1, earlier, free), 1, 1)
    third = second * pltpu.roll(jnp.where(lane >= rows - 2, earlier, free), 2, 1)
    turned = jnp.where(line == 0, free, jnp.where(line == 1, second, third)).T
    keeping = [jnp.broadcast_to(turned[:, k : k + 1], (rows, 128)) for k in range(3)]

    def filtered(block, tail, taps):
        pad_ref[:margin] = tail.astype(f32)
        pad_ref[margin:] = block.astype(f32)
        summed = taps[0:1] * pad_ref[margin:]
        for k in range(1, 4):
            summed = summed + keeping[k - 1] * taps[k : k + 1] * pad_ref[margin - k : margin - k + rows]
        return (summed * jax.nn.sigmoid(summed)).astype(bf16)

    writes = filtered(state_ref[0], tail_ref[:, channels : channels + states], state_taps_ref[0])
    reads = filtered(state_ref[1], tail_ref[:, channels + states : width], state_taps_ref[1])

    place = jnp.zeros((8, 128), jnp.int32)
    for k in range(count):
        place = jnp.where(line == k, scored_ref[k] - base_ref[0], place)
    rate = jnp.zeros((heads, rows), f32)
    skip = jnp.zeros((heads, rows), f32)
    head = lax.broadcasted_iota(jnp.int32, (heads, rows), 0)
    for k in range(heads):
        rate = jnp.where(head == k, rate_ref[k], rate)
        skip = jnp.where(head == k, skip_ref[k], skip)
    chosen = lane == place
    pick = chosen.astype(bf16)
    rows_reads = jnp.dot(pick, reads, preferred_element_type=f32)
    first = lax.broadcasted_iota(jnp.int32, (rows, rows), 0)
    upto = (first <= lax.broadcasted_iota(jnp.int32, (rows, rows), 1)).astype(bf16)
    step = step_ref[...]
    drift = jnp.concatenate(split(-rate * step, 3), axis=0)
    summed = jnp.dot(drift, upto, preferred_element_type=f32)
    cumulated = summed[:heads] + summed[heads : 2 * heads] + summed[2 * heads :]
    segment = jnp.dot(flag.astype(bf16), upto, preferred_element_type=f32)
    rows_segment = jnp.sum(jnp.where(chosen, segment, 0.0), axis=1, keepdims=True)
    rows_log = jnp.sum(jnp.where(chosen[None], cumulated[:, None, :], 0.0), axis=2, keepdims=True)
    causal = (lane <= place) & (segment == rows_segment)
    scores = lax.dot_general(
        rows_reads.astype(bf16), writes, (((1,), (1,)), ((), ())), preferred_element_type=f32
    )
    gaps = jnp.where(causal[None], rows_log - cumulated[:, None, :], 0.0)
    mixing = jnp.where(causal[None], jnp.exp(gaps), 0.0) * scores[None] * step[:, None, :]
    mixing = mixing + jnp.where(chosen[None], skip[:, None, :], 0.0)
    mixing = split(mixing.reshape(heads * count, rows), 3)

    end_segment = segment[0:1, rows - 1 :]
    end_log = cumulated[:, rows - 1 :]
    to_end = jnp.where(segment[0:1] == end_segment, jnp.exp(end_log - cumulated) * step, 0.0)
    end_high, end_low = coded_log(end_log, jnp.broadcast_to(end_segment == 0.0, end_log.shape))
    log_high, log_low = coded_log(rows_log, jnp.broadcast_to((rows_segment == 0.0)[None], rows_log.shape))

    power = exponent(rows_reads, 1)
    rows_reads = coded(rows_reads, power)
    folded = jnp.concatenate([pltpu.roll(rows_reads, 64, 1), rows_reads], axis=0)
    folded = jnp.broadcast_to(folded[None], (8, 16, 128)).reshape(128, 128)
    powers = jnp.broadcast_to(power, (8, 128))
    left = lane < 64
    wide = lax.broadcasted_iota(jnp.int32, (128, 128), 1)
    empty = jnp.zeros((80, 128), f32)
    for b in range(channels // 128):
        span = slice(b * 128, (b + 1) * 128)
        p, q = 2 * b, 2 * b + 1
        values = filtered(stream_ref[:, span], tail_ref[:, span], taps_ref[:, span])
        ends = jnp.concatenate(
            [jnp.broadcast_to(to_end[p : p + 1], (64, rows)), jnp.broadcast_to(to_end[q : q + 1], (64, rows))], axis=0
        )
        high, low = split(values.astype(f32).T * ends, 2)
        state = jnp.dot(high, writes, preferred_element_type=f32) + jnp.dot(low, writes, preferred_element_type=f32)
        both = jnp.concatenate([part[16 * b : 16 * b + 16] for part in mixing], axis=0)
        met = jnp.dot(both, values, preferred_element_type=f32)
        met = met[:16] + met[16:32] + met[32:]
        local = jnp.where(left, met[:8], met[8:])
        gate = jnp.dot(pick, gate_ref[:, span], preferred_element_type=f32)
        local_power, gate_power, state_power = exponent(local, 0), exponent(gate, 0), exponent(state, 1)
        others = jnp.where(line == 2, local_power, jnp.where(line == 3, gate_power, 0.0))
        others = jnp.where(line == 1, jnp.where(left, end_low[p : p + 1], end_low[q : q + 1]), others)
        others = jnp.where(line == 0, jnp.where(left, end_high[p : p + 1], end_high[q : q + 1]), others)
        side = jnp.concatenate(
            [
                coded(local, local_power),
                coded(gate, gate_power),
                jnp.where(left, log_high[p], log_high[q]),
                jnp.where(left, log_low[p], log_low[q]),
                others,
                powers,
                empty,
            ],
            axis=0,
        ).T
        side = jnp.where(wide == 36, state_power, jnp.where(wide < 64, side, folded))
        for at, part in ((0, coded(state, state_power)), (16, side)):
            part = part.astype(jnp.int32).reshape(8, 16, 128)
            out_ref[8 * b : 8 * b + 8, at : at + 16, :] = part.astype(jnp.int16)


def local_part(base, scored, rate, skip, stream, states, tail, gate, step, resets, taps, state_taps):
    channels = stream.shape[1]
    return pl.pallas_call(
        local_kernel,
        out_shape=jax.ShapeDtypeStruct((channels // 16, 32, 128), jnp.int16),
        in_specs=[pl.BlockSpec(memory_space=pltpu.SMEM)] * 4 + [whole] * 8,
        out_specs=whole,
        scratch_shapes=[pltpu.VMEM((tail.shape[0] + stream.shape[0], 128), f32)],
        compiler_params=pltpu.CompilerParams(vmem_limit_bytes=58 * 2**20),
        cost_estimate=pl.CostEstimate(flops=1 << 27, bytes_accessed=2 << 20, transcendentals=1 << 18),
    )(base, scored, rate, skip, stream, states, tail, gate, step, resets, taps, state_taps)


def carry_kernel(came_ref, out_ref, side_ref, met_ref, weight_ref, *, planes, subs):
    chunks, _, states = came_ref.shape
    part = 16
    count = 8
    group = planes * count
    total = chunks * count
    side = came_ref[:, part:, :].astype(jnp.int32).astype(f32)
    side_ref[...] = side.reshape(chunks * part, 128)
    scale = jnp.exp2(side - 15.0)
    state = came_ref[:, :part, :].astype(jnp.int32).astype(f32) * scale[:, :, 36:37]
    state_high, state_low = split(state.reshape(chunks * part, states), 2)
    wide = lax.broadcasted_iota(jnp.int32, (chunks, 8, 128), 2)
    reads = jnp.where(wide < 64, pltpu.roll(side[:, :8], 64, 2), side[:, 8:])
    order = [z * subs + k for k in range(subs) for z in range(planes)]
    reads = jnp.concatenate([reads[c] for c in order], axis=0)
    reads_high, reads_low = split(reads, 2)
    contract = (((1,), (1,)), ((), ()))
    met_ref[...] = (
        lax.dot_general(state_high, reads_high, contract, preferred_element_type=f32)
        + lax.dot_general(state_high, reads_low, contract, preferred_element_type=f32)
        + lax.dot_general(state_low, reads_high, contract, preferred_element_type=f32)
    )

    lane = lax.broadcasted_iota(jnp.int32, (8, 128), 1)

    def by_lane(block_of, offset):
        columns = []
        for j in range(chunks // 16):
            column = None
            for i in range(16):
                block = block_of(order[16 * j + i])
                tall = block.shape[0]
                if (8 * i - offset) % 128:
                    block = pltpu.roll(block, (8 * i - offset) % 128, 1)
                place = lax.broadcasted_iota(jnp.int32, (tall, 128), 1)
                column = block if column is None else jnp.where(place >= 8 * i, block, column)
            columns.append(column)
        return jnp.concatenate(columns, axis=1)

    local = side * scale[:, :, 34:35]
    gate = side * scale[:, :, 35:36]
    local = by_lane(lambda c: local[c], 0)
    gate = by_lane(lambda c: gate[c], 8)
    log_high = by_lane(lambda c: side[c, :8], 16)[:1]
    log_low = by_lane(lambda c: side[c, :8], 24)[:1]
    power = by_lane(lambda c: side[c, :8], 40)[:1]
    rows_log = decoded_log(log_high, log_low)

    one = side_ref[pl.ds(0, chunks, stride=part), :]
    end_log = decoded_log(one[:, 32:33], one[:, 33:34])
    chunk = lax.broadcasted_iota(jnp.int32, (chunks, total), 0)
    at = lax.broadcasted_iota(jnp.int32, (chunks, total), 1)
    before = chunk < ((at // count) % planes) * subs + at // group
    upper = lax.broadcasted_iota(jnp.int32, (chunks, chunks), 0) < lax.broadcasted_iota(jnp.int32, (chunks, chunks), 1)
    upper = upper.astype(bf16)
    between = jnp.zeros((chunks, total), f32)
    for piece in split(jnp.where(before, end_log, 0.0), 3):
        between = between + jnp.dot(upper, piece, preferred_element_type=f32)
    weight_ref[...] = jnp.where(before, jnp.exp(between + rows_log), 0.0) * jnp.exp2(power - 15.0)

    across = jnp.zeros((part, total), f32)
    for c in range(chunks):
        across = across + weight_ref[c : c + 1, :] * met_ref[part * c : part * c + part, :]
    gated = (across + local) * (gate * jax.nn.sigmoid(gate))
    for k in range(subs):
        columns = slice(k // 2 * 128, k // 2 * 128 + 128)
        first, second = gated[:8, columns], gated[8:, columns]
        if k % 2:
            first = pltpu.roll(first, 64, 1)
        else:
            second = pltpu.roll(second, 64, 1)
        tile = jnp.where(lane < 64, first, second)
        for z in range(planes):
            out_ref[z * subs + k] = tile


def carry(came, planes, subs):
    chunks = came.shape[0]
    return pl.pallas_call(
        functools.partial(carry_kernel, planes=planes, subs=subs),
        out_shape=jax.ShapeDtypeStruct((chunks, 8, 128), f32),
        in_specs=[whole],
        out_specs=whole,
        scratch_shapes=[
            pltpu.VMEM((chunks * 16, 128), f32),
            pltpu.VMEM((chunks * 16, chunks * 8), f32),
            pltpu.VMEM((chunks, chunks * 8), f32),
        ],
        compiler_params=pltpu.CompilerParams(vmem_limit_bytes=24 * 2**20),
        cost_estimate=pl.CostEstimate(flops=1 << 28, bytes_accessed=1 << 20, transcendentals=1 << 16),
    )(came)


def project_kernel(gated_ref, gain_ref, weight_ref, out_ref):
    gated = gated_ref[...]
    depth, lanes = gated.shape
    half = lanes // 2
    squares = jnp.broadcast_to(jnp.sum(gated * gated, axis=0, keepdims=True), (8, lanes))
    squares = squares + pltpu.roll(squares, half, 1)
    normed = gated * lax.rsqrt(squares[:1] / (2 * depth) + epsilon)
    pair = [a.reshape(depth // 8, 1, 8, lanes) for a in (normed, pltpu.roll(normed, half, 1))]
    normed = jnp.concatenate(pair, axis=1).reshape(2 * depth, lanes).T[:half]
    normed = (normed * gain_ref[...]).astype(bf16)
    out_ref[...] = lax.dot_general(
        normed, weight_ref[...], (((1,), (1,)), ((), ())), preferred_element_type=f32
    )


def project(gated, gain, weight):
    return pl.pallas_call(
        project_kernel,
        out_shape=jax.ShapeDtypeStruct((gated.shape[1] // 2, weight.shape[0]), f32),
        in_specs=[whole] * 3,
        out_specs=whole,
        compiler_params=pltpu.CompilerParams(vmem_limit_bytes=8 * 2**20),
        cost_estimate=pl.CostEstimate(flops=2 * 64 * 1024 * 512, bytes_accessed=1 << 21, transcendentals=0),
    )(gated, gain, weight)


def spread_kernel(partial_ref, residual_ref, out_ref):
    total = residual_ref[...].astype(f32)
    summed = partial_ref[0]
    for k in range(1, partial_ref.shape[0]):
        summed = summed + partial_ref[k]
    out_ref[...] = jnp.broadcast_to((summed + total).astype(bf16)[None], out_ref.shape)


def spread(partial, residual, copies):
    return pl.pallas_call(
        spread_kernel,
        out_shape=jax.ShapeDtypeStruct((copies, *residual.shape), bf16),
        in_specs=[whole] * 2,
        out_specs=whole,
        compiler_params=pltpu.CompilerParams(vmem_limit_bytes=8 * 2**20),
        cost_estimate=pl.CostEstimate(flops=1 << 16, bytes_accessed=1 << 20, transcendentals=0),
    )(partial, residual)


def logits_kernel(start_ref, chosen_ref, gain_ref, target_ref, from_ref, out_ref, weight_ref, sems, *, stride):
    slabs, group, width = chosen_ref.shape
    subs, _, columns = weight_ref.shape
    fetches = []
    for k in range(slabs):
        block = (slice(None), slice(k * width, (k + 1) * width), slice(None))
        fetches.append(pltpu.make_async_copy(from_ref.at[block], weight_ref.at[block], sems.at[k]))
        fetches[k].start()
    squares = jnp.zeros((group, 1), f32)
    for k in range(slabs):
        slab = chosen_ref[k].astype(f32)
        squares = squares + jnp.sum(slab * slab, axis=1, keepdims=True)
    inverse = lax.rsqrt(squares / (slabs * width) + epsilon)
    logits = jnp.zeros((group, subs * columns), f32)
    for k in range(slabs):
        features = chosen_ref[k].astype(f32) * inverse * gain_ref[k : k + 1, :]
        fetches[k].wait()
        weight = jnp.concatenate([weight_ref[j, k * width : (k + 1) * width, :] for j in range(subs)], axis=1)
        logits = logits + jnp.dot(features.astype(bf16), weight, preferred_element_type=f32)
    top = jnp.max(logits, axis=1, keepdims=True)
    summed = jnp.sum(jnp.exp(logits - top), axis=1, keepdims=True)
    picked = jnp.zeros((group, 1), f32)
    lane = lax.broadcasted_iota(jnp.int32, (group, columns), 1)
    for k in range(subs):
        own = lane + (start_ref[0] + k * stride) == target_ref[...]
        picked = picked + jnp.sum(
            jnp.where(own, logits[:, k * columns : (k + 1) * columns], 0.0), axis=1, keepdims=True
        )
    place = lax.broadcasted_iota(jnp.int32, (group, 128), 1)
    found = jnp.where(place == 0, top, jnp.where(place == 1, summed, picked)).T
    out_ref[...] = jnp.concatenate([found[0:1], found[1:2], found[2:3], found[2:3]], axis=1)


def score(start, chosen, gain, target, weight, stride):
    slabs, group, width = chosen.shape
    return pl.pallas_call(
        functools.partial(logits_kernel, stride=stride),
        out_shape=jax.ShapeDtypeStruct((1, 4 * group), f32),
        in_specs=[pl.BlockSpec(memory_space=pltpu.SMEM), whole, whole, whole, pl.BlockSpec(memory_space=pl.ANY)],
        out_specs=whole,
        scratch_shapes=[pltpu.VMEM(weight.shape, bf16), pltpu.SemaphoreType.DMA((slabs,))],
        compiler_params=pltpu.CompilerParams(vmem_limit_bytes=54 * 2**20),
        cost_estimate=pl.CostEstimate(flops=2 * 64 * 4096 * 1024, bytes_accessed=9 << 20, transcendentals=0),
    )(start, chosen, gain, target, weight)


def body(
    inner_input,
    gate_input,
    state_inputs,
    step_size,
    resets,
    decay_rate,
    skip_gain,
    conv_inner,
    conv_state,
    norm_gain,
    out_weight,
    residual,
    final_gain,
    head_weight,
    scored,
    targets,
    policy_logprob,
):
    rows, channels = inner_input.shape
    chunks = lax.axis_size(CTX)
    part = channels // chunks
    planes, subs = lax.axis_size("z"), lax.axis_size(SUB)
    count = scored.shape[0]
    group = planes * count
    total = chunks * count
    local_rows = scored - lax.axis_index(CTX) * rows

    flags = resets.reshape(1, rows)
    tail = last_rows(inner_input, state_inputs, flags, 16)
    tail = lax.ppermute(tail, CTX, [(i, i + 1) for i in range(chunks - 1)])

    out_full = lax.all_gather(out_weight.T, SUB, axis=0, tiled=True)
    head_full = lax.all_gather(head_weight, SUB, axis=0)
    pick = (jnp.arange(rows)[None, :] == local_rows[:, None]).astype(bf16)
    rows_residual = jnp.dot(pick, residual, preferred_element_type=f32).astype(bf16)
    own = lax.dynamic_index_in_dim(targets.reshape(planes, subs, count), lax.axis_index(SUB), 1, False).reshape(group, 1)

    base = (lax.axis_index(CTX) * rows).reshape(1)
    message = local_part(
        base, scored, decay_rate, skip_gain, inner_input, state_inputs, tail, gate_input, step_size, flags, conv_inner, conv_state
    )
    message, rows_residual = lax.optimization_barrier((message, rows_residual))
    came = exchange(message, CTX)
    swap = [(i * planes + k, k * planes + i) for i in range(planes) for k in range(planes)]
    rows_residual = lax.ppermute(rows_residual, PLANE, swap)
    came, rows_residual = lax.optimization_barrier((came, rows_residual))

    gated, out_full = lax.optimization_barrier((carry(came, planes, subs), out_full))
    gated = exchange(gated, CTX).reshape(channels // 2, 2 * group)

    partial = exchange(project(gated, norm_gain.reshape(1, -1), out_full).reshape(planes, count, -1), "tp")
    chosen = exchange(spread(partial, rows_residual, chunks), PLANE).reshape(planes, group, -1)
    columns = head_weight.shape[1]
    ways = lax.axis_size("tp")
    start = (lax.axis_index("z") * subs * ways + lax.axis_index("tp")) * columns
    found = score(start.reshape(1), chosen, final_gain.reshape(planes, -1), own, head_full, ways * columns)

    found = to_everyone(found, PLANE).reshape(chunks, 4, group)
    top = jnp.max(found[:, 0], axis=0)
    summed = jnp.sum(found[:, 1] * jnp.exp(found[:, 0] - top[None, :]), axis=0)
    ref = jnp.sum(found[:, 2], axis=0) - top - jnp.log(summed)
    ref = to_everyone(ref.reshape(planes, count), SUB)
    ref_logprob = ref.swapaxes(0, 1).reshape(total)
    token_kl = 0.5 * jnp.square(ref_logprob - policy_logprob)
    return (ref_logprob, token_kl)


def solution(mesh):
    heads_split = mesh.shape["tp"]
    finer = Mesh(mesh.devices.reshape(heads_split, -1, 2, heads_split), ("z", "x", "core", "tp"))
    placed = (
        P(CTX, "tp"),
        P(CTX, "tp"),
        P(None, CTX, "tp"),
        P("tp", CTX),
        P(CTX),
        P("tp"),
        P("tp"),
        P(None, "tp"),
        P(None, None, "tp"),
        P("tp"),
        P("tp", CTX),
        P(CTX, "tp"),
        P(),
        P(None, (*CTX, "tp")),
        P(CTX),
        P(),
        P(),
    )
    return jax.shard_map(body, mesh=finer, in_specs=placed, out_specs=(P(), P()), check_vma=False)
```

```python
import functools

import jax
import jax.numpy as jnp
from jax import lax
from jax.experimental import pallas as pl
from jax.experimental.pallas import tpu as pltpu
from jax.sharding import Mesh
from jax.sharding import PartitionSpec as P

CTX = ("z", "x", "core")
SUB = ("x", "core")
PLANE = ("z", "tp")

epsilon = 1e-05
blocked = -1e9
precise = lax.Precision.HIGHEST
f32 = jnp.float32
bf16 = jnp.bfloat16


def exchange(blocks, axes):
    return lax.all_to_all(blocks, axes, 0, 0, tiled=True)


def to_everyone(shard, axes):
    return exchange(jnp.broadcast_to(shard[None], (lax.axis_size(axes), *shard.shape)), axes)


whole = pl.BlockSpec(memory_space=pltpu.VMEM)


def split(value, count):
    parts = []
    for _ in range(count):
        part = value.astype(bf16)
        parts.append(part)
        value = value - part.astype(f32)
    return parts


def exponent(value, axis):
    top = jnp.max(jnp.abs(value), axis=axis, keepdims=True)
    return jnp.floor(jnp.log2(jnp.maximum(top, 1e-30))) + 1.0


def coded(value, power):
    return jnp.clip(jnp.round(value * jnp.exp2(15.0 - power)), -32767.0, 32767.0)


def coded_log(value, free):
    high = jnp.round(value * 2048.0)
    low = jnp.round((value - high / 2048.0) * 2.0**26)
    return jnp.where(free, high, -32768.0), jnp.where(free, low, 0.0)


def decoded_log(high, low):
    return jnp.where(high < -32767.5, blocked, high / 2048.0 + low * 2.0**-26)


def tail_kernel(stream_ref, state_ref, reset_ref, out_ref):
    channels, states = stream_ref.shape[1], state_ref.shape[2]
    out_ref[:, :channels] = stream_ref[...]
    out_ref[:, channels : channels + states] = state_ref[0]
    out_ref[:, channels + states : channels + 2 * states] = state_ref[1]
    flags = jnp.broadcast_to(reset_ref[...].astype(f32), (out_ref.shape[0], reset_ref.shape[1]))
    out_ref[:, channels + 2 * states :] = flags.astype(bf16)


def last_rows(stream, states, resets, margin):
    rows, channels = stream.shape
    at = rows // margin - 1
    width = states.shape[2]
    return pl.pallas_call(
        tail_kernel,
        grid=(1,),
        out_shape=jax.ShapeDtypeStruct((margin, channels + 2 * width + rows), bf16),
        in_specs=[
            pl.BlockSpec((margin, channels), lambda k: (at, 0)),
            pl.BlockSpec((2, margin, width), lambda k: (0, at, 0)),
            pl.BlockSpec((1, rows), lambda k: (0, 0)),
        ],
        out_specs=pl.BlockSpec((margin, channels + 2 * width + rows), lambda k: (0, 0)),
        compiler_params=pltpu.CompilerParams(vmem_limit_bytes=58 * 2**20),
    )(stream, states, resets)


def local_kernel(
    base_ref,
    scored_ref,
    rate_ref,
    skip_ref,
    stream_ref,
    state_ref,
    tail_ref,
    gate_ref,
    step_ref,
    reset_ref,
    taps_ref,
    state_taps_ref,
    out_ref,
    pad_ref,
):
    rows, channels = stream_ref.shape
    states = state_ref.shape[2]
    heads = step_ref.shape[0]
    margin = tail_ref.shape[0]
    width = tail_ref.shape[1] - 128
    count = scored_ref.shape[0]
    lane = lax.broadcasted_iota(jnp.int32, (8, 128), 1)
    line = lax.broadcasted_iota(jnp.int32, (8, 128), 0)

    flag = jnp.broadcast_to(reset_ref[...].astype(f32), (8, rows))
    free = 1.0 - flag
    earlier = 1.0 - tail_ref[:, width:].astype(f32)[:8]
    second = free * pltpu.roll(jnp.where(lane == rows - 1, earlier, free), 1, 1)
    third = second * pltpu.roll(jnp.where(lane >= rows - 2, earlier, free), 2, 1)
    turned = jnp.where(line == 0, free, jnp.where(line == 1, second, third)).T
    keeping = [jnp.broadcast_to(turned[:, k : k + 1], (rows, 128)) for k in range(3)]

    def filtered(block, tail, taps):
        pad_ref[:margin] = tail.astype(f32)
        pad_ref[margin:] = block.astype(f32)
        summed = taps[0:1] * pad_ref[margin:]
        for k in range(1, 4):
            summed = summed + keeping[k - 1] * taps[k : k + 1] * pad_ref[margin - k : margin - k + rows]
        return (summed * jax.nn.sigmoid(summed)).astype(bf16)

    writes = filtered(state_ref[0], tail_ref[:, channels : channels + states], state_taps_ref[0])
    reads = filtered(state_ref[1], tail_ref[:, channels + states : width], state_taps_ref[1])

    place = jnp.zeros((8, 128), jnp.int32)
    for k in range(count):
        place = jnp.where(line == k, scored_ref[k] - base_ref[0], place)
    rate = jnp.zeros((heads, rows), f32)
    skip = jnp.zeros((heads, rows), f32)
    head = lax.broadcasted_iota(jnp.int32, (heads, rows), 0)
    for k in range(heads):
        rate = jnp.where(head == k, rate_ref[k], rate)
        skip = jnp.where(head == k, skip_ref[k], skip)
    chosen = lane == place
    pick = chosen.astype(bf16)
    rows_reads = jnp.dot(pick, reads, preferred_element_type=f32)
    first = lax.broadcasted_iota(jnp.int32, (rows, rows), 0)
    upto = (first <= lax.broadcasted_iota(jnp.int32, (rows, rows), 1)).astype(bf16)
    step = step_ref[...]
    drift = jnp.concatenate(split(-rate * step, 3), axis=0)
    summed = jnp.dot(drift, upto, preferred_element_type=f32)
    cumulated = summed[:heads] + summed[heads : 2 * heads] + summed[2 * heads :]
    segment = jnp.dot(flag.astype(bf16), upto, preferred_element_type=f32)
    rows_segment = jnp.sum(jnp.where(chosen, segment, 0.0), axis=1, keepdims=True)
    rows_log = jnp.sum(jnp.where(chosen[None], cumulated[:, None, :], 0.0), axis=2, keepdims=True)
    causal = (lane <= place) & (segment == rows_segment)
    scores = lax.dot_general(
        rows_reads.astype(bf16), writes, (((1,), (1,)), ((), ())), preferred_element_type=f32
    )
    gaps = jnp.where(causal[None], rows_log - cumulated[:, None, :], 0.0)
    mixing = jnp.where(causal[None], jnp.exp(gaps), 0.0) * scores[None] * step[:, None, :]
    mixing = mixing + jnp.where(chosen[None], skip[:, None, :], 0.0)
    mixing = split(mixing.reshape(heads * count, rows), 3)

    end_segment = segment[0:1, rows - 1 :]
    end_log = cumulated[:, rows - 1 :]
    to_end = jnp.where(segment[0:1] == end_segment, jnp.exp(end_log - cumulated) * step, 0.0)
    end_high, end_low = coded_log(end_log, jnp.broadcast_to(end_segment == 0.0, end_log.shape))
    log_high, log_low = coded_log(rows_log, jnp.broadcast_to((rows_segment == 0.0)[None], rows_log.shape))

    power = exponent(rows_reads, 1)
    rows_reads = coded(rows_reads, power)
    folded = jnp.concatenate([pltpu.roll(rows_reads, 64, 1), rows_reads], axis=0)
    folded = jnp.broadcast_to(folded[None], (8, 16, 128)).reshape(128, 128)
    powers = jnp.broadcast_to(power, (8, 128))
    left = lane < 64
    wide = lax.broadcasted_iota(jnp.int32, (128, 128), 1)
    empty = jnp.zeros((80, 128), f32)
    for b in range(channels // 128):
        span = slice(b * 128, (b + 1) * 128)
        p, q = 2 * b, 2 * b + 1
        values = filtered(stream_ref[:, span], tail_ref[:, span], taps_ref[:, span])
        ends = jnp.concatenate(
            [jnp.broadcast_to(to_end[p : p + 1], (64, rows)), jnp.broadcast_to(to_end[q : q + 1], (64, rows))], axis=0
        )
        high, low = split(values.astype(f32).T * ends, 2)
        state = jnp.dot(high, writes, preferred_element_type=f32) + jnp.dot(low, writes, preferred_element_type=f32)
        both = jnp.concatenate([part[16 * b : 16 * b + 16] for part in mixing], axis=0)
        met = jnp.dot(both, values, preferred_element_type=f32)
        met = met[:16] + met[16:32] + met[32:]
        local = jnp.where(left, met[:8], met[8:])
        gate = jnp.dot(pick, gate_ref[:, span], preferred_element_type=f32)
        local_power, gate_power, state_power = exponent(local, 0), exponent(gate, 0), exponent(state, 1)
        others = jnp.where(line == 2, local_power, jnp.where(line == 3, gate_power, 0.0))
        others = jnp.where(line == 1, jnp.where(left, end_low[p : p + 1], end_low[q : q + 1]), others)
        others = jnp.where(line == 0, jnp.where(left, end_high[p : p + 1], end_high[q : q + 1]), others)
        side = jnp.concatenate(
            [
                coded(local, local_power),
                coded(gate, gate_power),
                jnp.where(left, log_high[p], log_high[q]),
                jnp.where(left, log_low[p], log_low[q]),
                others,
                powers,
                empty,
            ],
            axis=0,
        ).T
        side = jnp.where(wide == 36, state_power, jnp.where(wide < 64, side, folded))
        for at, part in ((0, coded(state, state_power)), (16, side)):
            part = part.astype(jnp.int32).reshape(8, 16, 128)
            out_ref[8 * b : 8 * b + 8, at : at + 16, :] = part.astype(jnp.int16)


def local_part(base, scored, rate, skip, stream, states, tail, gate, step, resets, taps, state_taps):
    channels = stream.shape[1]
    return pl.pallas_call(
        local_kernel,
        out_shape=jax.ShapeDtypeStruct((channels // 16, 32, 128), jnp.int16),
        in_specs=[pl.BlockSpec(memory_space=pltpu.SMEM)] * 4 + [whole] * 8,
        out_specs=whole,
        scratch_shapes=[pltpu.VMEM((tail.shape[0] + stream.shape[0], 128), f32)],
        compiler_params=pltpu.CompilerParams(vmem_limit_bytes=58 * 2**20),
        cost_estimate=pl.CostEstimate(flops=1 << 27, bytes_accessed=2 << 20, transcendentals=1 << 18),
    )(base, scored, rate, skip, stream, states, tail, gate, step, resets, taps, state_taps)


def carry_kernel(came_ref, out_ref, side_ref, met_ref, weight_ref, *, planes, subs):
    chunks, _, states = came_ref.shape
    part = 16
    count = 8
    group = planes * count
    total = chunks * count
    side = came_ref[:, part:, :].astype(jnp.int32).astype(f32)
    side_ref[...] = side.reshape(chunks * part, 128)
    scale = jnp.exp2(side - 15.0)
    state = came_ref[:, :part, :].astype(jnp.int32).astype(f32) * scale[:, :, 36:37]
    state_high, state_low = split(state.reshape(chunks * part, states), 2)
    wide = lax.broadcasted_iota(jnp.int32, (chunks, 8, 128), 2)
    reads = jnp.where(wide < 64, pltpu.roll(side[:, :8], 64, 2), side[:, 8:])
    order = [z * subs + k for k in range(subs) for z in range(planes)]
    reads = jnp.concatenate([reads[c] for c in order], axis=0)
    reads_high, reads_low = split(reads, 2)
    contract = (((1,), (1,)), ((), ()))
    met_ref[...] = (
        lax.dot_general(state_high, reads_high, contract, preferred_element_type=f32)
        + lax.dot_general(state_high, reads_low, contract, preferred_element_type=f32)
        + lax.dot_general(state_low, reads_high, contract, preferred_element_type=f32)
    )

    lane = lax.broadcasted_iota(jnp.int32, (8, 128), 1)

    def by_lane(block_of, offset):
        columns = []
        for j in range(chunks // 16):
            column = None
            for i in range(16):
                block = block_of(order[16 * j + i])
                tall = block.shape[0]
                if (8 * i - offset) % 128:
                    block = pltpu.roll(block, (8 * i - offset) % 128, 1)
                place = lax.broadcasted_iota(jnp.int32, (tall, 128), 1)
                column = block if column is None else jnp.where(place >= 8 * i, block, column)
            columns.append(column)
        return jnp.concatenate(columns, axis=1)

    local = side * scale[:, :, 34:35]
    gate = side * scale[:, :, 35:36]
    local = by_lane(lambda c: local[c], 0)
    gate = by_lane(lambda c: gate[c], 8)
    log_high = by_lane(lambda c: side[c, :8], 16)[:1]
    log_low = by_lane(lambda c: side[c, :8], 24)[:1]
    power = by_lane(lambda c: side[c, :8], 40)[:1]
    rows_log = decoded_log(log_high, log_low)

    one = side_ref[pl.ds(0, chunks, stride=part), :]
    end_log = decoded_log(one[:, 32:33], one[:, 33:34])
    chunk = lax.broadcasted_iota(jnp.int32, (chunks, total), 0)
    at = lax.broadcasted_iota(jnp.int32, (chunks, total), 1)
    before = chunk < ((at // count) % planes) * subs + at // group
    upper = lax.broadcasted_iota(jnp.int32, (chunks, chunks), 0) < lax.broadcasted_iota(jnp.int32, (chunks, chunks), 1)
    upper = upper.astype(bf16)
    between = jnp.zeros((chunks, total), f32)
    for piece in split(jnp.where(before, end_log, 0.0), 3):
        between = between + jnp.dot(upper, piece, preferred_element_type=f32)
    weight_ref[...] = jnp.where(before, jnp.exp(between + rows_log), 0.0) * jnp.exp2(power - 15.0)

    across = jnp.zeros((part, total), f32)
    for c in range(chunks):
        across = across + weight_ref[c : c + 1, :] * met_ref[part * c : part * c + part, :]
    gated = (across + local) * (gate * jax.nn.sigmoid(gate))
    for k in range(subs):
        columns = slice(k // 2 * 128, k // 2 * 128 + 128)
        first, second = gated[:8, columns], gated[8:, columns]
        if k % 2:
            first = pltpu.roll(first, 64, 1)
        else:
            second = pltpu.roll(second, 64, 1)
        tile = jnp.where(lane < 64, first, second)
        for z in range(planes):
            out_ref[z * subs + k] = tile


def carry(came, planes, subs):
    chunks = came.shape[0]
    return pl.pallas_call(
        functools.partial(carry_kernel, planes=planes, subs=subs),
        out_shape=jax.ShapeDtypeStruct((chunks, 8, 128), f32),
        in_specs=[whole],
        out_specs=whole,
        scratch_shapes=[
            pltpu.VMEM((chunks * 16, 128), f32),
            pltpu.VMEM((chunks * 16, chunks * 8), f32),
            pltpu.VMEM((chunks, chunks * 8), f32),
        ],
        compiler_params=pltpu.CompilerParams(vmem_limit_bytes=24 * 2**20),
        cost_estimate=pl.CostEstimate(flops=1 << 28, bytes_accessed=1 << 20, transcendentals=1 << 16),
    )(came)


def fetch_kernel(full_ref, gain_ref, after_ref, full_out_ref, gain_out_ref, sem):
    fetch = pltpu.make_async_copy(full_ref, full_out_ref, sem)
    fetch.start()
    gain_out_ref[...] = gain_ref[...]
    fetch.wait()


def fetched(full, gain, after):
    anywhere = pl.BlockSpec(memory_space=pl.ANY)
    return pl.pallas_call(
        fetch_kernel,
        out_shape=[pltpu.VMEM(full.shape, full.dtype), pltpu.VMEM(gain.shape, gain.dtype)],
        in_specs=[anywhere, whole, anywhere],
        out_specs=[whole] * 2,
        scratch_shapes=[pltpu.SemaphoreType.DMA],
        compiler_params=pltpu.CompilerParams(vmem_limit_bytes=4 * 2**20),
        cost_estimate=pl.CostEstimate(flops=0, bytes_accessed=2 << 20, transcendentals=0),
    )(full, gain, after)


def project_kernel(gated_ref, gain_ref, weight_ref, out_ref):
    gated = gated_ref[...]
    depth, lanes = gated.shape
    half = lanes // 2
    squares = jnp.broadcast_to(jnp.sum(gated * gated, axis=0, keepdims=True), (8, lanes))
    squares = squares + pltpu.roll(squares, half, 1)
    normed = gated * lax.rsqrt(squares[:1] / (2 * depth) + epsilon)
    pair = [a.reshape(depth // 8, 1, 8, lanes) for a in (normed, pltpu.roll(normed, half, 1))]
    normed = jnp.concatenate(pair, axis=1).reshape(2 * depth, lanes).T[:half]
    normed = (normed * gain_ref[...]).astype(bf16)
    out_ref[...] = lax.dot_general(
        normed, weight_ref[...], (((1,), (1,)), ((), ())), preferred_element_type=f32
    )


def project(gated, gain, weight):
    return pl.pallas_call(
        project_kernel,
        out_shape=jax.ShapeDtypeStruct((gated.shape[1] // 2, weight.shape[0]), f32),
        in_specs=[whole] * 3,
        out_specs=whole,
        compiler_params=pltpu.CompilerParams(vmem_limit_bytes=8 * 2**20),
        cost_estimate=pl.CostEstimate(flops=2 * 64 * 1024 * 512, bytes_accessed=1 << 21, transcendentals=0),
    )(gated, gain, weight)


def spread_kernel(partial_ref, residual_ref, out_ref):
    total = residual_ref[...].astype(f32)
    summed = partial_ref[0]
    for k in range(1, partial_ref.shape[0]):
        summed = summed + partial_ref[k]
    out_ref[...] = jnp.broadcast_to((summed + total).astype(bf16)[None], out_ref.shape)


def spread(partial, residual, copies):
    return pl.pallas_call(
        spread_kernel,
        out_shape=jax.ShapeDtypeStruct((copies, *residual.shape), bf16),
        in_specs=[whole] * 2,
        out_specs=whole,
        compiler_params=pltpu.CompilerParams(vmem_limit_bytes=8 * 2**20),
        cost_estimate=pl.CostEstimate(flops=1 << 16, bytes_accessed=1 << 20, transcendentals=0),
    )(partial, residual)


def logits_kernel(start_ref, chosen_ref, gain_ref, target_ref, from_ref, out_ref, weight_ref, sems, *, stride):
    slabs, group, width = chosen_ref.shape
    subs, _, columns = weight_ref.shape
    fetches = []
    for k in range(slabs):
        block = (slice(None), slice(k * width, (k + 1) * width), slice(None))
        fetches.append(pltpu.make_async_copy(from_ref.at[block], weight_ref.at[block], sems.at[k]))
        fetches[k].start()
    squares = jnp.zeros((group, 1), f32)
    for k in range(slabs):
        slab = chosen_ref[k].astype(f32)
        squares = squares + jnp.sum(slab * slab, axis=1, keepdims=True)
    inverse = lax.rsqrt(squares / (slabs * width) + epsilon)
    logits = jnp.zeros((group, subs * columns), f32)
    for k in range(slabs):
        features = chosen_ref[k].astype(f32) * inverse * gain_ref[k : k + 1, :]
        fetches[k].wait()
        weight = jnp.concatenate([weight_ref[j, k * width : (k + 1) * width, :] for j in range(subs)], axis=1)
        logits = logits + jnp.dot(features.astype(bf16), weight, preferred_element_type=f32)
    top = jnp.max(logits, axis=1, keepdims=True)
    summed = jnp.sum(jnp.exp(logits - top), axis=1, keepdims=True)
    picked = jnp.zeros((group, 1), f32)
    lane = lax.broadcasted_iota(jnp.int32, (group, columns), 1)
    for k in range(subs):
        own = lane + (start_ref[0] + k * stride) == target_ref[...]
        picked = picked + jnp.sum(
            jnp.where(own, logits[:, k * columns : (k + 1) * columns], 0.0), axis=1, keepdims=True
        )
    place = lax.broadcasted_iota(jnp.int32, (group, 128), 1)
    found = jnp.where(place == 0, top, jnp.where(place == 1, summed, picked)).T
    row = jnp.concatenate([found[0:1], found[1:2], found[2:3], found[2:3]], axis=1)
    for k in range(out_ref.shape[0]):
        out_ref[k] = row


def score(start, chosen, gain, target, weight, stride, copies):
    slabs, group, width = chosen.shape
    return pl.pallas_call(
        functools.partial(logits_kernel, stride=stride),
        out_shape=jax.ShapeDtypeStruct((copies, 1, 4 * group), f32),
        in_specs=[pl.BlockSpec(memory_space=pltpu.SMEM), whole, whole, whole, pl.BlockSpec(memory_space=pl.ANY)],
        out_specs=whole,
        scratch_shapes=[pltpu.VMEM(weight.shape, bf16), pltpu.SemaphoreType.DMA((slabs,))],
        compiler_params=pltpu.CompilerParams(vmem_limit_bytes=52 * 2**20),
        cost_estimate=pl.CostEstimate(flops=2 * 64 * 4096 * 1024, bytes_accessed=9 << 20, transcendentals=0),
    )(start, chosen, gain, target, weight)


def body(
    inner_input,
    gate_input,
    state_inputs,
    step_size,
    resets,
    decay_rate,
    skip_gain,
    conv_inner,
    conv_state,
    norm_gain,
    out_weight,
    residual,
    final_gain,
    head_weight,
    scored,
    targets,
    policy_logprob,
):
    rows, channels = inner_input.shape
    chunks = lax.axis_size(CTX)
    part = channels // chunks
    planes, subs = lax.axis_size("z"), lax.axis_size(SUB)
    count = scored.shape[0]
    group = planes * count
    total = chunks * count
    local_rows = scored - lax.axis_index(CTX) * rows

    flags = resets.reshape(1, rows)
    tail = last_rows(inner_input, state_inputs, flags, 16)
    tail = lax.ppermute(tail, CTX, [(i, i + 1) for i in range(chunks - 1)])

    out_full = lax.all_gather(out_weight.T, SUB, axis=0, tiled=True)
    head_full = lax.all_gather(head_weight, SUB, axis=0)
    pick = (jnp.arange(rows)[None, :] == local_rows[:, None]).astype(bf16)
    rows_residual = jnp.dot(pick, residual, preferred_element_type=f32).astype(bf16)
    own = lax.dynamic_index_in_dim(targets.reshape(planes, subs, count), lax.axis_index(SUB), 1, False).reshape(group, 1)

    base = (lax.axis_index(CTX) * rows).reshape(1)
    message = local_part(
        base, scored, decay_rate, skip_gain, inner_input, state_inputs, tail, gate_input, step_size, flags, conv_inner, conv_state
    )
    message, rows_residual = lax.optimization_barrier((message, rows_residual))
    came = exchange(message, CTX)
    swap = [(i * planes + k, k * planes + i) for i in range(planes) for k in range(planes)]
    rows_residual = lax.ppermute(rows_residual, PLANE, swap)
    out_full, gain = fetched(out_full, norm_gain.reshape(1, -1), rows_residual)
    came, rows_residual, out_full, gain = lax.optimization_barrier((came, rows_residual, out_full, gain))

    gated = exchange(carry(came, planes, subs), CTX).reshape(channels // 2, 2 * group)

    partial = exchange(project(gated, gain, out_full).reshape(planes, count, -1), "tp")
    chosen = exchange(spread(partial, rows_residual, chunks), PLANE).reshape(planes, group, -1)
    columns = head_weight.shape[1]
    ways = lax.axis_size("tp")
    start = (lax.axis_index("z") * subs * ways + lax.axis_index("tp")) * columns
    found = score(start.reshape(1), chosen, final_gain.reshape(planes, -1), own, head_full, ways * columns, chunks)

    found = exchange(found, PLANE).reshape(chunks, 4, group)
    top = jnp.max(found[:, 0], axis=0)
    summed = jnp.sum(found[:, 1] * jnp.exp(found[:, 0] - top[None, :]), axis=0)
    ref = jnp.sum(found[:, 2], axis=0) - top - jnp.log(summed)
    ref = to_everyone(ref.reshape(planes, count), SUB)
    ref_logprob = ref.swapaxes(0, 1).reshape(total)
    token_kl = 0.5 * jnp.square(ref_logprob - policy_logprob)
    return (ref_logprob, token_kl)


def solution(mesh):
    heads_split = mesh.shape["tp"]
    finer = Mesh(mesh.devices.reshape(heads_split, -1, 2, heads_split), ("z", "x", "core", "tp"))
    placed = (
        P(CTX, "tp"),
        P(CTX, "tp"),
        P(None, CTX, "tp"),
        P("tp", CTX),
        P(CTX),
        P("tp"),
        P("tp"),
        P(None, "tp"),
        P(None, None, "tp"),
        P("tp"),
        P("tp", CTX),
        P(CTX, "tp"),
        P(),
        P(None, (*CTX, "tp")),
        P(CTX),
        P(),
        P(),
    )
    return jax.shard_map(body, mesh=finer, in_specs=placed, out_specs=(P(), P()), check_vma=False)
```

```python
import functools

import jax
import jax.numpy as jnp
from jax import lax
from jax.experimental import pallas as pl
from jax.experimental.pallas import tpu as pltpu
from jax.sharding import Mesh
from jax.sharding import PartitionSpec as P

CTX = ("z", "x", "core")
SUB = ("x", "core")
PLANE = ("z", "tp")

epsilon = 1e-05
blocked = -1e9
precise = lax.Precision.HIGHEST
f32 = jnp.float32
bf16 = jnp.bfloat16


def exchange(blocks, axes):
    return lax.all_to_all(blocks, axes, 0, 0, tiled=True)


def to_everyone(shard, axes):
    return exchange(jnp.broadcast_to(shard[None], (lax.axis_size(axes), *shard.shape)), axes)


whole = pl.BlockSpec(memory_space=pltpu.VMEM)


def split(value, count):
    parts = []
    for _ in range(count):
        part = value.astype(bf16)
        parts.append(part)
        value = value - part.astype(f32)
    return parts


def exponent(value, axis):
    top = jnp.max(jnp.abs(value), axis=axis, keepdims=True)
    return jnp.floor(jnp.log2(jnp.maximum(top, 1e-30))) + 1.0


def coded(value, power):
    return jnp.clip(jnp.round(value * jnp.exp2(15.0 - power)), -32767.0, 32767.0)


def coded_log(value, free):
    high = jnp.round(value * 2048.0)
    low = jnp.round((value - high / 2048.0) * 2.0**26)
    return jnp.where(free, high, -32768.0), jnp.where(free, low, 0.0)


def decoded_log(high, low):
    return jnp.where(high < -32767.5, blocked, high / 2048.0 + low * 2.0**-26)


def tail_kernel(stream_ref, state_ref, reset_ref, out_ref):
    channels, states = stream_ref.shape[1], state_ref.shape[2]
    out_ref[:, :channels] = stream_ref[...]
    out_ref[:, channels : channels + states] = state_ref[0]
    out_ref[:, channels + states : channels + 2 * states] = state_ref[1]
    flags = jnp.broadcast_to(reset_ref[...].astype(f32), (out_ref.shape[0], reset_ref.shape[1]))
    out_ref[:, channels + 2 * states :] = flags.astype(bf16)


def last_rows(stream, states, resets, margin):
    rows, channels = stream.shape
    at = rows // margin - 1
    width = states.shape[2]
    return pl.pallas_call(
        tail_kernel,
        grid=(1,),
        out_shape=jax.ShapeDtypeStruct((margin, channels + 2 * width + rows), bf16),
        in_specs=[
            pl.BlockSpec((margin, channels), lambda k: (at, 0)),
            pl.BlockSpec((2, margin, width), lambda k: (0, at, 0)),
            pl.BlockSpec((1, rows), lambda k: (0, 0)),
        ],
        out_specs=pl.BlockSpec((margin, channels + 2 * width + rows), lambda k: (0, 0)),
        compiler_params=pltpu.CompilerParams(vmem_limit_bytes=58 * 2**20),
    )(stream, states, resets)


def silu_filter(pad_ref, keeping, taps, rows, margin):
    summed = taps[0:1] * pad_ref[margin : margin + rows]
    for k in range(1, 4):
        summed = summed + keeping[k - 1] * taps[k : k + 1] * pad_ref[margin - k : margin - k + rows]
    return (summed * jax.nn.sigmoid(summed)).astype(bf16)


def kept(free, second, third, rows):
    line = lax.broadcasted_iota(jnp.int32, free.shape, 0)
    turned = jnp.where(line == 0, free, jnp.where(line == 1, second, third)).T
    return [jnp.broadcast_to(turned[:rows, k : k + 1], (rows, 128)) for k in range(3)]


def ready_kernel(
    base_ref,
    scored_ref,
    rate_ref,
    skip_ref,
    stream_ref,
    state_ref,
    gate_ref,
    step_ref,
    reset_ref,
    taps_ref,
    state_taps_ref,
    values_ref,
    lead_ref,
    taps_out_ref,
    free_ref,
    gates_ref,
    mixing_ref,
    own_ref,
    to_end_ref,
    logs_ref,
    ends_ref,
    pick_ref,
    pad_ref,
):
    rows, channels = stream_ref.shape
    states = state_ref.shape[2]
    heads = step_ref.shape[0]
    margin = lead_ref.shape[0]
    count = scored_ref.shape[0]
    lane = lax.broadcasted_iota(jnp.int32, (8, 128), 1)
    line = lax.broadcasted_iota(jnp.int32, (8, 128), 0)
    flag = jnp.broadcast_to(reset_ref[...].astype(f32), (8, rows))
    free = 1.0 - flag
    free_ref[...] = free
    second = free * pltpu.roll(free, 1, 1)
    keeping = kept(free, second, second * pltpu.roll(free, 2, 1), rows)
    lead_ref[:, :channels] = stream_ref[:margin]
    taps_out_ref[:, :channels] = taps_ref[...]
    for k in range(2):
        span = slice(channels + k * states, channels + (k + 1) * states)
        lead_ref[:, span] = state_ref[k, :margin]
        taps_out_ref[:, span] = state_taps_ref[k]
    pad_ref[:margin] = jnp.zeros((margin, 128), f32)
    for b in range(channels // 128 + 2):
        span = slice(b * 128, (b + 1) * 128)
        k = b - channels // 128
        pad_ref[margin:] = (stream_ref[:, span] if k < 0 else state_ref[k]).astype(f32)
        taps = taps_ref[:, span] if k < 0 else state_taps_ref[k]
        values_ref[:, span] = silu_filter(pad_ref, keeping, taps, rows, margin)

    place = jnp.zeros((8, 128), jnp.int32)
    for k in range(count):
        place = jnp.where(line == k, scored_ref[k] - base_ref[0], place)
    rate = jnp.zeros((heads, rows), f32)
    skip = jnp.zeros((heads, rows), f32)
    head = lax.broadcasted_iota(jnp.int32, (heads, rows), 0)
    for k in range(heads):
        rate = jnp.where(head == k, rate_ref[k], rate)
        skip = jnp.where(head == k, skip_ref[k], skip)
    chosen = lane == place
    pick_ref[...] = chosen.astype(f32)
    first = lax.broadcasted_iota(jnp.int32, (rows, rows), 0)
    upto = (first <= lax.broadcasted_iota(jnp.int32, (rows, rows), 1)).astype(bf16)
    step = step_ref[...]
    drift = jnp.concatenate(split(-rate * step, 3), axis=0)
    summed = jnp.dot(drift, upto, preferred_element_type=f32)
    cumulated = summed[:heads] + summed[heads : 2 * heads] + summed[2 * heads :]
    segment = jnp.dot(flag.astype(bf16), upto, preferred_element_type=f32)
    rows_segment = jnp.sum(jnp.where(chosen, segment, 0.0), axis=1, keepdims=True)
    rows_log = jnp.sum(jnp.where(chosen[None], cumulated[:, None, :], 0.0), axis=2, keepdims=True)
    causal = (lane <= place) & (segment == rows_segment)
    gaps = jnp.where(causal[None], rows_log - cumulated[:, None, :], 0.0)
    mixing = jnp.where(causal[None], jnp.exp(gaps), 0.0) * step[:, None, :]
    mixing_ref[...] = mixing.reshape(heads * count, rows)
    own_ref[...] = jnp.where(chosen[None], skip[:, None, :], 0.0).reshape(heads * count, rows)

    end_segment = segment[0:1, rows - 1 :]
    end_log = cumulated[:, rows - 1 :]
    to_end_ref[...] = jnp.where(segment[0:1] == end_segment, jnp.exp(end_log - cumulated) * step, 0.0)
    end_high, end_low = coded_log(end_log, jnp.broadcast_to(end_segment == 0.0, end_log.shape))
    log_high, log_low = coded_log(rows_log, jnp.broadcast_to((rows_segment == 0.0)[None], rows_log.shape))
    ends_ref[0] = jnp.broadcast_to(end_high, (heads, 128))
    ends_ref[1] = jnp.broadcast_to(end_low, (heads, 128))
    logs_ref[0] = jnp.broadcast_to(log_high, (heads, 8, 128))
    logs_ref[1] = jnp.broadcast_to(log_low, (heads, 8, 128))
    gate = jnp.dot(chosen.astype(bf16), gate_ref[...], preferred_element_type=f32)
    power = exponent(gate, 0)
    gates_ref[:8] = coded(gate, power)
    gates_ref[8:] = jnp.broadcast_to(power, gate.shape)


def ready(base, scored, rate, skip, stream, states, gate, step, resets, taps, state_taps, margin):
    rows, channels = stream.shape
    heads = step.shape[0]
    width = channels + 2 * states.shape[2]
    shapes = [
        ((rows, width), bf16),
        ((margin, width), bf16),
        ((4, width), f32),
        ((8, rows), f32),
        ((16, channels), f32),
        ((heads * 8, rows), f32),
        ((heads * 8, rows), f32),
        ((heads, rows), f32),
        ((2, heads, 8, 128), f32),
        ((2, heads, 128), f32),
        ((8, rows), f32),
    ]
    return pl.pallas_call(
        ready_kernel,
        out_shape=[pltpu.VMEM(*shape) for shape in shapes],
        in_specs=[pl.BlockSpec(memory_space=pltpu.SMEM)] * 4 + [whole] * 7,
        out_specs=[whole] * len(shapes),
        scratch_shapes=[pltpu.VMEM((margin + rows, 128), f32)],
        compiler_params=pltpu.CompilerParams(vmem_limit_bytes=54 * 2**20),
        cost_estimate=pl.CostEstimate(flops=1 << 24, bytes_accessed=2 << 20, transcendentals=1 << 18),
    )(base, scored, rate, skip, stream, states, gate, step, resets, taps, state_taps)


def local_kernel(
    values_ref,
    lead_ref,
    taps_ref,
    free_ref,
    gates_ref,
    mixing_ref,
    own_ref,
    to_end_ref,
    logs_ref,
    ends_ref,
    pick_ref,
    tail_ref,
    out_ref,
    pad_ref,
):
    rows, width = values_ref.shape
    margin = lead_ref.shape[0]
    channels = gates_ref.shape[1]
    lane = lax.broadcasted_iota(jnp.int32, (8, 128), 1)
    line = lax.broadcasted_iota(jnp.int32, (8, 128), 0)
    free = free_ref[...]
    earlier = 1.0 - tail_ref[:, width:].astype(f32)[:8]
    second = free * pltpu.roll(jnp.where(lane == rows - 1, earlier, free), 1, 1)
    third = second * pltpu.roll(jnp.where(lane >= rows - 2, earlier, free), 2, 1)
    keeping = kept(free, second, third, margin)

    def filtered(span):
        pad_ref[:margin] = tail_ref[:, span].astype(f32)
        pad_ref[margin:] = lead_ref[:, span].astype(f32)
        start = silu_filter(pad_ref, keeping, taps_ref[:, span], margin, margin)
        return jnp.concatenate([start, values_ref[margin:, span]], axis=0)

    writes = filtered(slice(channels, channels + 128))
    reads = filtered(slice(channels + 128, width))
    rows_reads = jnp.dot(pick_ref[...].astype(bf16), reads, preferred_element_type=f32)
    scores = lax.dot_general(
        rows_reads.astype(bf16), writes, (((1,), (1,)), ((), ())), preferred_element_type=f32
    )
    heads = to_end_ref.shape[0]
    scores = jnp.broadcast_to(scores[None], (heads, 8, rows)).reshape(heads * 8, rows)
    mixing = split(mixing_ref[...] * scores + own_ref[...], 3)
    to_end = to_end_ref[...]
    end_high, end_low = ends_ref[0], ends_ref[1]

    power = exponent(rows_reads, 1)
    rows_reads = coded(rows_reads, power)
    folded = jnp.concatenate([pltpu.roll(rows_reads, 64, 1), rows_reads], axis=0)
    folded = jnp.broadcast_to(folded[None], (8, 16, 128)).reshape(128, 128)
    powers = jnp.broadcast_to(power, (8, 128))
    left = lane < 64
    wide = lax.broadcasted_iota(jnp.int32, (128, 128), 1)
    empty = jnp.zeros((80, 128), f32)
    for b in range(channels // 128):
        span = slice(b * 128, (b + 1) * 128)
        p, q = 2 * b, 2 * b + 1
        values = filtered(span)
        ends = jnp.concatenate(
            [jnp.broadcast_to(to_end[p : p + 1], (64, rows)), jnp.broadcast_to(to_end[q : q + 1], (64, rows))], axis=0
        )
        high, low = split(values.astype(f32).T * ends, 2)
        state = jnp.dot(high, writes, preferred_element_type=f32) + jnp.dot(low, writes, preferred_element_type=f32)
        both = jnp.concatenate([part[16 * b : 16 * b + 16] for part in mixing], axis=0)
        met = jnp.dot(both, values, preferred_element_type=f32)
        met = met[:16] + met[16:32] + met[32:]
        local = jnp.where(left, met[:8], met[8:])
        local_power, state_power = exponent(local, 0), exponent(state, 1)
        others = jnp.where(line == 2, local_power, jnp.where(line == 3, gates_ref[8:, span], 0.0))
        others = jnp.where(line == 1, jnp.where(left, end_low[p : p + 1], end_low[q : q + 1]), others)
        others = jnp.where(line == 0, jnp.where(left, end_high[p : p + 1], end_high[q : q + 1]), others)
        side = jnp.concatenate(
            [
                coded(local, local_power),
                gates_ref[:8, span],
                jnp.where(left, logs_ref[0, p], logs_ref[0, q]),
                jnp.where(left, logs_ref[1, p], logs_ref[1, q]),
                others,
                powers,
                empty,
            ],
            axis=0,
        ).T
        side = jnp.where(wide == 36, state_power, jnp.where(wide < 64, side, folded))
        for at, part in ((0, coded(state, state_power)), (16, side)):
            part = part.astype(jnp.int32).reshape(8, 16, 128)
            out_ref[8 * b : 8 * b + 8, at : at + 16, :] = part.astype(jnp.int16)


def local_part(made, tail):
    channels = made[4].shape[1]
    return pl.pallas_call(
        local_kernel,
        out_shape=jax.ShapeDtypeStruct((channels // 16, 32, 128), jnp.int16),
        in_specs=[whole] * (len(made) + 1),
        out_specs=whole,
        scratch_shapes=[pltpu.VMEM((2 * tail.shape[0], 128), f32)],
        compiler_params=pltpu.CompilerParams(vmem_limit_bytes=12 * 2**20),
        cost_estimate=pl.CostEstimate(flops=1 << 27, bytes_accessed=2 << 20, transcendentals=1 << 18),
    )(*made, tail)


def carry_kernel(came_ref, out_ref, side_ref, met_ref, weight_ref, *, planes, subs):
    chunks, _, states = came_ref.shape
    part = 16
    count = 8
    group = planes * count
    total = chunks * count
    side = came_ref[:, part:, :].astype(jnp.int32).astype(f32)
    side_ref[...] = side.reshape(chunks * part, 128)
    scale = jnp.exp2(side - 15.0)
    state = came_ref[:, :part, :].astype(jnp.int32).astype(f32) * scale[:, :, 36:37]
    state_high, state_low = split(state.reshape(chunks * part, states), 2)
    wide = lax.broadcasted_iota(jnp.int32, (chunks, 8, 128), 2)
    reads = jnp.where(wide < 64, pltpu.roll(side[:, :8], 64, 2), side[:, 8:])
    order = [z * subs + k for k in range(subs) for z in range(planes)]
    reads = jnp.concatenate([reads[c] for c in order], axis=0)
    reads_high, reads_low = split(reads, 2)
    contract = (((1,), (1,)), ((), ()))
    met_ref[...] = (
        lax.dot_general(state_high, reads_high, contract, preferred_element_type=f32)
        + lax.dot_general(state_high, reads_low, contract, preferred_element_type=f32)
        + lax.dot_general(state_low, reads_high, contract, preferred_element_type=f32)
    )

    lane = lax.broadcasted_iota(jnp.int32, (8, 128), 1)

    def by_lane(block_of, offset):
        columns = []
        for j in range(chunks // 16):
            column = None
            for i in range(16):
                block = block_of(order[16 * j + i])
                tall = block.shape[0]
                if (8 * i - offset) % 128:
                    block = pltpu.roll(block, (8 * i - offset) % 128, 1)
                place = lax.broadcasted_iota(jnp.int32, (tall, 128), 1)
                column = block if column is None else jnp.where(place >= 8 * i, block, column)
            columns.append(column)
        return jnp.concatenate(columns, axis=1)

    local = side * scale[:, :, 34:35]
    gate = side * scale[:, :, 35:36]
    local = by_lane(lambda c: local[c], 0)
    gate = by_lane(lambda c: gate[c], 8)
    log_high = by_lane(lambda c: side[c, :8], 16)[:1]
    log_low = by_lane(lambda c: side[c, :8], 24)[:1]
    power = by_lane(lambda c: side[c, :8], 40)[:1]
    rows_log = decoded_log(log_high, log_low)

    one = side_ref[pl.ds(0, chunks, stride=part), :]
    end_log = decoded_log(one[:, 32:33], one[:, 33:34])
    chunk = lax.broadcasted_iota(jnp.int32, (chunks, total), 0)
    at = lax.broadcasted_iota(jnp.int32, (chunks, total), 1)
    before = chunk < ((at // count) % planes) * subs + at // group
    upper = lax.broadcasted_iota(jnp.int32, (chunks, chunks), 0) < lax.broadcasted_iota(jnp.int32, (chunks, chunks), 1)
    upper = upper.astype(bf16)
    between = jnp.zeros((chunks, total), f32)
    for piece in split(jnp.where(before, end_log, 0.0), 3):
        between = between + jnp.dot(upper, piece, preferred_element_type=f32)
    weight_ref[...] = jnp.where(before, jnp.exp(between + rows_log), 0.0) * jnp.exp2(power - 15.0)

    across = jnp.zeros((part, total), f32)
    for c in range(chunks):
        across = across + weight_ref[c : c + 1, :] * met_ref[part * c : part * c + part, :]
    gated = (across + local) * (gate * jax.nn.sigmoid(gate))
    for k in range(subs):
        columns = slice(k // 2 * 128, k // 2 * 128 + 128)
        first, second = gated[:8, columns], gated[8:, columns]
        if k % 2:
            first = pltpu.roll(first, 64, 1)
        else:
            second = pltpu.roll(second, 64, 1)
        tile = jnp.where(lane < 64, first, second)
        for z in range(planes):
            out_ref[z * subs + k] = tile


def carry(came, planes, subs):
    chunks = came.shape[0]
    return pl.pallas_call(
        functools.partial(carry_kernel, planes=planes, subs=subs),
        out_shape=jax.ShapeDtypeStruct((chunks, 8, 128), f32),
        in_specs=[whole],
        out_specs=whole,
        scratch_shapes=[
            pltpu.VMEM((chunks * 16, 128), f32),
            pltpu.VMEM((chunks * 16, chunks * 8), f32),
            pltpu.VMEM((chunks, chunks * 8), f32),
        ],
        compiler_params=pltpu.CompilerParams(vmem_limit_bytes=24 * 2**20),
        cost_estimate=pl.CostEstimate(flops=1 << 28, bytes_accessed=1 << 20, transcendentals=1 << 16),
    )(came)


def fetch_kernel(full_ref, gain_ref, after_ref, full_out_ref, gain_out_ref, sem):
    fetch = pltpu.make_async_copy(full_ref, full_out_ref, sem)
    fetch.start()
    gain_out_ref[...] = gain_ref[...]
    fetch.wait()


def fetched(full, gain, after):
    anywhere = pl.BlockSpec(memory_space=pl.ANY)
    return pl.pallas_call(
        fetch_kernel,
        out_shape=[pltpu.VMEM(full.shape, full.dtype), pltpu.VMEM(gain.shape, gain.dtype)],
        in_specs=[anywhere, whole, anywhere],
        out_specs=[whole] * 2,
        scratch_shapes=[pltpu.SemaphoreType.DMA],
        compiler_params=pltpu.CompilerParams(vmem_limit_bytes=4 * 2**20),
        cost_estimate=pl.CostEstimate(flops=0, bytes_accessed=2 << 20, transcendentals=0),
    )(full, gain, after)


def project_kernel(gated_ref, gain_ref, weight_ref, out_ref):
    gated = gated_ref[...]
    depth, lanes = gated.shape
    half = lanes // 2
    squares = jnp.broadcast_to(jnp.sum(gated * gated, axis=0, keepdims=True), (8, lanes))
    squares = squares + pltpu.roll(squares, half, 1)
    normed = gated * lax.rsqrt(squares[:1] / (2 * depth) + epsilon)
    pair = [a.reshape(depth // 8, 1, 8, lanes) for a in (normed, pltpu.roll(normed, half, 1))]
    normed = jnp.concatenate(pair, axis=1).reshape(2 * depth, lanes).T[:half]
    normed = (normed * gain_ref[...]).astype(bf16)
    out_ref[...] = lax.dot_general(
        normed, weight_ref[...], (((1,), (1,)), ((), ())), preferred_element_type=f32
    )


def project(gated, gain, weight):
    return pl.pallas_call(
        project_kernel,
        out_shape=jax.ShapeDtypeStruct((gated.shape[1] // 2, weight.shape[0]), f32),
        in_specs=[whole] * 3,
        out_specs=whole,
        compiler_params=pltpu.CompilerParams(vmem_limit_bytes=8 * 2**20),
        cost_estimate=pl.CostEstimate(flops=2 * 64 * 1024 * 512, bytes_accessed=1 << 21, transcendentals=0),
    )(gated, gain, weight)


def spread_kernel(partial_ref, residual_ref, out_ref):
    total = residual_ref[...].astype(f32)
    summed = partial_ref[0]
    for k in range(1, partial_ref.shape[0]):
        summed = summed + partial_ref[k]
    out_ref[...] = jnp.broadcast_to((summed + total).astype(bf16)[None], out_ref.shape)


def spread(partial, residual, copies):
    return pl.pallas_call(
        spread_kernel,
        out_shape=jax.ShapeDtypeStruct((copies, *residual.shape), bf16),
        in_specs=[whole] * 2,
        out_specs=whole,
        compiler_params=pltpu.CompilerParams(vmem_limit_bytes=8 * 2**20),
        cost_estimate=pl.CostEstimate(flops=1 << 16, bytes_accessed=1 << 20, transcendentals=0),
    )(partial, residual)


def logits_kernel(start_ref, chosen_ref, gain_ref, target_ref, from_ref, out_ref, weight_ref, sems, *, stride):
    slabs, group, width = chosen_ref.shape
    subs, _, columns = weight_ref.shape
    fetches = []
    for k in range(slabs):
        block = (slice(None), slice(k * width, (k + 1) * width), slice(None))
        fetches.append(pltpu.make_async_copy(from_ref.at[block], weight_ref.at[block], sems.at[k]))
        fetches[k].start()
    squares = jnp.zeros((group, 1), f32)
    for k in range(slabs):
        slab = chosen_ref[k].astype(f32)
        squares = squares + jnp.sum(slab * slab, axis=1, keepdims=True)
    inverse = lax.rsqrt(squares / (slabs * width) + epsilon)
    logits = jnp.zeros((group, subs * columns), f32)
    for k in range(slabs):
        features = chosen_ref[k].astype(f32) * inverse * gain_ref[k : k + 1, :]
        fetches[k].wait()
        weight = jnp.concatenate([weight_ref[j, k * width : (k + 1) * width, :] for j in range(subs)], axis=1)
        logits = logits + jnp.dot(features.astype(bf16), weight, preferred_element_type=f32)
    top = jnp.max(logits, axis=1, keepdims=True)
    summed = jnp.sum(jnp.exp(logits - top), axis=1, keepdims=True)
    picked = jnp.zeros((group, 1), f32)
    lane = lax.broadcasted_iota(jnp.int32, (group, columns), 1)
    for k in range(subs):
        own = lane + (start_ref[0] + k * stride) == target_ref[...]
        picked = picked + jnp.sum(
            jnp.where(own, logits[:, k * columns : (k + 1) * columns], 0.0), axis=1, keepdims=True
        )
    place = lax.broadcasted_iota(jnp.int32, (group, 128), 1)
    found = jnp.where(place == 0, top, jnp.where(place == 1, summed, picked)).T
    row = jnp.concatenate([found[0:1], found[1:2], found[2:3], found[2:3]], axis=1)
    for k in range(out_ref.shape[0]):
        out_ref[k] = row


def score(start, chosen, gain, target, weight, stride, copies):
    slabs, group, width = chosen.shape
    return pl.pallas_call(
        functools.partial(logits_kernel, stride=stride),
        out_shape=jax.ShapeDtypeStruct((copies, 1, 4 * group), f32),
        in_specs=[pl.BlockSpec(memory_space=pltpu.SMEM), whole, whole, whole, pl.BlockSpec(memory_space=pl.ANY)],
        out_specs=whole,
        scratch_shapes=[pltpu.VMEM(weight.shape, bf16), pltpu.SemaphoreType.DMA((slabs,))],
        compiler_params=pltpu.CompilerParams(vmem_limit_bytes=52 * 2**20),
        cost_estimate=pl.CostEstimate(flops=2 * 64 * 4096 * 1024, bytes_accessed=9 << 20, transcendentals=0),
    )(start, chosen, gain, target, weight)


def body(
    inner_input,
    gate_input,
    state_inputs,
    step_size,
    resets,
    decay_rate,
    skip_gain,
    conv_inner,
    conv_state,
    norm_gain,
    out_weight,
    residual,
    final_gain,
    head_weight,
    scored,
    targets,
    policy_logprob,
):
    rows, channels = inner_input.shape
    chunks = lax.axis_size(CTX)
    part = channels // chunks
    planes, subs = lax.axis_size("z"), lax.axis_size(SUB)
    count = scored.shape[0]
    group = planes * count
    total = chunks * count
    local_rows = scored - lax.axis_index(CTX) * rows

    flags = resets.reshape(1, rows)
    tail = last_rows(inner_input, state_inputs, flags, 16)
    tail = lax.ppermute(tail, CTX, [(i, i + 1) for i in range(chunks - 1)])

    out_full = lax.all_gather(out_weight.T, SUB, axis=0, tiled=True)
    head_full = lax.all_gather(head_weight, SUB, axis=0)
    pick = (jnp.arange(rows)[None, :] == local_rows[:, None]).astype(bf16)
    rows_residual = jnp.dot(pick, residual, preferred_element_type=f32).astype(bf16)
    own = lax.dynamic_index_in_dim(targets.reshape(planes, subs, count), lax.axis_index(SUB), 1, False).reshape(group, 1)

    base = (lax.axis_index(CTX) * rows).reshape(1)
    made = ready(
        base, scored, decay_rate, skip_gain, inner_input, state_inputs, gate_input, step_size, flags, conv_inner, conv_state, tail.shape[0]
    )
    message = local_part(made, tail)
    message, rows_residual = lax.optimization_barrier((message, rows_residual))
    came = exchange(message, CTX)
    swap = [(i * planes + k, k * planes + i) for i in range(planes) for k in range(planes)]
    rows_residual = lax.ppermute(rows_residual, PLANE, swap)
    out_full, gain = fetched(out_full, norm_gain.reshape(1, -1), rows_residual)
    came, rows_residual, out_full, gain = lax.optimization_barrier((came, rows_residual, out_full, gain))

    gated = exchange(carry(came, planes, subs), CTX).reshape(channels // 2, 2 * group)

    partial = exchange(project(gated, gain, out_full).reshape(planes, count, -1), "tp")
    chosen = exchange(spread(partial, rows_residual, chunks), PLANE).reshape(planes, group, -1)
    columns = head_weight.shape[1]
    ways = lax.axis_size("tp")
    start = (lax.axis_index("z") * subs * ways + lax.axis_index("tp")) * columns
    found = score(start.reshape(1), chosen, final_gain.reshape(planes, -1), own, head_full, ways * columns, chunks)

    found = exchange(found, PLANE).reshape(chunks, 4, group)
    top = jnp.max(found[:, 0], axis=0)
    summed = jnp.sum(found[:, 1] * jnp.exp(found[:, 0] - top[None, :]), axis=0)
    ref = jnp.sum(found[:, 2], axis=0) - top - jnp.log(summed)
    ref = to_everyone(ref.reshape(planes, count), SUB)
    ref_logprob = ref.swapaxes(0, 1).reshape(total)
    token_kl = 0.5 * jnp.square(ref_logprob - policy_logprob)
    return (ref_logprob, token_kl)


def solution(mesh):
    heads_split = mesh.shape["tp"]
    finer = Mesh(mesh.devices.reshape(heads_split, -1, 2, heads_split), ("z", "x", "core", "tp"))
    placed = (
        P(CTX, "tp"),
        P(CTX, "tp"),
        P(None, CTX, "tp"),
        P("tp", CTX),
        P(CTX),
        P("tp"),
        P("tp"),
        P(None, "tp"),
        P(None, None, "tp"),
        P("tp"),
        P("tp", CTX),
        P(CTX, "tp"),
        P(),
        P(None, (*CTX, "tp")),
        P(CTX),
        P(),
        P(),
    )
    return jax.shard_map(body, mesh=finer, in_specs=placed, out_specs=(P(), P()), check_vma=False)
```

```python
import functools

import jax
import jax.numpy as jnp
from jax import lax
from jax.experimental import pallas as pl
from jax.experimental.pallas import tpu as pltpu
from jax.sharding import Mesh
from jax.sharding import PartitionSpec as P

CTX = ("z", "x", "core")
SUB = ("x", "core")
PLANE = ("z", "tp")

epsilon = 1e-05
blocked = -1e9
precise = lax.Precision.HIGHEST
f32 = jnp.float32
bf16 = jnp.bfloat16


def exchange(blocks, axes):
    return lax.all_to_all(blocks, axes, 0, 0, tiled=True)


def to_everyone(shard, axes):
    return exchange(jnp.broadcast_to(shard[None], (lax.axis_size(axes), *shard.shape)), axes)


whole = pl.BlockSpec(memory_space=pltpu.VMEM)


def split(value, count):
    parts = []
    for _ in range(count):
        part = value.astype(bf16)
        parts.append(part)
        value = value - part.astype(f32)
    return parts


def exponent(value, axis):
    top = jnp.max(jnp.abs(value), axis=axis, keepdims=True)
    return jnp.floor(jnp.log2(jnp.maximum(top, 1e-30))) + 1.0


def coded(value, power):
    return jnp.clip(jnp.round(value * jnp.exp2(15.0 - power)), -32767.0, 32767.0)


def coded_log(value, free):
    high = jnp.round(value * 2048.0)
    low = jnp.round((value - high / 2048.0) * 2.0**26)
    return jnp.where(free, high, -32768.0), jnp.where(free, low, 0.0)


def decoded_log(high, low):
    return jnp.where(high < -32767.5, blocked, high / 2048.0 + low * 2.0**-26)


def tail_kernel(stream_ref, state_ref, reset_ref, out_ref):
    channels, states = stream_ref.shape[1], state_ref.shape[2]
    out_ref[:, :channels] = stream_ref[...]
    out_ref[:, channels : channels + states] = state_ref[0]
    out_ref[:, channels + states : channels + 2 * states] = state_ref[1]
    flags = jnp.broadcast_to(reset_ref[...].astype(f32), (out_ref.shape[0], reset_ref.shape[1]))
    out_ref[:, channels + 2 * states :] = flags.astype(bf16)


def last_rows(stream, states, resets, margin):
    rows, channels = stream.shape
    at = rows // margin - 1
    width = states.shape[2]
    return pl.pallas_call(
        tail_kernel,
        grid=(1,),
        out_shape=jax.ShapeDtypeStruct((margin, channels + 2 * width + rows), bf16),
        in_specs=[
            pl.BlockSpec((margin, channels), lambda k: (at, 0)),
            pl.BlockSpec((2, margin, width), lambda k: (0, at, 0)),
            pl.BlockSpec((1, rows), lambda k: (0, 0)),
        ],
        out_specs=pl.BlockSpec((margin, channels + 2 * width + rows), lambda k: (0, 0)),
        compiler_params=pltpu.CompilerParams(vmem_limit_bytes=58 * 2**20),
    )(stream, states, resets)


def silu_filter(pad_ref, keeping, taps, rows, margin):
    summed = taps[0:1] * pad_ref[margin : margin + rows]
    for k in range(1, 4):
        summed = summed + keeping[k - 1] * taps[k : k + 1] * pad_ref[margin - k : margin - k + rows]
    return (summed * jax.nn.sigmoid(summed)).astype(bf16)


def kept(free, second, third, rows):
    line = lax.broadcasted_iota(jnp.int32, free.shape, 0)
    turned = jnp.where(line == 0, free, jnp.where(line == 1, second, third)).T
    return [jnp.broadcast_to(turned[:rows, k : k + 1], (rows, 128)) for k in range(3)]


def ready_kernel(
    base_ref,
    scored_ref,
    rate_ref,
    skip_ref,
    stream_ref,
    state_ref,
    gate_ref,
    step_ref,
    reset_ref,
    taps_ref,
    state_taps_ref,
    values_ref,
    lead_ref,
    taps_out_ref,
    free_ref,
    gates_ref,
    mixing_ref,
    own_ref,
    to_end_ref,
    logs_ref,
    ends_ref,
    pick_ref,
    pad_ref,
):
    rows, channels = stream_ref.shape
    states = state_ref.shape[2]
    heads = step_ref.shape[0]
    margin = lead_ref.shape[0]
    count = scored_ref.shape[0]
    lane = lax.broadcasted_iota(jnp.int32, (8, 128), 1)
    line = lax.broadcasted_iota(jnp.int32, (8, 128), 0)
    flag = jnp.broadcast_to(reset_ref[...].astype(f32), (8, rows))
    free = 1.0 - flag
    free_ref[...] = free
    second = free * pltpu.roll(free, 1, 1)
    keeping = kept(free, second, second * pltpu.roll(free, 2, 1), rows)
    lead_ref[:, :channels] = stream_ref[:margin]
    taps_out_ref[:, :channels] = taps_ref[...]
    for k in range(2):
        span = slice(channels + k * states, channels + (k + 1) * states)
        lead_ref[:, span] = state_ref[k, :margin]
        taps_out_ref[:, span] = state_taps_ref[k]
    pad_ref[:margin] = jnp.zeros((margin, 128), f32)
    for b in range(channels // 128 + 2):
        span = slice(b * 128, (b + 1) * 128)
        k = b - channels // 128
        pad_ref[margin:] = (stream_ref[:, span] if k < 0 else state_ref[k]).astype(f32)
        taps = taps_ref[:, span] if k < 0 else state_taps_ref[k]
        values_ref[:, span] = silu_filter(pad_ref, keeping, taps, rows, margin)

    place = jnp.zeros((8, 128), jnp.int32)
    for k in range(count):
        place = jnp.where(line == k, scored_ref[k] - base_ref[0], place)
    rate = jnp.zeros((heads, rows), f32)
    skip = jnp.zeros((heads, rows), f32)
    head = lax.broadcasted_iota(jnp.int32, (heads, rows), 0)
    for k in range(heads):
        rate = jnp.where(head == k, rate_ref[k], rate)
        skip = jnp.where(head == k, skip_ref[k], skip)
    chosen = lane == place
    pick_ref[...] = chosen.astype(f32)
    first = lax.broadcasted_iota(jnp.int32, (rows, rows), 0)
    upto = (first <= lax.broadcasted_iota(jnp.int32, (rows, rows), 1)).astype(bf16)
    step = step_ref[...]
    drift = jnp.concatenate(split(-rate * step, 3), axis=0)
    summed = jnp.dot(drift, upto, preferred_element_type=f32)
    cumulated = summed[:heads] + summed[heads : 2 * heads] + summed[2 * heads :]
    segment = jnp.dot(flag.astype(bf16), upto, preferred_element_type=f32)
    rows_segment = jnp.sum(jnp.where(chosen, segment, 0.0), axis=1, keepdims=True)
    rows_log = jnp.sum(jnp.where(chosen[None], cumulated[:, None, :], 0.0), axis=2, keepdims=True)
    causal = (lane <= place) & (segment == rows_segment)
    gaps = jnp.where(causal[None], rows_log - cumulated[:, None, :], 0.0)
    mixing = jnp.where(causal[None], jnp.exp(gaps), 0.0) * step[:, None, :]
    mixing_ref[...] = mixing.reshape(heads * count, rows)
    own_ref[...] = jnp.where(chosen[None], skip[:, None, :], 0.0).reshape(heads * count, rows)

    end_segment = segment[0:1, rows - 1 :]
    end_log = cumulated[:, rows - 1 :]
    to_end_ref[...] = jnp.where(segment[0:1] == end_segment, jnp.exp(end_log - cumulated) * step, 0.0)
    end_high, end_low = coded_log(end_log, jnp.broadcast_to(end_segment == 0.0, end_log.shape))
    log_high, log_low = coded_log(rows_log, jnp.broadcast_to((rows_segment == 0.0)[None], rows_log.shape))
    ends_ref[0] = jnp.broadcast_to(end_high, (heads, 128))
    ends_ref[1] = jnp.broadcast_to(end_low, (heads, 128))
    logs_ref[0] = jnp.broadcast_to(log_high, (heads, 8, 128))
    logs_ref[1] = jnp.broadcast_to(log_low, (heads, 8, 128))
    gate = jnp.dot(chosen.astype(bf16), gate_ref[...], preferred_element_type=f32)
    power = exponent(gate, 0)
    gates_ref[:8] = coded(gate, power)
    gates_ref[8:] = jnp.broadcast_to(power, gate.shape)


def ready(base, scored, rate, skip, stream, states, gate, step, resets, taps, state_taps, margin):
    rows, channels = stream.shape
    heads = step.shape[0]
    width = channels + 2 * states.shape[2]
    shapes = [
        ((rows, width), bf16),
        ((margin, width), bf16),
        ((4, width), f32),
        ((8, rows), f32),
        ((16, channels), f32),
        ((heads * 8, rows), f32),
        ((heads * 8, rows), f32),
        ((heads, rows), f32),
        ((2, heads, 8, 128), f32),
        ((2, heads, 128), f32),
        ((8, rows), f32),
    ]
    return pl.pallas_call(
        ready_kernel,
        out_shape=[pltpu.VMEM(*shape) for shape in shapes],
        in_specs=[pl.BlockSpec(memory_space=pltpu.SMEM)] * 4 + [whole] * 7,
        out_specs=[whole] * len(shapes),
        scratch_shapes=[pltpu.VMEM((margin + rows, 128), f32)],
        compiler_params=pltpu.CompilerParams(vmem_limit_bytes=54 * 2**20),
        cost_estimate=pl.CostEstimate(flops=1 << 24, bytes_accessed=2 << 20, transcendentals=1 << 18),
    )(base, scored, rate, skip, stream, states, gate, step, resets, taps, state_taps)


def local_kernel(
    values_ref,
    lead_ref,
    taps_ref,
    free_ref,
    gates_ref,
    mixing_ref,
    own_ref,
    to_end_ref,
    logs_ref,
    ends_ref,
    pick_ref,
    tail_ref,
    out_ref,
    pad_ref,
):
    rows, width = values_ref.shape
    margin = lead_ref.shape[0]
    channels = gates_ref.shape[1]
    lane = lax.broadcasted_iota(jnp.int32, (8, 128), 1)
    line = lax.broadcasted_iota(jnp.int32, (8, 128), 0)
    free = free_ref[...]
    earlier = 1.0 - tail_ref[:, width:].astype(f32)[:8]
    second = free * pltpu.roll(jnp.where(lane == rows - 1, earlier, free), 1, 1)
    third = second * pltpu.roll(jnp.where(lane >= rows - 2, earlier, free), 2, 1)
    keeping = kept(free, second, third, margin)

    def filtered(span):
        pad_ref[:margin] = tail_ref[:, span].astype(f32)
        pad_ref[margin:] = lead_ref[:, span].astype(f32)
        start = silu_filter(pad_ref, keeping, taps_ref[:, span], margin, margin)
        return jnp.concatenate([start, values_ref[margin:, span]], axis=0)

    writes = filtered(slice(channels, channels + 128))
    reads = filtered(slice(channels + 128, width))
    rows_reads = jnp.dot(pick_ref[...].astype(bf16), reads, preferred_element_type=f32)
    scores = lax.dot_general(
        rows_reads.astype(bf16), writes, (((1,), (1,)), ((), ())), preferred_element_type=f32
    )
    heads = to_end_ref.shape[0]
    scores = jnp.broadcast_to(scores[None], (heads, 8, rows)).reshape(heads * 8, rows)
    mixing = split(mixing_ref[...] * scores + own_ref[...], 3)
    to_end = to_end_ref[...]
    end_high, end_low = ends_ref[0], ends_ref[1]

    power = exponent(rows_reads, 1)
    rows_reads = coded(rows_reads, power)
    folded = jnp.concatenate([pltpu.roll(rows_reads, 64, 1), rows_reads], axis=0)
    folded = jnp.broadcast_to(folded[None], (8, 16, 128)).reshape(128, 128)
    powers = jnp.broadcast_to(power, (8, 128))
    left = lane < 64
    wide = lax.broadcasted_iota(jnp.int32, (128, 128), 1)
    empty = jnp.zeros((80, 128), f32)
    for b in range(channels // 128):
        span = slice(b * 128, (b + 1) * 128)
        p, q = 2 * b, 2 * b + 1
        values = filtered(span)
        ends = jnp.concatenate(
            [jnp.broadcast_to(to_end[p : p + 1], (64, rows)), jnp.broadcast_to(to_end[q : q + 1], (64, rows))], axis=0
        )
        high, low = split(values.astype(f32).T * ends, 2)
        state = jnp.dot(high, writes, preferred_element_type=f32) + jnp.dot(low, writes, preferred_element_type=f32)
        both = jnp.concatenate([part[16 * b : 16 * b + 16] for part in mixing], axis=0)
        met = jnp.dot(both, values, preferred_element_type=f32)
        met = met[:16] + met[16:32] + met[32:]
        local = jnp.where(left, met[:8], met[8:])
        local_power, state_power = exponent(local, 0), exponent(state, 1)
        others = jnp.where(line == 2, local_power, jnp.where(line == 3, gates_ref[8:, span], 0.0))
        others = jnp.where(line == 1, jnp.where(left, end_low[p : p + 1], end_low[q : q + 1]), others)
        others = jnp.where(line == 0, jnp.where(left, end_high[p : p + 1], end_high[q : q + 1]), others)
        side = jnp.concatenate(
            [
                coded(local, local_power),
                gates_ref[:8, span],
                jnp.where(left, logs_ref[0, p], logs_ref[0, q]),
                jnp.where(left, logs_ref[1, p], logs_ref[1, q]),
                others,
                powers,
                empty,
            ],
            axis=0,
        ).T
        side = jnp.where(wide == 36, state_power, jnp.where(wide < 64, side, folded))
        for at, part in ((0, coded(state, state_power)), (16, side)):
            part = part.astype(jnp.int32).reshape(8, 16, 128)
            out_ref[8 * b : 8 * b + 8, at : at + 16, :] = part.astype(jnp.int16)


def local_part(made, tail):
    channels = made[4].shape[1]
    return pl.pallas_call(
        local_kernel,
        out_shape=jax.ShapeDtypeStruct((channels // 16, 32, 128), jnp.int16),
        in_specs=[whole] * (len(made) + 1),
        out_specs=whole,
        scratch_shapes=[pltpu.VMEM((2 * tail.shape[0], 128), f32)],
        compiler_params=pltpu.CompilerParams(vmem_limit_bytes=12 * 2**20),
        cost_estimate=pl.CostEstimate(flops=1 << 27, bytes_accessed=2 << 20, transcendentals=1 << 18),
    )(*made, tail)


def carry_kernel(came_ref, out_ref, side_ref, met_ref, weight_ref, *, planes, subs):
    chunks, _, states = came_ref.shape
    part = 16
    count = 8
    group = planes * count
    total = chunks * count
    side = came_ref[:, part:, :].astype(jnp.int32).astype(f32)
    side_ref[...] = side.reshape(chunks * part, 128)
    scale = jnp.exp2(side - 15.0)
    state = came_ref[:, :part, :].astype(jnp.int32).astype(f32) * scale[:, :, 36:37]
    state_high, state_low = split(state.reshape(chunks * part, states), 2)
    wide = lax.broadcasted_iota(jnp.int32, (chunks, 8, 128), 2)
    reads = jnp.where(wide < 64, pltpu.roll(side[:, :8], 64, 2), side[:, 8:])
    order = [z * subs + k for k in range(subs) for z in range(planes)]
    reads = jnp.concatenate([reads[c] for c in order], axis=0)
    reads_high, reads_low = split(reads, 2)
    contract = (((1,), (1,)), ((), ()))
    met_ref[...] = (
        lax.dot_general(state_high, reads_high, contract, preferred_element_type=f32)
        + lax.dot_general(state_high, reads_low, contract, preferred_element_type=f32)
        + lax.dot_general(state_low, reads_high, contract, preferred_element_type=f32)
    )

    lane = lax.broadcasted_iota(jnp.int32, (8, 128), 1)

    def by_lane(block_of, offset):
        columns = []
        for j in range(chunks // 16):
            column = None
            for i in range(16):
                block = block_of(order[16 * j + i])
                tall = block.shape[0]
                if (8 * i - offset) % 128:
                    block = pltpu.roll(block, (8 * i - offset) % 128, 1)
                place = lax.broadcasted_iota(jnp.int32, (tall, 128), 1)
                column = block if column is None else jnp.where(place >= 8 * i, block, column)
            columns.append(column)
        return jnp.concatenate(columns, axis=1)

    local = side * scale[:, :, 34:35]
    gate = side * scale[:, :, 35:36]
    local = by_lane(lambda c: local[c], 0)
    gate = by_lane(lambda c: gate[c], 8)
    log_high = by_lane(lambda c: side[c, :8], 16)[:1]
    log_low = by_lane(lambda c: side[c, :8], 24)[:1]
    power = by_lane(lambda c: side[c, :8], 40)[:1]
    rows_log = decoded_log(log_high, log_low)

    one = side_ref[pl.ds(0, chunks, stride=part), :]
    end_log = decoded_log(one[:, 32:33], one[:, 33:34])
    chunk = lax.broadcasted_iota(jnp.int32, (chunks, total), 0)
    at = lax.broadcasted_iota(jnp.int32, (chunks, total), 1)
    before = chunk < ((at // count) % planes) * subs + at // group
    upper = lax.broadcasted_iota(jnp.int32, (chunks, chunks), 0) < lax.broadcasted_iota(jnp.int32, (chunks, chunks), 1)
    upper = upper.astype(bf16)
    between = jnp.zeros((chunks, total), f32)
    for piece in split(jnp.where(before, end_log, 0.0), 3):
        between = between + jnp.dot(upper, piece, preferred_element_type=f32)
    weight_ref[...] = jnp.where(before, jnp.exp(between + rows_log), 0.0) * jnp.exp2(power - 15.0)

    across = jnp.zeros((part, total), f32)
    for c in range(chunks):
        across = across + weight_ref[c : c + 1, :] * met_ref[part * c : part * c + part, :]
    gated = (across + local) * (gate * jax.nn.sigmoid(gate))
    for k in range(subs):
        columns = slice(k // 2 * 128, k // 2 * 128 + 128)
        first, second = gated[:8, columns], gated[8:, columns]
        if k % 2:
            first = pltpu.roll(first, 64, 1)
        else:
            second = pltpu.roll(second, 64, 1)
        tile = jnp.where(lane < 64, first, second)
        for z in range(planes):
            out_ref[z * subs + k] = tile


def carry(came, planes, subs):
    chunks = came.shape[0]
    return pl.pallas_call(
        functools.partial(carry_kernel, planes=planes, subs=subs),
        out_shape=jax.ShapeDtypeStruct((chunks, 8, 128), f32),
        in_specs=[whole],
        out_specs=whole,
        scratch_shapes=[
            pltpu.VMEM((chunks * 16, 128), f32),
            pltpu.VMEM((chunks * 16, chunks * 8), f32),
            pltpu.VMEM((chunks, chunks * 8), f32),
        ],
        compiler_params=pltpu.CompilerParams(vmem_limit_bytes=24 * 2**20),
        cost_estimate=pl.CostEstimate(flops=1 << 28, bytes_accessed=1 << 20, transcendentals=1 << 16),
    )(came)


def fetch_kernel(full_ref, gain_ref, after_ref, full_out_ref, gain_out_ref, sem):
    fetch = pltpu.make_async_copy(full_ref, full_out_ref, sem)
    fetch.start()
    gain_out_ref[...] = gain_ref[...]
    fetch.wait()


def fetched(full, gain, after):
    anywhere = pl.BlockSpec(memory_space=pl.ANY)
    return pl.pallas_call(
        fetch_kernel,
        out_shape=[pltpu.VMEM(full.shape, full.dtype), pltpu.VMEM(gain.shape, gain.dtype)],
        in_specs=[anywhere, whole, anywhere],
        out_specs=[whole] * 2,
        scratch_shapes=[pltpu.SemaphoreType.DMA],
        compiler_params=pltpu.CompilerParams(vmem_limit_bytes=4 * 2**20),
        cost_estimate=pl.CostEstimate(flops=0, bytes_accessed=2 << 20, transcendentals=0),
    )(full, gain, after)


def project_kernel(gated_ref, gain_ref, weight_ref, out_ref):
    gated = gated_ref[...]
    depth, lanes = gated.shape
    half = lanes // 2
    squares = jnp.broadcast_to(jnp.sum(gated * gated, axis=0, keepdims=True), (8, lanes))
    squares = squares + pltpu.roll(squares, half, 1)
    normed = gated * lax.rsqrt(squares[:1] / (2 * depth) + epsilon)
    pair = [a.reshape(depth // 8, 1, 8, lanes) for a in (normed, pltpu.roll(normed, half, 1))]
    normed = jnp.concatenate(pair, axis=1).reshape(2 * depth, lanes).T[:half]
    normed = (normed * gain_ref[...]).astype(bf16)
    out_ref[...] = lax.dot_general(
        normed, weight_ref[...], (((1,), (1,)), ((), ())), preferred_element_type=f32
    )


def project(gated, gain, weight):
    return pl.pallas_call(
        project_kernel,
        out_shape=jax.ShapeDtypeStruct((gated.shape[1] // 2, weight.shape[0]), f32),
        in_specs=[whole] * 3,
        out_specs=whole,
        compiler_params=pltpu.CompilerParams(vmem_limit_bytes=8 * 2**20),
        cost_estimate=pl.CostEstimate(flops=2 * 64 * 1024 * 512, bytes_accessed=1 << 21, transcendentals=0),
    )(gated, gain, weight)


def spread_kernel(partial_ref, residual_ref, out_ref):
    total = residual_ref[...].astype(f32)
    summed = partial_ref[0]
    for k in range(1, partial_ref.shape[0]):
        summed = summed + partial_ref[k]
    out_ref[...] = jnp.broadcast_to((summed + total).astype(bf16)[None], out_ref.shape)


def spread(partial, residual, copies):
    return pl.pallas_call(
        spread_kernel,
        out_shape=jax.ShapeDtypeStruct((copies, *residual.shape), bf16),
        in_specs=[whole] * 2,
        out_specs=whole,
        compiler_params=pltpu.CompilerParams(vmem_limit_bytes=8 * 2**20),
        cost_estimate=pl.CostEstimate(flops=1 << 16, bytes_accessed=1 << 20, transcendentals=0),
    )(partial, residual)


def logits_kernel(start_ref, chosen_ref, gain_ref, target_ref, from_ref, out_ref, weight_ref, sems, *, stride):
    slabs, group, width = chosen_ref.shape
    subs, _, columns = weight_ref.shape
    fetches = []
    for k in range(slabs):
        block = (slice(None), slice(k * width, (k + 1) * width), slice(None))
        fetches.append(pltpu.make_async_copy(from_ref.at[block], weight_ref.at[block], sems.at[k]))
        fetches[k].start()
    squares = jnp.zeros((group, 1), f32)
    for k in range(slabs):
        slab = chosen_ref[k].astype(f32)
        squares = squares + jnp.sum(slab * slab, axis=1, keepdims=True)
    inverse = lax.rsqrt(squares / (slabs * width) + epsilon)
    logits = jnp.zeros((group, subs * columns), f32)
    for k in range(slabs):
        features = chosen_ref[k].astype(f32) * inverse * gain_ref[k : k + 1, :]
        fetches[k].wait()
        weight = jnp.concatenate([weight_ref[j, k * width : (k + 1) * width, :] for j in range(subs)], axis=1)
        logits = logits + jnp.dot(features.astype(bf16), weight, preferred_element_type=f32)
    top = jnp.max(logits, axis=1, keepdims=True)
    summed = jnp.sum(jnp.exp(logits - top), axis=1, keepdims=True)
    picked = jnp.zeros((group, 1), f32)
    lane = lax.broadcasted_iota(jnp.int32, (group, columns), 1)
    for k in range(subs):
        own = lane + (start_ref[0] + k * stride) == target_ref[...]
        picked = picked + jnp.sum(
            jnp.where(own, logits[:, k * columns : (k + 1) * columns], 0.0), axis=1, keepdims=True
        )
    place = lax.broadcasted_iota(jnp.int32, (group, 128), 1)
    found = jnp.where(place == 0, top, jnp.where(place == 1, summed, picked)).T
    row = jnp.concatenate([found[0:1], found[1:2], found[2:3], found[2:3]], axis=1)
    for k in range(out_ref.shape[0]):
        out_ref[k] = row


def score(start, chosen, gain, target, weight, stride, copies):
    slabs, group, width = chosen.shape
    return pl.pallas_call(
        functools.partial(logits_kernel, stride=stride),
        out_shape=jax.ShapeDtypeStruct((copies, 1, 4 * group), f32),
        in_specs=[pl.BlockSpec(memory_space=pltpu.SMEM), whole, whole, whole, pl.BlockSpec(memory_space=pl.ANY)],
        out_specs=whole,
        scratch_shapes=[pltpu.VMEM(weight.shape, bf16), pltpu.SemaphoreType.DMA((slabs,))],
        compiler_params=pltpu.CompilerParams(vmem_limit_bytes=52 * 2**20),
        cost_estimate=pl.CostEstimate(flops=2 * 64 * 4096 * 1024, bytes_accessed=9 << 20, transcendentals=0),
    )(start, chosen, gain, target, weight)


def body(
    inner_input,
    gate_input,
    state_inputs,
    step_size,
    resets,
    decay_rate,
    skip_gain,
    conv_inner,
    conv_state,
    norm_gain,
    out_weight,
    residual,
    final_gain,
    head_weight,
    scored,
    targets,
    policy_logprob,
):
    rows, channels = inner_input.shape
    chunks = lax.axis_size(CTX)
    part = channels // chunks
    planes, subs = lax.axis_size("z"), lax.axis_size(SUB)
    count = scored.shape[0]
    group = planes * count
    total = chunks * count
    local_rows = scored - lax.axis_index(CTX) * rows

    flags = resets.reshape(1, rows)
    tail = last_rows(inner_input, state_inputs, flags, 16)
    tail = lax.ppermute(tail, CTX, [(i, i + 1) for i in range(chunks - 1)])

    out_full = lax.all_gather(out_weight.T, SUB, axis=0, tiled=True)
    head_full = lax.all_gather(head_weight, SUB, axis=0)
    pick = (jnp.arange(rows)[None, :] == local_rows[:, None]).astype(bf16)
    rows_residual = jnp.dot(pick, residual, preferred_element_type=f32).astype(bf16)
    own = lax.dynamic_index_in_dim(targets.reshape(planes, subs, count), lax.axis_index(SUB), 1, False).reshape(group, 1)

    base = (lax.axis_index(CTX) * rows).reshape(1)
    made = ready(
        base, scored, decay_rate, skip_gain, inner_input, state_inputs, gate_input, step_size, flags, conv_inner, conv_state, tail.shape[0]
    )
    message = local_part(made, tail)
    message, rows_residual = lax.optimization_barrier((message, rows_residual))
    came = exchange(message, CTX)
    swap = [(i * planes + k, k * planes + i) for i in range(planes) for k in range(planes)]
    rows_residual = lax.ppermute(rows_residual, PLANE, swap)
    came, rows_residual = lax.optimization_barrier((came, rows_residual))

    gated = carry(came, planes, subs)
    out_full, gain = fetched(out_full, norm_gain.reshape(1, -1), gated)
    gated, out_full, gain = lax.optimization_barrier((exchange(gated, CTX), out_full, gain))
    gated = gated.reshape(channels // 2, 2 * group)

    partial = exchange(project(gated, gain, out_full).reshape(planes, count, -1), "tp")
    chosen = exchange(spread(partial, rows_residual, chunks), PLANE).reshape(planes, group, -1)
    columns = head_weight.shape[1]
    ways = lax.axis_size("tp")
    start = (lax.axis_index("z") * subs * ways + lax.axis_index("tp")) * columns
    found = score(start.reshape(1), chosen, final_gain.reshape(planes, -1), own, head_full, ways * columns, chunks)

    found = exchange(found, PLANE).reshape(chunks, 4, group)
    top = jnp.max(found[:, 0], axis=0)
    summed = jnp.sum(found[:, 1] * jnp.exp(found[:, 0] - top[None, :]), axis=0)
    ref = jnp.sum(found[:, 2], axis=0) - top - jnp.log(summed)
    ref = to_everyone(ref.reshape(planes, count), SUB)
    ref_logprob = ref.swapaxes(0, 1).reshape(total)
    token_kl = 0.5 * jnp.square(ref_logprob - policy_logprob)
    return (ref_logprob, token_kl)


def solution(mesh):
    heads_split = mesh.shape["tp"]
    finer = Mesh(mesh.devices.reshape(heads_split, -1, 2, heads_split), ("z", "x", "core", "tp"))
    placed = (
        P(CTX, "tp"),
        P(CTX, "tp"),
        P(None, CTX, "tp"),
        P("tp", CTX),
        P(CTX),
        P("tp"),
        P("tp"),
        P(None, "tp"),
        P(None, None, "tp"),
        P("tp"),
        P("tp", CTX),
        P(CTX, "tp"),
        P(),
        P(None, (*CTX, "tp")),
        P(CTX),
        P(),
        P(),
    )
    return jax.shard_map(body, mesh=finer, in_specs=placed, out_specs=(P(), P()), check_vma=False)
```

```python
import functools

import jax
import jax.numpy as jnp
from jax import lax
from jax.experimental import pallas as pl
from jax.experimental.pallas import tpu as pltpu
from jax.sharding import Mesh
from jax.sharding import PartitionSpec as P

CTX = ("z", "x", "core")
SUB = ("x", "core")
PLANE = ("z", "tp")

epsilon = 1e-05
blocked = -1e9
precise = lax.Precision.HIGHEST
f32 = jnp.float32
bf16 = jnp.bfloat16


def exchange(blocks, axes):
    return lax.all_to_all(blocks, axes, 0, 0, tiled=True)


def to_everyone(shard, axes):
    return exchange(jnp.broadcast_to(shard[None], (lax.axis_size(axes), *shard.shape)), axes)


whole = pl.BlockSpec(memory_space=pltpu.VMEM)


def split(value, count):
    parts = []
    for _ in range(count):
        part = value.astype(bf16)
        parts.append(part)
        value = value - part.astype(f32)
    return parts


def exponent(value, axis):
    top = jnp.max(jnp.abs(value), axis=axis, keepdims=True)
    return jnp.floor(jnp.log2(jnp.maximum(top, 1e-30))) + 1.0


def coded(value, power):
    return jnp.clip(jnp.round(value * jnp.exp2(15.0 - power)), -32767.0, 32767.0)


def coded_log(value, free):
    high = jnp.round(value * 2048.0)
    low = jnp.round((value - high / 2048.0) * 2.0**26)
    return jnp.where(free, high, -32768.0), jnp.where(free, low, 0.0)


def decoded_log(high, low):
    return jnp.where(high < -32767.5, blocked, high / 2048.0 + low * 2.0**-26)


def tail_kernel(stream_ref, state_ref, reset_ref, out_ref):
    channels, states = stream_ref.shape[1], state_ref.shape[2]
    out_ref[:, :channels] = stream_ref[...]
    out_ref[:, channels : channels + states] = state_ref[0]
    out_ref[:, channels + states : channels + 2 * states] = state_ref[1]
    flags = jnp.broadcast_to(reset_ref[...].astype(f32), (out_ref.shape[0], reset_ref.shape[1]))
    out_ref[:, channels + 2 * states :] = flags.astype(bf16)


def last_rows(stream, states, resets, margin):
    rows, channels = stream.shape
    at = rows // margin - 1
    width = states.shape[2]
    return pl.pallas_call(
        tail_kernel,
        grid=(1,),
        out_shape=jax.ShapeDtypeStruct((margin, channels + 2 * width + rows), bf16),
        in_specs=[
            pl.BlockSpec((margin, channels), lambda k: (at, 0)),
            pl.BlockSpec((2, margin, width), lambda k: (0, at, 0)),
            pl.BlockSpec((1, rows), lambda k: (0, 0)),
        ],
        out_specs=pl.BlockSpec((margin, channels + 2 * width + rows), lambda k: (0, 0)),
        compiler_params=pltpu.CompilerParams(vmem_limit_bytes=58 * 2**20),
    )(stream, states, resets)


def silu_filter(pad_ref, keeping, taps, rows, margin):
    summed = taps[0:1] * pad_ref[margin : margin + rows]
    for k in range(1, 4):
        summed = summed + keeping[k - 1] * taps[k : k + 1] * pad_ref[margin - k : margin - k + rows]
    return (summed * jax.nn.sigmoid(summed)).astype(bf16)


def kept(free, second, third, rows):
    line = lax.broadcasted_iota(jnp.int32, free.shape, 0)
    turned = jnp.where(line == 0, free, jnp.where(line == 1, second, third)).T
    return [jnp.broadcast_to(turned[:rows, k : k + 1], (rows, 128)) for k in range(3)]


def ready_kernel(
    base_ref,
    scored_ref,
    rate_ref,
    skip_ref,
    stream_ref,
    state_ref,
    gate_ref,
    step_ref,
    reset_ref,
    taps_ref,
    state_taps_ref,
    values_ref,
    lead_ref,
    taps_out_ref,
    free_ref,
    gates_ref,
    mixing_ref,
    own_ref,
    to_end_ref,
    logs_ref,
    ends_ref,
    pick_ref,
    pad_ref,
):
    rows, channels = stream_ref.shape
    states = state_ref.shape[2]
    heads = step_ref.shape[0]
    margin = lead_ref.shape[0]
    count = scored_ref.shape[0]
    lane = lax.broadcasted_iota(jnp.int32, (8, 128), 1)
    line = lax.broadcasted_iota(jnp.int32, (8, 128), 0)
    flag = jnp.broadcast_to(reset_ref[...].astype(f32), (8, rows))
    free = 1.0 - flag
    free_ref[...] = free
    second = free * pltpu.roll(free, 1, 1)
    keeping = kept(free, second, second * pltpu.roll(free, 2, 1), rows)
    lead_ref[:, :channels] = stream_ref[:margin]
    taps_out_ref[:, :channels] = taps_ref[...]
    for k in range(2):
        span = slice(channels + k * states, channels + (k + 1) * states)
        lead_ref[:, span] = state_ref[k, :margin]
        taps_out_ref[:, span] = state_taps_ref[k]
    pad_ref[:margin] = jnp.zeros((margin, 128), f32)
    for b in range(channels // 128 + 2):
        span = slice(b * 128, (b + 1) * 128)
        k = b - channels // 128
        pad_ref[margin:] = (stream_ref[:, span] if k < 0 else state_ref[k]).astype(f32)
        taps = taps_ref[:, span] if k < 0 else state_taps_ref[k]
        values_ref[:, span] = silu_filter(pad_ref, keeping, taps, rows, margin)

    place = jnp.zeros((8, 128), jnp.int32)
    for k in range(count):
        place = jnp.where(line == k, scored_ref[k] - base_ref[0], place)
    rate = jnp.zeros((heads, rows), f32)
    skip = jnp.zeros((heads, rows), f32)
    head = lax.broadcasted_iota(jnp.int32, (heads, rows), 0)
    for k in range(heads):
        rate = jnp.where(head == k, rate_ref[k], rate)
        skip = jnp.where(head == k, skip_ref[k], skip)
    chosen = lane == place
    pick_ref[...] = chosen.astype(f32)
    first = lax.broadcasted_iota(jnp.int32, (rows, rows), 0)
    upto = (first <= lax.broadcasted_iota(jnp.int32, (rows, rows), 1)).astype(bf16)
    step = step_ref[...]
    drift = jnp.concatenate(split(-rate * step, 3), axis=0)
    summed = jnp.dot(drift, upto, preferred_element_type=f32)
    cumulated = summed[:heads] + summed[heads : 2 * heads] + summed[2 * heads :]
    segment = jnp.dot(flag.astype(bf16), upto, preferred_element_type=f32)
    rows_segment = jnp.sum(jnp.where(chosen, segment, 0.0), axis=1, keepdims=True)
    rows_log = jnp.sum(jnp.where(chosen[None], cumulated[:, None, :], 0.0), axis=2, keepdims=True)
    causal = (lane <= place) & (segment == rows_segment)
    gaps = jnp.where(causal[None], rows_log - cumulated[:, None, :], 0.0)
    mixing = jnp.where(causal[None], jnp.exp(gaps), 0.0) * step[:, None, :]
    mixing_ref[...] = mixing.reshape(heads * count, rows)
    own_ref[...] = jnp.where(chosen[None], skip[:, None, :], 0.0).reshape(heads * count, rows)

    end_segment = segment[0:1, rows - 1 :]
    end_log = cumulated[:, rows - 1 :]
    to_end_ref[...] = jnp.where(segment[0:1] == end_segment, jnp.exp(end_log - cumulated) * step, 0.0)
    end_high, end_low = coded_log(end_log, jnp.broadcast_to(end_segment == 0.0, end_log.shape))
    log_high, log_low = coded_log(rows_log, jnp.broadcast_to((rows_segment == 0.0)[None], rows_log.shape))
    ends_ref[0] = jnp.broadcast_to(end_high, (heads, 128))
    ends_ref[1] = jnp.broadcast_to(end_low, (heads, 128))
    logs_ref[0] = jnp.broadcast_to(log_high, (heads, 8, 128))
    logs_ref[1] = jnp.broadcast_to(log_low, (heads, 8, 128))
    gate = jnp.dot(chosen.astype(bf16), gate_ref[...], preferred_element_type=f32)
    power = exponent(gate, 0)
    gates_ref[:8] = coded(gate, power)
    gates_ref[8:] = jnp.broadcast_to(power, gate.shape)


def ready(base, scored, rate, skip, stream, states, gate, step, resets, taps, state_taps, margin):
    rows, channels = stream.shape
    heads = step.shape[0]
    width = channels + 2 * states.shape[2]
    shapes = [
        ((rows, width), bf16),
        ((margin, width), bf16),
        ((4, width), f32),
        ((8, rows), f32),
        ((16, channels), f32),
        ((heads * 8, rows), f32),
        ((heads * 8, rows), f32),
        ((heads, rows), f32),
        ((2, heads, 8, 128), f32),
        ((2, heads, 128), f32),
        ((8, rows), f32),
    ]
    return pl.pallas_call(
        ready_kernel,
        out_shape=[pltpu.VMEM(*shape) for shape in shapes],
        in_specs=[pl.BlockSpec(memory_space=pltpu.SMEM)] * 4 + [whole] * 7,
        out_specs=[whole] * len(shapes),
        scratch_shapes=[pltpu.VMEM((margin + rows, 128), f32)],
        compiler_params=pltpu.CompilerParams(vmem_limit_bytes=54 * 2**20),
        cost_estimate=pl.CostEstimate(flops=1 << 24, bytes_accessed=2 << 20, transcendentals=1 << 18),
    )(base, scored, rate, skip, stream, states, gate, step, resets, taps, state_taps)


def local_kernel(
    values_ref,
    lead_ref,
    taps_ref,
    free_ref,
    gates_ref,
    mixing_ref,
    own_ref,
    to_end_ref,
    logs_ref,
    ends_ref,
    pick_ref,
    tail_ref,
    out_ref,
    pad_ref,
):
    rows, width = values_ref.shape
    margin = lead_ref.shape[0]
    channels = gates_ref.shape[1]
    lane = lax.broadcasted_iota(jnp.int32, (8, 128), 1)
    line = lax.broadcasted_iota(jnp.int32, (8, 128), 0)
    free = free_ref[...]
    earlier = 1.0 - tail_ref[:, width:].astype(f32)[:8]
    second = free * pltpu.roll(jnp.where(lane == rows - 1, earlier, free), 1, 1)
    third = second * pltpu.roll(jnp.where(lane >= rows - 2, earlier, free), 2, 1)
    keeping = kept(free, second, third, margin)

    def filtered(span):
        pad_ref[:margin] = tail_ref[:, span].astype(f32)
        pad_ref[margin:] = lead_ref[:, span].astype(f32)
        start = silu_filter(pad_ref, keeping, taps_ref[:, span], margin, margin)
        return jnp.concatenate([start, values_ref[margin:, span]], axis=0)

    writes = filtered(slice(channels, channels + 128))
    reads = filtered(slice(channels + 128, width))
    rows_reads = jnp.dot(pick_ref[...].astype(bf16), reads, preferred_element_type=f32)
    scores = lax.dot_general(
        rows_reads.astype(bf16), writes, (((1,), (1,)), ((), ())), preferred_element_type=f32
    )
    heads = to_end_ref.shape[0]
    scores = jnp.broadcast_to(scores[None], (heads, 8, rows)).reshape(heads * 8, rows)
    mixing = split(mixing_ref[...] * scores + own_ref[...], 3)
    to_end = to_end_ref[...]
    end_high, end_low = ends_ref[0], ends_ref[1]

    power = exponent(rows_reads, 1)
    rows_reads = coded(rows_reads, power)
    folded = jnp.concatenate([pltpu.roll(rows_reads, 64, 1), rows_reads], axis=0)
    folded = jnp.broadcast_to(folded[None], (8, 16, 128)).reshape(128, 128)
    powers = jnp.broadcast_to(power, (8, 128))
    left = lane < 64
    wide = lax.broadcasted_iota(jnp.int32, (128, 128), 1)
    empty = jnp.zeros((80, 128), f32)
    for b in range(channels // 128):
        span = slice(b * 128, (b + 1) * 128)
        p, q = 2 * b, 2 * b + 1
        values = filtered(span)
        ends = jnp.concatenate(
            [jnp.broadcast_to(to_end[p : p + 1], (64, rows)), jnp.broadcast_to(to_end[q : q + 1], (64, rows))], axis=0
        )
        high, low = split(values.astype(f32).T * ends, 2)
        state = jnp.dot(high, writes, preferred_element_type=f32) + jnp.dot(low, writes, preferred_element_type=f32)
        both = jnp.concatenate([part[16 * b : 16 * b + 16] for part in mixing], axis=0)
        met = jnp.dot(both, values, preferred_element_type=f32)
        met = met[:16] + met[16:32] + met[32:]
        local = jnp.where(left, met[:8], met[8:])
        local_power, state_power = exponent(local, 0), exponent(state, 1)
        others = jnp.where(line == 2, local_power, jnp.where(line == 3, gates_ref[8:, span], 0.0))
        others = jnp.where(line == 1, jnp.where(left, end_low[p : p + 1], end_low[q : q + 1]), others)
        others = jnp.where(line == 0, jnp.where(left, end_high[p : p + 1], end_high[q : q + 1]), others)
        side = jnp.concatenate(
            [
                coded(local, local_power),
                gates_ref[:8, span],
                jnp.where(left, logs_ref[0, p], logs_ref[0, q]),
                jnp.where(left, logs_ref[1, p], logs_ref[1, q]),
                others,
                powers,
                empty,
            ],
            axis=0,
        ).T
        side = jnp.where(wide == 36, state_power, jnp.where(wide < 64, side, folded))
        for at, part in ((0, coded(state, state_power)), (16, side)):
            part = part.astype(jnp.int32).reshape(8, 16, 128)
            out_ref[8 * b : 8 * b + 8, at : at + 16, :] = part.astype(jnp.int16)


def local_part(made, tail):
    channels = made[4].shape[1]
    return pl.pallas_call(
        local_kernel,
        out_shape=jax.ShapeDtypeStruct((channels // 16, 32, 128), jnp.int16),
        in_specs=[whole] * (len(made) + 1),
        out_specs=whole,
        scratch_shapes=[pltpu.VMEM((2 * tail.shape[0], 128), f32)],
        compiler_params=pltpu.CompilerParams(vmem_limit_bytes=12 * 2**20),
        cost_estimate=pl.CostEstimate(flops=1 << 27, bytes_accessed=2 << 20, transcendentals=1 << 18),
    )(*made, tail)


def carry_kernel(came_ref, out_ref, side_ref, met_ref, weight_ref, *, planes, subs):
    chunks, _, states = came_ref.shape
    part = 16
    count = 8
    group = planes * count
    total = chunks * count
    side = came_ref[:, part:, :].astype(jnp.int32).astype(f32)
    side_ref[...] = side.reshape(chunks * part, 128)
    scale = jnp.exp2(side - 15.0)
    state = came_ref[:, :part, :].astype(jnp.int32).astype(f32) * scale[:, :, 36:37]
    state_high, state_low = split(state.reshape(chunks * part, states), 2)
    wide = lax.broadcasted_iota(jnp.int32, (chunks, 8, 128), 2)
    reads = jnp.where(wide < 64, pltpu.roll(side[:, :8], 64, 2), side[:, 8:])
    order = [z * subs + k for k in range(subs) for z in range(planes)]
    reads = jnp.concatenate([reads[c] for c in order], axis=0)
    reads_high, reads_low = split(reads, 2)
    contract = (((1,), (1,)), ((), ()))
    met_ref[...] = (
        lax.dot_general(state_high, reads_high, contract, preferred_element_type=f32)
        + lax.dot_general(state_high, reads_low, contract, preferred_element_type=f32)
        + lax.dot_general(state_low, reads_high, contract, preferred_element_type=f32)
    )

    lane = lax.broadcasted_iota(jnp.int32, (8, 128), 1)

    def by_lane(block_of, offset):
        columns = []
        for j in range(chunks // 16):
            column = None
            for i in range(16):
                block = block_of(order[16 * j + i])
                tall = block.shape[0]
                if (8 * i - offset) % 128:
                    block = pltpu.roll(block, (8 * i - offset) % 128, 1)
                place = lax.broadcasted_iota(jnp.int32, (tall, 128), 1)
                column = block if column is None else jnp.where(place >= 8 * i, block, column)
            columns.append(column)
        return jnp.concatenate(columns, axis=1)

    local = side * scale[:, :, 34:35]
    gate = side * scale[:, :, 35:36]
    local = by_lane(lambda c: local[c], 0)
    gate = by_lane(lambda c: gate[c], 8)
    log_high = by_lane(lambda c: side[c, :8], 16)[:1]
    log_low = by_lane(lambda c: side[c, :8], 24)[:1]
    power = by_lane(lambda c: side[c, :8], 40)[:1]
    rows_log = decoded_log(log_high, log_low)

    one = side_ref[pl.ds(0, chunks, stride=part), :]
    end_log = decoded_log(one[:, 32:33], one[:, 33:34])
    chunk = lax.broadcasted_iota(jnp.int32, (chunks, total), 0)
    at = lax.broadcasted_iota(jnp.int32, (chunks, total), 1)
    before = chunk < ((at // count) % planes) * subs + at // group
    upper = lax.broadcasted_iota(jnp.int32, (chunks, chunks), 0) < lax.broadcasted_iota(jnp.int32, (chunks, chunks), 1)
    upper = upper.astype(bf16)
    between = jnp.zeros((chunks, total), f32)
    for piece in split(jnp.where(before, end_log, 0.0), 3):
        between = between + jnp.dot(upper, piece, preferred_element_type=f32)
    weight_ref[...] = jnp.where(before, jnp.exp(between + rows_log), 0.0) * jnp.exp2(power - 15.0)

    across = jnp.zeros((part, total), f32)
    for c in range(chunks):
        across = across + weight_ref[c : c + 1, :] * met_ref[part * c : part * c + part, :]
    gated = (across + local) * (gate * jax.nn.sigmoid(gate))
    for k in range(subs):
        columns = slice(k // 2 * 128, k // 2 * 128 + 128)
        first, second = gated[:8, columns], gated[8:, columns]
        if k % 2:
            first = pltpu.roll(first, 64, 1)
        else:
            second = pltpu.roll(second, 64, 1)
        tile = jnp.where(lane < 64, first, second)
        for z in range(planes):
            out_ref[z * subs + k] = tile


def carry(came, planes, subs):
    chunks = came.shape[0]
    return pl.pallas_call(
        functools.partial(carry_kernel, planes=planes, subs=subs),
        out_shape=jax.ShapeDtypeStruct((chunks, 8, 128), f32),
        in_specs=[whole],
        out_specs=whole,
        scratch_shapes=[
            pltpu.VMEM((chunks * 16, 128), f32),
            pltpu.VMEM((chunks * 16, chunks * 8), f32),
            pltpu.VMEM((chunks, chunks * 8), f32),
        ],
        compiler_params=pltpu.CompilerParams(vmem_limit_bytes=24 * 2**20),
        cost_estimate=pl.CostEstimate(flops=1 << 28, bytes_accessed=1 << 20, transcendentals=1 << 16),
    )(came)


def fetch_kernel(full_ref, gain_ref, after_ref, full_out_ref, gain_out_ref, sem):
    fetch = pltpu.make_async_copy(full_ref, full_out_ref, sem)
    fetch.start()
    gain_out_ref[...] = gain_ref[...]
    fetch.wait()


def fetched(full, gain, after):
    anywhere = pl.BlockSpec(memory_space=pl.ANY)
    return pl.pallas_call(
        fetch_kernel,
        out_shape=[pltpu.VMEM(full.shape, full.dtype), pltpu.VMEM(gain.shape, gain.dtype)],
        in_specs=[anywhere, whole, anywhere],
        out_specs=[whole] * 2,
        scratch_shapes=[pltpu.SemaphoreType.DMA],
        compiler_params=pltpu.CompilerParams(vmem_limit_bytes=4 * 2**20),
        cost_estimate=pl.CostEstimate(flops=0, bytes_accessed=2 << 20, transcendentals=0),
    )(full, gain, after)


def project_kernel(gated_ref, gain_ref, weight_ref, out_ref):
    gated = gated_ref[...]
    depth, lanes = gated.shape
    half = lanes // 2
    squares = jnp.broadcast_to(jnp.sum(gated * gated, axis=0, keepdims=True), (8, lanes))
    squares = squares + pltpu.roll(squares, half, 1)
    normed = gated * lax.rsqrt(squares[:1] / (2 * depth) + epsilon)
    pair = [a.reshape(depth // 8, 1, 8, lanes) for a in (normed, pltpu.roll(normed, half, 1))]
    normed = jnp.concatenate(pair, axis=1).reshape(2 * depth, lanes).T[:half]
    normed = (normed * gain_ref[...]).astype(bf16)
    out_ref[...] = lax.dot_general(
        normed, weight_ref[...], (((1,), (1,)), ((), ())), preferred_element_type=f32
    )


def project(gated, gain, weight):
    return pl.pallas_call(
        project_kernel,
        out_shape=jax.ShapeDtypeStruct((gated.shape[1] // 2, weight.shape[0]), f32),
        in_specs=[whole] * 3,
        out_specs=whole,
        compiler_params=pltpu.CompilerParams(vmem_limit_bytes=8 * 2**20),
        cost_estimate=pl.CostEstimate(flops=2 * 64 * 1024 * 512, bytes_accessed=1 << 21, transcendentals=0),
    )(gated, gain, weight)


def spread_kernel(partial_ref, residual_ref, out_ref):
    total = residual_ref[...].astype(f32)
    summed = partial_ref[0]
    for k in range(1, partial_ref.shape[0]):
        summed = summed + partial_ref[k]
    out_ref[...] = jnp.broadcast_to((summed + total).astype(bf16)[None], out_ref.shape)


def spread(partial, residual, copies):
    return pl.pallas_call(
        spread_kernel,
        out_shape=jax.ShapeDtypeStruct((copies, *residual.shape), bf16),
        in_specs=[whole] * 2,
        out_specs=whole,
        compiler_params=pltpu.CompilerParams(vmem_limit_bytes=8 * 2**20),
        cost_estimate=pl.CostEstimate(flops=1 << 16, bytes_accessed=1 << 20, transcendentals=0),
    )(partial, residual)


def logits_kernel(start_ref, chosen_ref, gain_ref, target_ref, from_ref, out_ref, weight_ref, sems, *, stride):
    slabs, group, width = chosen_ref.shape
    subs, _, columns = weight_ref.shape
    fetches = []
    for k in range(slabs):
        block = (slice(None), slice(k * width, (k + 1) * width), slice(None))
        fetches.append(pltpu.make_async_copy(from_ref.at[block], weight_ref.at[block], sems.at[k]))
        fetches[k].start()
    squares = jnp.zeros((group, 1), f32)
    for k in range(slabs):
        slab = chosen_ref[k].astype(f32)
        squares = squares + jnp.sum(slab * slab, axis=1, keepdims=True)
    inverse = lax.rsqrt(squares / (slabs * width) + epsilon)
    logits = jnp.zeros((group, subs * columns), f32)
    for k in range(slabs):
        features = chosen_ref[k].astype(f32) * inverse * gain_ref[k : k + 1, :]
        fetches[k].wait()
        weight = jnp.concatenate([weight_ref[j, k * width : (k + 1) * width, :] for j in range(subs)], axis=1)
        logits = logits + jnp.dot(features.astype(bf16), weight, preferred_element_type=f32)
    top = jnp.max(logits, axis=1, keepdims=True)
    summed = jnp.sum(jnp.exp(logits - top), axis=1, keepdims=True)
    picked = jnp.zeros((group, 1), f32)
    lane = lax.broadcasted_iota(jnp.int32, (group, columns), 1)
    for k in range(subs):
        own = lane + (start_ref[0] + k * stride) == target_ref[...]
        picked = picked + jnp.sum(
            jnp.where(own, logits[:, k * columns : (k + 1) * columns], 0.0), axis=1, keepdims=True
        )
    place = lax.broadcasted_iota(jnp.int32, (group, 128), 1)
    found = jnp.where(place == 0, top + jnp.log(summed), picked).T
    row = jnp.concatenate([found[0:1], found[1:2]], axis=1)
    for k in range(out_ref.shape[0]):
        out_ref[k] = row


def score(start, chosen, gain, target, weight, stride, copies):
    slabs, group, width = chosen.shape
    return pl.pallas_call(
        functools.partial(logits_kernel, stride=stride),
        out_shape=jax.ShapeDtypeStruct((copies, 1, 2 * group), f32),
        in_specs=[pl.BlockSpec(memory_space=pltpu.SMEM), whole, whole, whole, pl.BlockSpec(memory_space=pl.ANY)],
        out_specs=whole,
        scratch_shapes=[pltpu.VMEM(weight.shape, bf16), pltpu.SemaphoreType.DMA((slabs,))],
        compiler_params=pltpu.CompilerParams(vmem_limit_bytes=52 * 2**20),
        cost_estimate=pl.CostEstimate(flops=2 * 64 * 4096 * 1024, bytes_accessed=9 << 20, transcendentals=0),
    )(start, chosen, gain, target, weight)


def body(
    inner_input,
    gate_input,
    state_inputs,
    step_size,
    resets,
    decay_rate,
    skip_gain,
    conv_inner,
    conv_state,
    norm_gain,
    out_weight,
    residual,
    final_gain,
    head_weight,
    scored,
    targets,
    policy_logprob,
):
    rows, channels = inner_input.shape
    chunks = lax.axis_size(CTX)
    part = channels // chunks
    planes, subs = lax.axis_size("z"), lax.axis_size(SUB)
    count = scored.shape[0]
    group = planes * count
    total = chunks * count
    local_rows = scored - lax.axis_index(CTX) * rows

    flags = resets.reshape(1, rows)
    tail = last_rows(inner_input, state_inputs, flags, 16)
    tail = lax.ppermute(tail, CTX, [(i, i + 1) for i in range(chunks - 1)])

    out_full = lax.all_gather(out_weight.T, SUB, axis=0, tiled=True)
    head_full = lax.all_gather(head_weight, SUB, axis=0)
    pick = (jnp.arange(rows)[None, :] == local_rows[:, None]).astype(bf16)
    rows_residual = jnp.dot(pick, residual, preferred_element_type=f32).astype(bf16)
    own = lax.dynamic_index_in_dim(targets.reshape(planes, subs, count), lax.axis_index(SUB), 1, False).reshape(group, 1)

    base = (lax.axis_index(CTX) * rows).reshape(1)
    made = ready(
        base, scored, decay_rate, skip_gain, inner_input, state_inputs, gate_input, step_size, flags, conv_inner, conv_state, tail.shape[0]
    )
    message = local_part(made, tail)
    message, rows_residual = lax.optimization_barrier((message, rows_residual))
    came = exchange(message, CTX)
    swap = [(i * planes + k, k * planes + i) for i in range(planes) for k in range(planes)]
    rows_residual = lax.ppermute(rows_residual, PLANE, swap)
    out_full, gain = fetched(out_full, norm_gain.reshape(1, -1), rows_residual)
    came, rows_residual, out_full, gain = lax.optimization_barrier((came, rows_residual, out_full, gain))

    gated = exchange(carry(came, planes, subs), CTX).reshape(channels // 2, 2 * group)

    partial = exchange(project(gated, gain, out_full).reshape(planes, count, -1), "tp")
    chosen = exchange(spread(partial, rows_residual, chunks), PLANE).reshape(planes, group, -1)
    columns = head_weight.shape[1]
    ways = lax.axis_size("tp")
    start = (lax.axis_index("z") * subs * ways + lax.axis_index("tp")) * columns
    found = score(start.reshape(1), chosen, final_gain.reshape(planes, -1), own, head_full, ways * columns, chunks)

    found = exchange(found, PLANE).reshape(chunks, 2, group)
    top = jnp.max(found[:, 0], axis=0)
    summed = jnp.sum(jnp.exp(found[:, 0] - top[None, :]), axis=0)
    ref = jnp.sum(found[:, 1], axis=0) - top - jnp.log(summed)
    ref = to_everyone(ref.reshape(planes, count), SUB)
    ref_logprob = ref.swapaxes(0, 1).reshape(total)
    token_kl = 0.5 * jnp.square(ref_logprob - policy_logprob)
    return (ref_logprob, token_kl)


def solution(mesh):
    heads_split = mesh.shape["tp"]
    finer = Mesh(mesh.devices.reshape(heads_split, -1, 2, heads_split), ("z", "x", "core", "tp"))
    placed = (
        P(CTX, "tp"),
        P(CTX, "tp"),
        P(None, CTX, "tp"),
        P("tp", CTX),
        P(CTX),
        P("tp"),
        P("tp"),
        P(None, "tp"),
        P(None, None, "tp"),
        P("tp"),
        P("tp", CTX),
        P(CTX, "tp"),
        P(),
        P(None, (*CTX, "tp")),
        P(CTX),
        P(),
        P(),
    )
    return jax.shard_map(body, mesh=finer, in_specs=placed, out_specs=(P(), P()), check_vma=False)
```
